32 devices in a mesh: group: 2 (over y), row: 8 (over z, x), probe: 2 (over core).
Axes of the slice: x: 2, y: 2, z: 4, core: 2. Of those that a mesh axis runs over, the one named last changes fastest.
Arguments:
- observations: float32 [4, 64, 8192], P('group', 'row'), parts along dimension 0, may hold values from -3 to 3
- coefficients: float32 [18, 64, 8192], P('group', 'row'), parts along dimension 0, may hold values from -0.25 to 3, as said below
- probes: float32 [4, 4, 64, 8192], P('probe', 'group', 'row'), parts along dimension 1, may hold values from -6 to 6
Outputs:
- gradient: float32 [18, 64, 8192], P('group', 'row', 'probe'), parts along dimension 0
The draws below stay inside these ranges and needn't reach their ends.
There are 2 independent parts, one for each index of `group`. The reference program is written for one: setup_inputs(seed, part) draws one part's arguments, and reference() takes and returns one part's arrays. A program takes and returns all parts, laid end to end along the dimension named above; each array names one. Nothing has to cross between parts.
Inputs may be any that keep to these rules, and one draw needn't show every extreme that they name: `coefficients`: channels 0 and 1 lie in [1, 3], channels 2 and 3 in [0.25, 1], channels 4 and 5 in [0.9, 1], channels 6 and 7 in [-0.25, 0.25], channel 8 in [-0.2, 0.2].
All inputs are finite; a program needn't handle non-finite values.
Results may differ from the reference program's by a relative error of at most 0.00002.
Values sent between devices are 32-bit elements; how exact they have to be, the bound alone decides.
No kernel may reach another device: no remote copies, remote signals or barrier semaphores. Data moves between devices by JAX's collectives and lax.ppermute only.
A program may use at most 64 MiB of HBM per device.

```python
import math
import jax
import jax.numpy as jnp

NY = 8192
CHEB = 6
PROBES = 4
NX = 64


def draw_coefficients(key, part):
    key = jax.random.fold_in(key, 11)
    base = jax.random.uniform(key, (9, NX, NY), jnp.float32)
    shaped = base
    kappa = jnp.exp(shaped[0:2] * jnp.log(3.0))
    cross_diffusion = 0.25 * jnp.exp(shaped[2:4] * jnp.log(4.0))
    along_diffusion = 0.9 * jnp.exp(shaped[4:6] * jnp.log(1.0 / 0.9))
    skew_part = 0.25 * (2.0 * shaped[6:8] - 1.0)
    coupling = 0.2 * (2.0 * shaped[8:9] - 1.0)
    return jnp.concatenate((kappa, cross_diffusion, along_diffusion, skew_part, coupling), axis=0).astype(jnp.float32)


def block_scale(key, dims, cuts, least, largest):
    level, own = 1.0, jax.random.fold_in(key, 6)
    for axis_at, blocks in cuts:
        draws = jnp.exp(jax.random.uniform(jax.random.fold_in(own, axis_at), (blocks,), jnp.float32, least / len(cuts), largest / len(cuts)))
        level = level * jnp.repeat(draws, dims[axis_at] // blocks).reshape([-1 if axis == axis_at else 1 for axis in range(len(dims))])
    return level


def scatter_about(stream_key, extent, width, most, pieces=(), dtype=jnp.bfloat16):
    drawn = jax.random.normal(stream_key, extent, jnp.float32) * width
    if len(pieces) > 0:
        drawn = block_scale(stream_key, extent, pieces, -0.22, 0.18) * drawn
    return jnp.clip(drawn, min=-most, max=most).astype(dtype)


def setup_inputs(seed: int = 0, part: int = 0) -> dict:
    key_list = jax.random.split(jax.random.key(seed), 4)
    part_keys = jax.random.split(jax.random.fold_in(key_list[3], part), 4)
    observations = scatter_about(part_keys[0], (2, NX, NY), 0.2, 3.0, ((1, 8),), jnp.float32)
    coefficients = draw_coefficients(jax.random.fold_in(jax.random.fold_in(key_list[3], part), 71), part)
    probes = scatter_about(part_keys[2], (PROBES, 2, NX, NY), 1.0, 6.0, ((0, 2), (2, 8)), jnp.float32)
    return dict(observations=observations, coefficients=coefficients, probes=probes)


lower_edge = 0.25
upper_edge = 12.0


def cheb_weights(degree, low_end, high_end):
    count = degree + 1
    values = []
    for order in range(count):
        accum = 0.0
        for node in range(count):
            angle = math.pi * (node + 0.5) / count
            point = 0.5 * (high_end - low_end) * math.cos(angle) + 0.5 * (high_end + low_end)
            accum += math.cos(order * angle) / point
        accum = accum * 2.0 / count
        if order == 0:
            accum = accum * 0.5
        values.append(accum)
    return values


def stencil_terms(padded):
    spread = [(0, 0)] * (padded.ndim - 1) + [(1, 1)]
    wide = jnp.pad(padded, spread)
    center = wide[..., 1:-1, 1:-1]
    across = wide[..., 1:-1, 2:] - 2.0 * center + wide[..., 1:-1, :-2]
    along = wide[..., 2:, 1:-1] - 2.0 * center + wide[..., :-2, 1:-1]
    skewed = (wide[..., 2:, 2:] - wide[..., 2:, :-2] - wide[..., :-2, 2:] + wide[..., :-2, :-2]) * 0.25
    return center, across, along, skewed


def apply_operator(coefficients, padded):
    center, across, along, skewed = stencil_terms(padded)
    return (coefficients[0:2] * center - coefficients[2:4] * across - coefficients[4:6] * along
            - 2.0 * coefficients[6:8] * skewed + coefficients[8] * jnp.flip(center, axis=-3))


def scaled(coefficients, padded):
    center = padded[..., 1:-1, :]
    return (2.0 * apply_operator(coefficients, padded) - (lower_edge + upper_edge) * center) / (upper_edge - lower_edge)


def gradient_terms(left, right_padded):
    center, across, along, skewed = stencil_terms(right_padded)
    cross_term = left[..., 0:1, :, :] * center[..., 1:2, :, :] + left[..., 1:2, :, :] * center[..., 0:1, :, :]
    return jnp.concatenate((left * center, -left * across, -left * along, -2.0 * left * skewed, cross_term), axis=-3)


def pad_rows(field):
    return jnp.pad(field, [(0, 0)] * (field.ndim - 2) + [(1, 1), (0, 0)])


def reference(observations, coefficients, probes):
    weights = cheb_weights(CHEB, lower_edge, upper_edge)
    previous = probes
    current = scaled(coefficients, pad_rows(previous))
    series = weights[0] * previous + weights[1] * current
    for degree in range(2, CHEB + 1):
        following = 2.0 * scaled(coefficients, pad_rows(current)) - previous
        series = series + weights[degree] * following
        previous, current = current, following
    probe_sum = jnp.sum(gradient_terms(probes, pad_rows(series)), axis=0)
    data_part = gradient_terms(observations, pad_rows(observations))
    return (0.5 / PROBES) * probe_sum - 0.5 * data_part
```

```python
import functools
import math

import jax
import jax.numpy as jnp
from jax import lax
from jax.experimental import pallas as pl
from jax.experimental.pallas import tpu as pltpu
from jax.sharding import PartitionSpec as P

CHEB = 6
LANES = 128
SUBS = 8
CHUNK = 3

lower_edge = 0.25
upper_edge = 12.0


def cheb_weights(degree, low_end, high_end):
    count = degree + 1
    values = []
    for order in range(count):
        accum = 0.0
        for node in range(count):
            angle = math.pi * (node + 0.5) / count
            point = 0.5 * (high_end - low_end) * math.cos(angle) + 0.5 * (high_end + low_end)
            accum += math.cos(order * angle) / point
        accum = accum * 2.0 / count
        if order == 0:
            accum = accum * 0.5
        values.append(accum)
    return values


def vmem_spec():
    return pl.BlockSpec(memory_space=pltpu.VMEM)


def any_spec():
    return pl.BlockSpec(memory_space=pl.ANY)


def params():
    return pltpu.CompilerParams(vmem_limit_bytes=40 * 1024 * 1024)


def cost(vregs):
    return pl.CostEstimate(flops=vregs * 1024 * 20, bytes_accessed=vregs * 4096 * 4, transcendentals=0)


def lane_index():
    return lax.broadcasted_iota(jnp.int32, (SUBS, LANES), 1)


def sideways(load, first, count, total):
    lane = lane_index()
    tiles = [load(first + k) for k in range(count)]
    before = load(jnp.maximum(first - 1, 0))
    after = load(jnp.minimum(first + count, total - 1))
    from_left = [jnp.where(first > 0, pltpu.roll(before, 1, 1), 0.0)]
    from_left += [pltpu.roll(tile, 1, 1) for tile in tiles]
    from_right = [pltpu.roll(tile, LANES - 1, 1) for tile in tiles]
    from_right += [jnp.where(first + count < total, pltpu.roll(after, LANES - 1, 1), 0.0)]
    result = []
    for k in range(count):
        left = jnp.where(lane == 0, from_left[k], from_left[k + 1])
        right = jnp.where(lane == LANES - 1, from_right[k + 1], from_right[k])
        result.append((tiles[k], left + right, right - left))
    return result


def sub(row):
    return pl.ds(row * SUBS, SUBS)


def prep_kernel(width, coefficients_ref, expanded_ref, window, sem):
    start = pl.multiple_of(lax.axis_index("probe") * (coefficients_ref.shape[2] - width), LANES)
    copy = pltpu.make_async_copy(coefficients_ref.at[:, :, pl.ds(start, width)], window, sem)
    copy.start()
    copy.wait()
    scale = 4.0 / (upper_edge - lower_edge)
    shift = 2.0 * (upper_edge + lower_edge) / (upper_edge - lower_edge)

    def body(tile, carry):
        cols = pl.ds(pl.multiple_of(tile * LANES, LANES), LANES)
        kappa, across, along, skew = [
            [window[2 * kind + c, :, cols] for c in range(2)] for kind in range(4)
        ]
        coupling = scale * window[8, :, cols]
        for c in range(2):
            values = (
                scale * (kappa[c] + 2.0 * (across[c] + along[c])) - shift,
                -scale * across[c],
                -scale * along[c],
                -0.5 * scale * skew[c],
                coupling,
            )
            for kind, value in enumerate(values):
                for probe in range(4):
                    expanded_ref[kind, tile, pl.ds(4 * c + probe, SUBS, stride=SUBS), :] = value
        return carry

    lax.fori_loop(0, width // LANES, body, 0)


def layout_kernel(width, probes_ref, other_ref, observed_ref, z_ref, top_ref, bottom_ref, seen_ref, own, sem):
    start = pl.multiple_of(lax.axis_index("probe") * (probes_ref.shape[3] - width), LANES)
    copies = [
        pltpu.make_async_copy(probes_ref.at[:, :, :, pl.ds(start, width)], own, sem.at[0]),
        pltpu.make_async_copy(observed_ref.at[:, :, pl.ds(start, width)], seen_ref, sem.at[1]),
    ]
    for copy in copies:
        copy.start()
    for copy in copies:
        copy.wait()
    tiles = width // LANES

    def body(tile, carry):
        cols = pl.ds(pl.multiple_of(tile * LANES, LANES), LANES)
        for c in range(2):
            for probe in range(2):
                z_ref[tile, pl.ds(4 * c + probe, SUBS, stride=SUBS), :] = own[probe, c, :, cols]
                z_ref[tile, pl.ds(4 * c + 2 + probe, SUBS, stride=SUBS), :] = other_ref[probe, c, :, cols]
        return carry

    lax.fori_loop(0, tiles, body, 0)

    def edges(tile, carry):
        top_ref[tile] = z_ref[tile, sub(0), :]
        bottom_ref[tile] = z_ref[tile, sub(SUBS - 1), :]
        return carry

    lax.fori_loop(0, tiles, edges, 0)
    for c in range(2):
        for tile in range(tiles):
            place = c * tiles + tile
            cols = pl.ds(tile * LANES, LANES)
            at = (tiles + place // SUBS, pl.ds(place % SUBS, 1))
            top_ref[at[0], at[1], :] = seen_ref[c, 0:1, cols]
            bottom_ref[at[0], at[1], :] = seen_ref[c, SUBS - 1 : SUBS, cols]


def step_kernel(upper, constants, offset, other_row, tiles, *refs):
    weight, scale, subtract = constants
    own_ref, other_ref, halo_ref, z_ref, coefficients_ref = refs[:5]
    rest = refs[5:]
    before_ref = None
    if subtract:
        before_ref, rest = rest[0], rest[1:]
    out_ref, edge_ref = rest
    first_row = 0 if upper else 4

    def load(row):
        if row == (-1 if upper else 4):
            return lambda tile: halo_ref[tile]
        if row == (4 if upper else -1):
            return lambda tile: other_ref[tile, sub(other_row), :]
        return lambda tile: own_ref[tile, sub(offset + row), :]

    def body(step, carry):
        first = step * CHUNK
        above = sideways(load(-1), first, CHUNK, tiles)
        here = sideways(load(0), first, CHUNK, tiles)
        for row in range(4):
            below = sideways(load(row + 1), first, CHUNK, tiles)
            for k in range(CHUNK):
                tile = first + k
                rows = sub(first_row + row)
                value, beside, _ = here[k]
                coefs = [coefficients_ref[kind, tile, rows, :] for kind in range(5)]
                total = (
                    coefs[0] * value
                    + coefs[1] * beside
                    + coefs[2] * (above[k][0] + below[k][0])
                    + coefs[3] * (below[k][2] - above[k][2])
                    + coefs[4] * pltpu.roll(value, 4, 0)
                )
                if scale != 1.0:
                    total = scale * total
                total = total + weight * z_ref[tile, rows, :]
                if subtract:
                    total = total - before_ref[tile, sub(row), :]
                out_ref[tile, sub(row), :] = total
                if row == (0 if upper else 3):
                    edge_ref[tile] = total
            above, here = here, below
        return carry

    lax.fori_loop(0, tiles // CHUNK, body, 0)


def data_kernel(tiles, seen_ref, up_ref, down_ref, out_ref):
    row = lax.broadcasted_iota(jnp.int32, (SUBS, LANES), 0)
    lane = lane_index()

    def halo(ref, c, tile):
        place = c * tiles + tile
        return ref[tiles + place // SUBS, pl.ds(place % SUBS, 1), :]

    def body(tile, carry):
        values = []
        for c in range(2):

            def load(at):
                return seen_ref[c, :, pl.ds(pl.multiple_of(at * LANES, LANES), LANES)]

            def edge(ref, at):
                return jnp.broadcast_to(halo(ref, c, at), (SUBS, LANES))

            def shifted(at):
                value = load(at)
                above = jnp.where(row == 0, edge(up_ref, at), pltpu.roll(value, 1, 0))
                below = jnp.where(row == SUBS - 1, edge(down_ref, at), pltpu.roll(value, SUBS - 1, 0))
                return value, above + below, below - above

            left = shifted(jnp.maximum(tile - 1, 0))
            center = shifted(tile)
            right = shifted(jnp.minimum(tile + 1, tiles - 1))

            def from_left(a, b):
                edge_value = jnp.where(tile > 0, pltpu.roll(a, 1, 1), 0.0)
                return jnp.where(lane == 0, edge_value, pltpu.roll(b, 1, 1))

            def from_right(a, b):
                edge_value = jnp.where(tile < tiles - 1, pltpu.roll(a, LANES - 1, 1), 0.0)
                return jnp.where(lane == LANES - 1, edge_value, pltpu.roll(b, LANES - 1, 1))

            value, along, _ = center
            across = from_left(left[0], value) + from_right(right[0], value)
            skew = from_right(right[2], center[2]) - from_left(left[2], center[2])
            half = -0.5 * value
            out_ref[tile, c] = half * value
            out_ref[tile, 2 + c] = -half * (across - 2.0 * value)
            out_ref[tile, 4 + c] = -half * (along - 2.0 * value)
            out_ref[tile, 6 + c] = -0.5 * half * skew
            values.append(value)
        out_ref[tile, 8] = -(values[0] * values[1])
        return carry

    lax.fori_loop(0, tiles, body, 0)


def gradient_kernel(tiles, factor, z_ref, top_ref, bottom_ref, up_ref, down_ref, data_ref, out_ref, products):
    kept = out_ref.shape[2] // LANES
    offset = lax.axis_index("probe") * (tiles - kept)

    def load(row):
        if row < 0:
            return lambda tile: up_ref[tile]
        if row >= SUBS:
            return lambda tile: down_ref[tile]
        if row < 4:
            return lambda tile: top_ref[tile, sub(row), :]
        return lambda tile: bottom_ref[tile, sub(row - 4), :]

    def body(index, carry):
        tile = index + offset
        above = sideways(load(-1), tile, 1, tiles)[0]
        here = sideways(load(0), tile, 1, tiles)[0]
        for row in range(SUBS):
            below = sideways(load(row + 1), tile, 1, tiles)[0]
            left = factor * z_ref[tile, sub(row), :]
            value, beside, _ = here
            twice = 2.0 * value
            products[0, sub(row), :] = left * value
            products[1, sub(row), :] = left * (twice - beside)
            products[2, sub(row), :] = left * (twice - (above[0] + below[0]))
            products[3, sub(row), :] = (-0.5 * left) * (below[2] - above[2])
            products[4, sub(row), :] = left * pltpu.roll(value, 4, 0)
            above, here = here, below
        cols = pl.ds(pl.multiple_of(index * LANES, LANES), LANES)
        for kind in range(5):
            parts = [products[kind, pl.ds(s, SUBS, stride=SUBS), :] for s in range(SUBS)]
            sums = [(parts[4 * c] + parts[4 * c + 1]) + (parts[4 * c + 2] + parts[4 * c + 3]) for c in range(2)]
            if kind < 4:
                for c in range(2):
                    out_ref[2 * kind + c, :, cols] = sums[c] + data_ref[tile, 2 * kind + c]
            else:
                out_ref[8, :, cols] = (sums[0] + sums[1]) + data_ref[tile, 8]
        return carry

    lax.fori_loop(0, kept, body, 0)


def per_device(observations, coefficients, probes):
    weights = cheb_weights(CHEB, lower_edge, upper_edge)
    f32 = jnp.float32
    columns = probes.shape[3]
    share = columns // lax.axis_size("probe")
    width = share + LANES
    tiles = width // LANES
    seen_tiles = -(-2 * tiles // SUBS)
    rows = lax.axis_size("row")
    down_pairs = [(i, i + 1) for i in range(rows - 1)]
    up_pairs = [(i + 1, i) for i in range(rows - 1)]

    def to_next(edge):
        return lax.ppermute(edge, "row", down_pairs)

    def to_previous(edge):
        return lax.ppermute(edge, "row", up_pairs)

    core = lax.axis_index("probe")
    theirs = lax.dynamic_slice_in_dim(probes, (1 - core) * (columns - width), width, axis=3)
    other = lax.ppermute(theirs, "probe", [(0, 1), (1, 0)])

    expanded = pl.pallas_call(
        functools.partial(prep_kernel, width),
        out_shape=pltpu.VMEM((5, tiles, SUBS * SUBS, LANES), f32),
        in_specs=[any_spec()],
        out_specs=vmem_spec(),
        scratch_shapes=[pltpu.VMEM((9, SUBS, width), f32), pltpu.SemaphoreType.DMA],
        compiler_params=params(),
        cost_estimate=cost(5 * 8 * tiles),
        name="prep",
    )(coefficients)

    message = (tiles + seen_tiles, SUBS, LANES)
    z, top, bottom, seen = pl.pallas_call(
        functools.partial(layout_kernel, width),
        out_shape=[
            pltpu.VMEM((tiles, SUBS * SUBS, LANES), f32),
            pltpu.VMEM(message, f32),
            pltpu.VMEM(message, f32),
            pltpu.VMEM((2, SUBS, width), f32),
        ],
        in_specs=[any_spec(), vmem_spec(), any_spec()],
        out_specs=[vmem_spec()] * 4,
        scratch_shapes=[pltpu.VMEM((2, 2, SUBS, width), f32), pltpu.SemaphoreType.DMA((2,))],
        compiler_params=params(),
        cost_estimate=cost(8 * tiles),
        name="layout",
    )(probes, other, observations)

    def half(upper, constants, own, other_half, halo, before):
        shared = own is z
        offset = (0 if upper else 4) if shared else 0
        other_row = (4 if upper else 3) if shared else (0 if upper else 3)
        operands = [own, other_half, halo, z, expanded]
        if constants[2]:
            operands.append(before)
        return pl.pallas_call(
            functools.partial(step_kernel, upper, constants, offset, other_row, tiles),
            out_shape=[
                pltpu.VMEM((tiles, 4 * SUBS, LANES), f32),
                pltpu.VMEM((tiles, SUBS, LANES), f32),
            ],
            in_specs=[vmem_spec()] * len(operands),
            out_specs=[vmem_spec()] * 2,
            compiler_params=params(),
            cost_estimate=cost(4 * tiles),
            name=("upper" if upper else "lower"),
        )(*operands)

    first_up, first_down = to_next(bottom), to_previous(top)
    up, down = first_up, first_down
    now = (z, z)
    before = (None, None)
    for order in range(CHEB - 1, -1, -1):
        if order == CHEB - 1:
            constants = (weights[order], weights[CHEB], False)
        elif order == CHEB - 2:
            constants = (weights[order] - weights[CHEB], 1.0, False)
        elif order > 0:
            constants = (weights[order], 1.0, True)
        else:
            constants = (weights[0], 0.5, True)
        upper, top = half(True, constants, now[0], now[1], up, before[0])
        next_down = to_previous(top)
        lower, bottom = half(False, constants, now[1], now[0], down, before[1])
        next_up = to_next(bottom)
        before, now = now, (upper, lower)
        up, down = next_up, next_down

    data = pl.pallas_call(
        functools.partial(data_kernel, tiles),
        out_shape=pltpu.VMEM((tiles, 9, SUBS, LANES), f32),
        in_specs=[vmem_spec()] * 3,
        out_specs=vmem_spec(),
        compiler_params=params(),
        cost_estimate=cost(9 * tiles),
        name="data",
    )(seen, first_up, first_down)

    total_probes = probes.shape[0] * lax.axis_size("probe")
    return pl.pallas_call(
        functools.partial(gradient_kernel, tiles, 0.5 / total_probes),
        out_shape=jax.ShapeDtypeStruct((9, SUBS, share), f32),
        in_specs=[vmem_spec()] * 6,
        out_specs=vmem_spec(),
        scratch_shapes=[pltpu.VMEM((5, SUBS * SUBS, LANES), f32)],
        compiler_params=params(),
        cost_estimate=cost(24 * tiles),
        name="gradient",
    )(z, now[0], now[1], up, down, data)


def solution(mesh):
    in_specs = (P("group", "row", None), P("group", "row", None), P("probe", "group", "row", None))
    out_specs = P("group", "row", "probe")
    return jax.shard_map(
        per_device, mesh=mesh, in_specs=in_specs, out_specs=out_specs, check_vma=False
    )
```

```python
import functools
import math

import jax
import jax.numpy as jnp
from jax import lax
from jax.experimental import pallas as pl
from jax.experimental.pallas import tpu as pltpu
from jax.sharding import PartitionSpec as P

CHEB = 6
LANES = 128
SUBS = 8

lower_edge = 0.25
upper_edge = 12.0


def cheb_weights(degree, low_end, high_end):
    count = degree + 1
    values = []
    for order in range(count):
        accum = 0.0
        for node in range(count):
            angle = math.pi * (node + 0.5) / count
            point = 0.5 * (high_end - low_end) * math.cos(angle) + 0.5 * (high_end + low_end)
            accum += math.cos(order * angle) / point
        accum = accum * 2.0 / count
        if order == 0:
            accum = accum * 0.5
        values.append(accum)
    return values


def vmem_spec():
    return pl.BlockSpec(memory_space=pltpu.VMEM)


def params():
    return pltpu.CompilerParams(vmem_limit_bytes=40 * 1024 * 1024)


def cost(vregs):
    return pl.CostEstimate(flops=vregs * 1024 * 20, bytes_accessed=vregs * 4096 * 4, transcendentals=0)


def masks():
    lane = lax.broadcasted_iota(jnp.int32, (SUBS, LANES), 1)
    return lane == 0, lane == LANES - 1


def window_tiles(load, first, count, total):
    before = jnp.where(first > 0, load(jnp.maximum(first - 1, 0)), 0.0)
    after = jnp.where(first + count < total, load(jnp.minimum(first + count, total - 1)), 0.0)
    return [before] + [load(first + k) for k in range(count)] + [after]


def beside(before, here, after, edges):
    left = pltpu.roll(jnp.where(edges[1], before, here), 1, 1)
    right = pltpu.roll(jnp.where(edges[0], after, here), LANES - 1, 1)
    return left, right


def sub(row):
    return pl.ds(row * SUBS, SUBS)


def tile_columns(tile):
    return pl.ds(pl.multiple_of(tile * LANES, LANES), LANES)


def chunk_of(tiles):
    return max(count for count in range(1, 12) if tiles % count == 0)


def load_kernel(width, probes_ref, observed_ref, coefficients_ref, theirs_ref, own_ref, seen_ref, window_ref, sem):
    core = lax.axis_index("probe")
    move = probes_ref.shape[3] - width
    mine = pl.ds(pl.multiple_of(core * move, LANES), width)
    other = pl.ds(pl.multiple_of((1 - core) * move, LANES), width)
    copies = [
        pltpu.make_async_copy(probes_ref.at[:, :, :, other], theirs_ref, sem.at[0]),
        pltpu.make_async_copy(probes_ref.at[:, :, :, mine], own_ref, sem.at[1]),
        pltpu.make_async_copy(coefficients_ref.at[:, :, mine], window_ref, sem.at[2]),
        pltpu.make_async_copy(observed_ref.at[:, :, mine], seen_ref, sem.at[3]),
    ]
    for copy in copies:
        copy.start()
    for copy in copies:
        copy.wait()


def prep_kernel(window_ref, expanded_ref):
    tiles = expanded_ref.shape[1]
    chunk = chunk_of(tiles)
    scale = 4.0 / (upper_edge - lower_edge)
    shift = 2.0 * (upper_edge + lower_edge) / (upper_edge - lower_edge)

    def body(step, carry):
        for k in range(chunk):
            tile = step * chunk + k
            cols = tile_columns(tile)
            kappa, across, along, skew = [
                [window_ref[2 * kind + c, :, cols] for c in range(2)] for kind in range(4)
            ]
            coupling = scale * window_ref[8, :, cols]
            for c in range(2):
                values = (
                    scale * (kappa[c] + 2.0 * (across[c] + along[c])) - shift,
                    -scale * across[c],
                    -scale * along[c],
                    -0.5 * scale * skew[c],
                    coupling,
                )
                for kind, value in enumerate(values):
                    for probe in range(4):
                        expanded_ref[kind, tile, pl.ds(4 * c + probe, SUBS, stride=SUBS), :] = value
        return carry

    lax.fori_loop(0, tiles // chunk, body, 0)


def layout_kernel(own_ref, other_ref, seen_ref, z_ref, top_ref, bottom_ref):
    tiles = z_ref.shape[0]
    chunk = chunk_of(tiles)

    def body(step, carry):
        for k in range(chunk):
            tile = step * chunk + k
            cols = tile_columns(tile)
            for c in range(2):
                for probe in range(2):
                    z_ref[tile, pl.ds(4 * c + probe, SUBS, stride=SUBS), :] = own_ref[probe, c, :, cols]
                    z_ref[tile, pl.ds(4 * c + 2 + probe, SUBS, stride=SUBS), :] = other_ref[probe, c, :, cols]
        return carry

    lax.fori_loop(0, tiles // chunk, body, 0)
    for tile in range(tiles):
        top_ref[tile] = z_ref[tile, sub(0), :]
        bottom_ref[tile] = z_ref[tile, sub(SUBS - 1), :]
    for c in range(2):
        for tile in range(tiles):
            place = c * tiles + tile
            cols = pl.ds(tile * LANES, LANES)
            at = (tiles + place // SUBS, pl.ds(place % SUBS, 1))
            top_ref[at[0], at[1], :] = seen_ref[c, 0:1, cols]
            bottom_ref[at[0], at[1], :] = seen_ref[c, SUBS - 1 : SUBS, cols]


def step_kernel(upper, constants, offset, other_row, tiles, *refs):
    weight, scale, subtract = constants
    own_ref, other_ref, halo_ref, z_ref, coefficients_ref = refs[:5]
    rest = refs[5:]
    before_ref = None
    if subtract:
        before_ref, rest = rest[0], rest[1:]
    out_ref, edge_ref = rest
    first_row = 0 if upper else 4
    chunk = chunk_of(tiles)

    def load(row):
        if row == (-1 if upper else 4):
            return lambda tile: halo_ref[tile]
        if row == (4 if upper else -1):
            return lambda tile: other_ref[tile, sub(other_row), :]
        return lambda tile: own_ref[tile, sub(offset + row), :]

    def body(step, carry):
        edges = masks()
        first = step * chunk
        for k in range(chunk):
            tile = first + k
            values, sums, slopes = [], [], []
            for row in range(-1, 5):
                loader = load(row)
                here = loader(tile)
                if k == 0:
                    before = jnp.where(first > 0, loader(jnp.maximum(first - 1, 0)), 0.0)
                else:
                    before = loader(tile - 1)
                if k == chunk - 1:
                    last = first + chunk < tiles
                    after = jnp.where(last, loader(jnp.minimum(first + chunk, tiles - 1)), 0.0)
                else:
                    after = loader(tile + 1)
                left, right = beside(before, here, after, edges)
                values.append(here)
                sums.append(left + right)
                slopes.append(right - left)
            for row in range(4):
                rows = sub(first_row + row)
                coefs = [coefficients_ref[kind, tile, rows, :] for kind in range(5)]
                total = (
                    coefs[0] * values[row + 1]
                    + coefs[1] * sums[row + 1]
                    + coefs[2] * (values[row] + values[row + 2])
                    + coefs[3] * (slopes[row + 2] - slopes[row])
                    + coefs[4] * pltpu.roll(values[row + 1], 4, 0)
                )
                if scale != 1.0:
                    total = scale * total
                total = total + weight * z_ref[tile, rows, :]
                if subtract:
                    total = total - before_ref[tile, sub(row), :]
                out_ref[tile, sub(row), :] = total
                if row == (0 if upper else 3):
                    edge_ref[tile] = total
        return carry

    lax.fori_loop(0, tiles // chunk, body, 0)


def data_kernel(tiles, seen_ref, up_ref, down_ref, out_ref):
    chunk = chunk_of(tiles)

    def halo(ref, c, tile):
        place = c * tiles + tile
        return jnp.broadcast_to(ref[tiles + place // SUBS, pl.ds(place % SUBS, 1), :], (SUBS, LANES))

    def body(step, carry):
        edges = masks()
        row = lax.broadcasted_iota(jnp.int32, (SUBS, LANES), 0)
        first = step * chunk
        kept = [[], []]
        for c in range(2):
            values = window_tiles(lambda tile: seen_ref[c, :, tile_columns(tile)], first, chunk, tiles)
            ups = window_tiles(lambda tile: halo(up_ref, c, tile), first, chunk, tiles)
            downs = window_tiles(lambda tile: halo(down_ref, c, tile), first, chunk, tiles)
            aboves = [jnp.where(row == 0, u, pltpu.roll(v, 1, 0)) for u, v in zip(ups, values)]
            belows = [jnp.where(row == SUBS - 1, d, pltpu.roll(v, SUBS - 1, 0)) for d, v in zip(downs, values)]
            tilts = [b - a for a, b in zip(aboves, belows)]
            for k in range(chunk):
                tile = first + k
                value = values[k + 1]
                left, right = beside(values[k], value, values[k + 2], edges)
                low, high = beside(tilts[k], tilts[k + 1], tilts[k + 2], edges)
                half = -0.5 * value
                out_ref[tile, c] = half * value
                out_ref[tile, 2 + c] = half * (2.0 * value - (left + right))
                out_ref[tile, 4 + c] = half * (2.0 * value - (aboves[k + 1] + belows[k + 1]))
                out_ref[tile, 6 + c] = (-0.5 * half) * (high - low)
                kept[c].append(value)
        for k in range(chunk):
            out_ref[first + k, 8] = -(kept[0][k] * kept[1][k])
        return carry

    lax.fori_loop(0, tiles // chunk, body, 0)


def gradient_kernel(tiles, factor, z_ref, top_ref, bottom_ref, data_ref, out_ref, products):
    kept = out_ref.shape[2] // LANES
    offset = lax.axis_index("probe") * (tiles - kept)
    count = products.shape[0]

    def load(row):
        if row < 4:
            return lambda tile: top_ref[tile, sub(row), :]
        return lambda tile: bottom_ref[tile, sub(row - 4), :]

    def body(step, carry):
        edges = masks()
        for k in range(count):
            index = step * count + k
            tile = index + offset
            values, sums, slopes = [], [], []
            for row in range(SUBS):
                loader = load(row)
                before, here, after = window_tiles(loader, tile, 1, tiles)
                left, right = beside(before, here, after, edges)
                values.append(here)
                sums.append(left + right)
                slopes.append(right - left)
            for row in range(SUBS):
                left = factor * z_ref[tile, sub(row), :]
                value = values[row]
                twice = 2.0 * value
                if row == 0:
                    along, skew = values[1], slopes[1]
                elif row == SUBS - 1:
                    along, skew = values[row - 1], -slopes[row - 1]
                else:
                    along, skew = values[row - 1] + values[row + 1], slopes[row + 1] - slopes[row - 1]
                products[k, 0, sub(row), :] = left * value
                products[k, 1, sub(row), :] = left * (twice - sums[row])
                products[k, 2, sub(row), :] = left * (twice - along)
                products[k, 3, sub(row), :] = (-0.5 * left) * skew
                products[k, 4, sub(row), :] = left * pltpu.roll(value, 4, 0)
        for k in range(count):
            index = step * count + k
            tile = index + offset
            cols = tile_columns(index)
            for kind in range(5):
                parts = [products[k, kind, pl.ds(s, SUBS, stride=SUBS), :] for s in range(SUBS)]
                sums = [(parts[4 * c] + parts[4 * c + 1]) + (parts[4 * c + 2] + parts[4 * c + 3]) for c in range(2)]
                if kind < 4:
                    for c in range(2):
                        out_ref[2 * kind + c, :, cols] = sums[c] + data_ref[tile, 2 * kind + c]
                else:
                    out_ref[8, :, cols] = (sums[0] + sums[1]) + data_ref[tile, 8]
        return carry

    lax.fori_loop(0, kept // count, body, 0)


def finish_kernel(tiles, factor, part_ref, z_ref, up_ref, down_ref, out_ref, fixed, sem):
    kept = out_ref.shape[2] // LANES
    offset = lax.axis_index("probe") * (tiles - kept)
    count = max(n for n in range(1, 9) if kept % n == 0)
    early = [
        pltpu.make_async_copy(part_ref.at[pl.ds(0, 4)], out_ref.at[pl.ds(0, 4)], sem.at[0]),
        pltpu.make_async_copy(part_ref.at[pl.ds(8, 1)], out_ref.at[pl.ds(8, 1)], sem.at[1]),
    ]
    for copy in early:
        copy.start()

    def body(step, carry):
        edges = masks()
        row = lax.broadcasted_iota(jnp.int32, (SUBS, LANES), 0)
        for k in range(count):
            index = step * count + k
            tile = index + offset
            cols = tile_columns(index)
            adds = []
            for ref, z_row, sign in ((up_ref, 0, 0.5), (down_ref, SUBS - 1, -0.5)):
                before, here, after = window_tiles(lambda at: ref[at], tile, 1, tiles)
                left, right = beside(before, here, after, edges)
                z = factor * z_ref[tile, sub(z_row), :]
                pair = []
                for term in (-z * here, (sign * z) * (right - left)):
                    term = term + pltpu.roll(term, 1, 0)
                    pair.append(term + pltpu.roll(term, 2, 0))
                adds.append(pair)
            for kind in range(2):
                for c in range(2):
                    at = 4 * c + 3
                    channel = 2 * kind + c
                    top = jnp.broadcast_to(adds[0][kind][at : at + 1, :], (SUBS, LANES))
                    bottom = jnp.broadcast_to(adds[1][kind][at : at + 1, :], (SUBS, LANES))
                    more = jnp.where(row == 0, top, jnp.where(row == SUBS - 1, bottom, 0.0))
                    fixed[channel, :, cols] = part_ref[4 + channel, :, cols] + more
        return carry

    lax.fori_loop(0, kept // count, body, 0)
    late = pltpu.make_async_copy(fixed, out_ref.at[pl.ds(4, 4)], sem.at[2])
    late.start()
    late.wait()
    for copy in early:
        copy.wait()


def per_device(observations, coefficients, probes):
    weights = cheb_weights(CHEB, lower_edge, upper_edge)
    f32 = jnp.float32
    columns = probes.shape[3]
    share = columns // lax.axis_size("probe")
    width = share + LANES
    tiles = width // LANES
    kept = share // LANES
    seen_tiles = -(-2 * tiles // SUBS)
    rows = lax.axis_size("row")
    down_pairs = [(i, i + 1) for i in range(rows - 1)]
    up_pairs = [(i + 1, i) for i in range(rows - 1)]

    def to_next(edge):
        return lax.ppermute(edge, "row", down_pairs)

    def to_previous(edge):
        return lax.ppermute(edge, "row", up_pairs)

    def call(kernel, name, vregs, operands, outs, scratch=(), in_specs=None, out_specs=None):
        return pl.pallas_call(
            kernel,
            out_shape=outs,
            in_specs=in_specs or [vmem_spec()] * len(operands),
            out_specs=out_specs or jax.tree.map(lambda _: vmem_spec(), outs),
            scratch_shapes=scratch,
            compiler_params=params(),
            cost_estimate=cost(vregs),
            name=name,
        )(*operands)

    theirs, own, seen, window = call(
        functools.partial(load_kernel, width),
        "load",
        100,
        [
            pltpu.with_memory_space_constraint(array, pltpu.HBM)
            for array in (probes, observations, coefficients)
        ],
        [
            pltpu.VMEM((2, 2, SUBS, width), f32),
            pltpu.VMEM((2, 2, SUBS, width), f32),
            pltpu.VMEM((2, SUBS, width), f32),
            pltpu.VMEM((9, SUBS, width), f32),
        ],
        [pltpu.SemaphoreType.DMA((4,))],
        [pl.BlockSpec(memory_space=pltpu.HBM)] * 3,
    )
    other = lax.ppermute(theirs, "probe", [(0, 1), (1, 0)])
    expanded = call(
        prep_kernel, "prep", 5 * 8 * tiles, (window,), pltpu.VMEM((5, tiles, SUBS * SUBS, LANES), f32)
    )
    own, expanded = lax.optimization_barrier((own, expanded))
    message = (tiles + seen_tiles, SUBS, LANES)
    z, top, bottom = call(
        layout_kernel,
        "layout",
        8 * tiles,
        (own, other, seen),
        [pltpu.VMEM((tiles, SUBS * SUBS, LANES), f32), pltpu.VMEM(message, f32), pltpu.VMEM(message, f32)],
    )

    def half(upper, constants, own, other_half, halo, before):
        shared = own is z
        offset = (0 if upper else 4) if shared else 0
        other_row = (4 if upper else 3) if shared else (0 if upper else 3)
        operands = [own, other_half, halo, z, expanded]
        if constants[2]:
            operands.append(before)
        return call(
            functools.partial(step_kernel, upper, constants, offset, other_row, tiles),
            "upper" if upper else "lower",
            4 * tiles,
            operands,
            [pltpu.VMEM((tiles, 4 * SUBS, LANES), f32), pltpu.VMEM((tiles, SUBS, LANES), f32)],
        )

    first_up, first_down = to_next(bottom), to_previous(top)
    up, down = first_up, first_down
    now = (z, z)
    before = (None, None)
    for order in range(CHEB - 1, -1, -1):
        if order == CHEB - 1:
            constants = (weights[order], weights[CHEB], False)
        elif order == CHEB - 2:
            constants = (weights[order] - weights[CHEB], 1.0, False)
        elif order > 0:
            constants = (weights[order], 1.0, True)
        else:
            constants = (weights[0], 0.5, True)
        upper, top = half(True, constants, now[0], now[1], up, before[0])
        next_down = to_previous(top)
        lower, bottom = half(False, constants, now[1], now[0], down, before[1])
        next_up = to_next(bottom)
        before, now = now, (upper, lower)
        up, down = next_up, next_down

    data = call(
        functools.partial(data_kernel, tiles),
        "data",
        9 * tiles,
        (seen, first_up, first_down),
        pltpu.VMEM((tiles, 9, SUBS, LANES), f32),
    )
    factor = 0.5 / (probes.shape[0] * lax.axis_size("probe"))
    count = max(n for n in range(1, 5) if kept % n == 0)
    part = call(
        functools.partial(gradient_kernel, tiles, factor),
        "gradient",
        24 * tiles,
        (z, now[0], now[1], data),
        pltpu.VMEM((9, SUBS, share), f32),
        [pltpu.VMEM((count, 5, SUBS * SUBS, LANES), f32)],
    )
    return call(
        functools.partial(finish_kernel, tiles, factor),
        "finish",
        8 * tiles,
        (part, z, up, down),
        jax.ShapeDtypeStruct((9, SUBS, share), f32),
        [pltpu.VMEM((4, SUBS, share), f32), pltpu.SemaphoreType.DMA((3,))],
        None,
        pl.BlockSpec(memory_space=pltpu.HBM),
    )


def solution(mesh):
    in_specs = (P("group", "row", None), P("group", "row", None), P("probe", "group", "row", None))
    out_specs = P("group", "row", "probe")
    return jax.shard_map(
        per_device, mesh=mesh, in_specs=in_specs, out_specs=out_specs, check_vma=False
    )
```

```python
import functools
import math

import jax
import jax.numpy as jnp
from jax import lax
from jax.experimental import pallas as pl
from jax.experimental.pallas import tpu as pltpu
from jax.sharding import PartitionSpec as P

CHEB = 6
LANES = 128
SUBS = 8

lower_edge = 0.25
upper_edge = 12.0


def cheb_weights(degree, low_end, high_end):
    count = degree + 1
    values = []
    for order in range(count):
        accum = 0.0
        for node in range(count):
            angle = math.pi * (node + 0.5) / count
            point = 0.5 * (high_end - low_end) * math.cos(angle) + 0.5 * (high_end + low_end)
            accum += math.cos(order * angle) / point
        accum = accum * 2.0 / count
        if order == 0:
            accum = accum * 0.5
        values.append(accum)
    return values


def vmem_spec():
    return pl.BlockSpec(memory_space=pltpu.VMEM)


def params():
    return pltpu.CompilerParams(vmem_limit_bytes=40 * 1024 * 1024)


def cost(vregs):
    return pl.CostEstimate(flops=vregs * 1024 * 20, bytes_accessed=vregs * 4096 * 4, transcendentals=0)


def masks():
    lane = lax.broadcasted_iota(jnp.int32, (SUBS, LANES), 1)
    return lane == 0, lane == LANES - 1


def window_tiles(load, first, count, total):
    before = jnp.where(first > 0, load(jnp.maximum(first - 1, 0)), 0.0)
    after = jnp.where(first + count < total, load(jnp.minimum(first + count, total - 1)), 0.0)
    return [before] + [load(first + k) for k in range(count)] + [after]


def beside(before, here, after, edges):
    left = pltpu.roll(jnp.where(edges[1], before, here), 1, 1)
    right = pltpu.roll(jnp.where(edges[0], after, here), LANES - 1, 1)
    return left, right


def sub(row):
    return pl.ds(row * SUBS, SUBS)


def tile_columns(tile):
    return pl.ds(pl.multiple_of(tile * LANES, LANES), LANES)


def chunk_of(tiles):
    return max(count for count in range(1, 12) if tiles % count == 0)


def load_kernel(width, probes_ref, observed_ref, coefficients_ref, theirs_ref, own_ref, seen_ref, window_ref, sem):
    core = lax.axis_index("probe")
    move = probes_ref.shape[3] - width
    mine = pl.ds(pl.multiple_of(core * move, LANES), width)
    other = pl.ds(pl.multiple_of((1 - core) * move, LANES), width)
    copies = [
        pltpu.make_async_copy(probes_ref.at[:, :, :, other], theirs_ref, sem.at[0]),
        pltpu.make_async_copy(probes_ref.at[:, :, :, mine], own_ref, sem.at[1]),
        pltpu.make_async_copy(coefficients_ref.at[:, :, mine], window_ref, sem.at[2]),
        pltpu.make_async_copy(observed_ref.at[:, :, mine], seen_ref, sem.at[3]),
    ]
    for copy in copies:
        copy.start()
    for copy in copies:
        copy.wait()


def combine(kappa, across, along, skew, coupling):
    scale = 4.0 / (upper_edge - lower_edge)
    shift = 2.0 * (upper_edge + lower_edge) / (upper_edge - lower_edge)
    return (
        scale * (kappa + 2.0 * (across + along)) - shift,
        -scale * across,
        -scale * along,
        -0.5 * scale * skew,
        scale * coupling,
    )


def prep_kernel(window_ref, seen_ref, expanded_ref, top_ref, bottom_ref, eight, rest):
    tiles = expanded_ref.shape[1]
    chunk = chunk_of(tiles)
    rest[...] = jnp.zeros_like(rest)

    def body(step, carry):
        for k in range(chunk):
            tile = step * chunk + k
            cols = tile_columns(tile)
            raw = [window_ref[channel, :, cols] for channel in range(9)]
            for c in range(2):
                values = combine(raw[c], raw[2 + c], raw[4 + c], raw[6 + c], raw[8])
                for kind, value in enumerate(values):
                    for probe in range(4):
                        expanded_ref[kind, tile, pl.ds(4 * c + probe, SUBS, stride=SUBS), :] = value
            for channel in range(8):
                eight[tile, pl.ds(channel, SUBS, stride=SUBS), :] = raw[channel]
            top_ref[tile] = eight[tile, sub(0), :]
            bottom_ref[tile] = eight[tile, sub(SUBS - 1), :]
        return carry

    lax.fori_loop(0, tiles // chunk, body, 0)
    for tile in range(tiles):
        cols = pl.ds(tile * LANES, LANES)
        for slot, row in enumerate((window_ref[8, :, cols], seen_ref[0, :, cols], seen_ref[1, :, cols])):
            rest[tile // 2, pl.ds(4 * (tile % 2) + slot, SUBS, stride=SUBS), :] = row
    for pair in range(rest.shape[0]):
        top_ref[tiles + pair] = rest[pair, sub(0), :]
        bottom_ref[tiles + pair] = rest[pair, sub(SUBS - 1), :]


def layout_kernel(own_ref, other_ref, more_top_ref, more_bottom_ref, z_ref, top_ref, bottom_ref):
    tiles = z_ref.shape[0]
    chunk = chunk_of(tiles)

    def body(step, carry):
        for k in range(chunk):
            tile = step * chunk + k
            cols = tile_columns(tile)
            for c in range(2):
                for probe in range(2):
                    z_ref[tile, pl.ds(4 * c + probe, SUBS, stride=SUBS), :] = own_ref[probe, c, :, cols]
                    z_ref[tile, pl.ds(4 * c + 2 + probe, SUBS, stride=SUBS), :] = other_ref[probe, c, :, cols]
        return carry

    lax.fori_loop(0, tiles // chunk, body, 0)
    for tile in range(tiles):
        for row in range(2):
            top_ref[2 * tile + row] = z_ref[tile, sub(row), :]
            bottom_ref[2 * tile + row] = z_ref[tile, sub(SUBS - 2 + row), :]
    for index in range(more_top_ref.shape[0]):
        top_ref[2 * tiles + index] = more_top_ref[index]
        bottom_ref[2 * tiles + index] = more_bottom_ref[index]


def rim(halo_ref, rim_ref, tiles):
    chunk = chunk_of(tiles)

    def spread(ref, index, row):
        return jnp.broadcast_to(ref[index, pl.ds(row, 1), :], (SUBS, LANES))

    def body(step, carry):
        low = lax.broadcasted_iota(jnp.int32, (SUBS, LANES), 0) < 4
        for k in range(chunk):
            tile = step * chunk + k
            pairs = [
                jnp.where(low, spread(halo_ref, 2 * tiles + tile, 2 * kind), spread(halo_ref, 2 * tiles + tile, 2 * kind + 1))
                for kind in range(4)
            ]
            coupling = spread(halo_ref, 3 * tiles + tile // 2, 4 * (tile % 2))
            for kind, value in enumerate(combine(*pairs, coupling)):
                rim_ref[kind, tile] = value
        return carry

    lax.fori_loop(0, tiles // chunk, body, 0)


def sweep(tiles, low, count, load, factor, z_row, before, constants, store):
    weight, scale = constants
    chunk = chunk_of(tiles)

    def body(step, carry):
        edges = masks()
        first = step * chunk
        for k in range(chunk):
            tile = first + k
            values, sums, slopes = [], [], []
            for row in range(low - 1, low + count + 1):
                here = load(row, tile)
                if k == 0:
                    last = jnp.where(first > 0, load(row, jnp.maximum(first - 1, 0)), 0.0)
                else:
                    last = load(row, tile - 1)
                if k == chunk - 1:
                    more = first + chunk < tiles
                    after = jnp.where(more, load(row, jnp.minimum(first + chunk, tiles - 1)), 0.0)
                else:
                    after = load(row, tile + 1)
                left, right = beside(last, here, after, edges)
                values.append(here)
                sums.append(left + right)
                slopes.append(right - left)
            for at in range(count):
                row = low + at
                total = (
                    factor(0, row, tile) * values[at + 1]
                    + factor(1, row, tile) * sums[at + 1]
                    + factor(2, row, tile) * (values[at] + values[at + 2])
                    + factor(3, row, tile) * (slopes[at + 2] - slopes[at])
                    + factor(4, row, tile) * pltpu.roll(values[at + 1], 4, 0)
                )
                if scale != 1.0:
                    total = scale * total
                total = total + weight * z_row(row, tile)
                if before is not None:
                    total = total - before(row, tile)
                store(row, tile, total)
        return carry

    lax.fori_loop(0, tiles // chunk, body, 0)


def middle_kernel(steps, tiles, first_round, *refs):
    if first_round:
        z_ref, expanded_ref, once_ref, twice_ref = refs
    else:
        z_ref, expanded_ref, top_ref, inner_ref, bottom_ref, older_ref, once_ref, twice_ref = refs

    def now(row, tile):
        if first_round:
            return z_ref[tile, sub(row), :]
        if row < 2:
            return top_ref[2 * tile + row]
        if row < 6:
            return inner_ref[tile, sub(row - 2), :]
        return bottom_ref[2 * tile + row - 6]

    def factor(kind, row, tile):
        return expanded_ref[kind, tile, sub(row), :]

    def z_row(row, tile):
        return z_ref[tile, sub(row), :]

    def once(row, tile):
        return once_ref[tile, sub(row - 1), :]

    def store_once(row, tile, value):
        once_ref[tile, sub(row - 1), :] = value

    def store_twice(row, tile, value):
        twice_ref[tile, sub(row - 2), :] = value

    older = None if first_round else (lambda row, tile: older_ref[tile, sub(row - 1), :])
    sweep(tiles, 1, 6, now, factor, z_row, older, steps[0], store_once)
    sweep(tiles, 2, 4, once, factor, z_row, None if first_round else now, steps[1], store_twice)


def edge_kernel(upper, steps, tiles, first_round, last_round, *refs):
    halo_ref, z_halo_ref, z_ref, expanded_ref, inner_ref = refs[:5]
    refs = refs[5:]
    if first_round:
        once_ref, twice_ref, rim_ref = refs[:3]
        rim(halo_ref, rim_ref, tiles)
    else:
        rim_ref, top_ref, older_ref, once_ref, twice_ref = refs[:5]
    row_ref = refs[-1]
    base = 0 if upper else 6
    low = -1 if upper else 7

    def now(row, tile):
        if row < 0 or row > 7:
            return halo_ref[2 * tile + (row + 2 if upper else row - 8)]
        if first_round:
            return z_ref[tile, sub(row), :]
        return top_ref[2 * tile + row - base]

    def factor(kind, row, tile):
        if row < 0 or row > 7:
            return rim_ref[kind, tile]
        return expanded_ref[kind, tile, sub(row), :]

    def z_row(row, tile):
        if row < 0 or row > 7:
            return z_halo_ref[2 * tile + (1 if upper else 0)]
        return z_ref[tile, sub(row), :]

    def once(row, tile):
        if 1 <= row <= 6:
            return inner_ref[tile, sub(row - 1), :]
        return once_ref[tile, sub(row - low), :]

    def store_once(row, tile, value):
        once_ref[tile, sub(row - low), :] = value

    def store_twice(row, tile, value):
        twice_ref[2 * tile + row - base] = value
        if last_round and row == (0 if upper else 7):
            row_ref[tile] = value

    older = None if first_round else (lambda row, tile: older_ref[tile, sub(row - low), :])
    sweep(tiles, low, 2, now, factor, z_row, older, steps[0], store_once)
    sweep(tiles, base, 2, once, factor, z_row, None if first_round else now, steps[1], store_twice)


def data_kernel(tiles, seen_ref, up_ref, down_ref, out_ref):
    chunk = chunk_of(tiles)

    def halo(ref, c, tile):
        row = ref[3 * tiles + tile // 2, pl.ds(4 * (tile % 2) + 1 + c, 1), :]
        return jnp.broadcast_to(row, (SUBS, LANES))

    def body(step, carry):
        edges = masks()
        row = lax.broadcasted_iota(jnp.int32, (SUBS, LANES), 0)
        first = step * chunk
        kept = [[], []]
        for c in range(2):
            values = window_tiles(lambda tile: seen_ref[c, :, tile_columns(tile)], first, chunk, tiles)
            ups = window_tiles(lambda tile: halo(up_ref, c, tile), first, chunk, tiles)
            downs = window_tiles(lambda tile: halo(down_ref, c, tile), first, chunk, tiles)
            aboves = [jnp.where(row == 0, u, pltpu.roll(v, 1, 0)) for u, v in zip(ups, values)]
            belows = [jnp.where(row == SUBS - 1, d, pltpu.roll(v, SUBS - 1, 0)) for d, v in zip(downs, values)]
            tilts = [b - a for a, b in zip(aboves, belows)]
            for k in range(chunk):
                tile = first + k
                value = values[k + 1]
                left, right = beside(values[k], value, values[k + 2], edges)
                low, high = beside(tilts[k], tilts[k + 1], tilts[k + 2], edges)
                half = -0.5 * value
                out_ref[tile, c] = half * value
                out_ref[tile, 2 + c] = half * (2.0 * value - (left + right))
                out_ref[tile, 4 + c] = half * (2.0 * value - (aboves[k + 1] + belows[k + 1]))
                out_ref[tile, 6 + c] = (-0.5 * half) * (high - low)
                kept[c].append(value)
        for k in range(chunk):
            out_ref[first + k, 8] = -(kept[0][k] * kept[1][k])
        return carry

    lax.fori_loop(0, tiles // chunk, body, 0)


def gradient_kernel(tiles, factor, z_ref, top_ref, inner_ref, bottom_ref, data_ref, out_ref, products):
    kept = out_ref.shape[2] // LANES
    offset = lax.axis_index("probe") * (tiles - kept)
    count = products.shape[0]

    def load(row):
        if row < 2:
            return lambda tile: top_ref[2 * tile + row]
        if row < 6:
            return lambda tile: inner_ref[tile, sub(row - 2), :]
        return lambda tile: bottom_ref[2 * tile + row - 6]

    def body(step, carry):
        edges = masks()
        for k in range(count):
            index = step * count + k
            tile = index + offset
            values, sums, slopes = [], [], []
            for row in range(SUBS):
                loader = load(row)
                before, here, after = window_tiles(loader, tile, 1, tiles)
                left, right = beside(before, here, after, edges)
                values.append(here)
                sums.append(left + right)
                slopes.append(right - left)
            for row in range(SUBS):
                left = factor * z_ref[tile, sub(row), :]
                value = values[row]
                twice = 2.0 * value
                if row == 0:
                    along, skew = values[1], slopes[1]
                elif row == SUBS - 1:
                    along, skew = values[row - 1], -slopes[row - 1]
                else:
                    along, skew = values[row - 1] + values[row + 1], slopes[row + 1] - slopes[row - 1]
                products[k, 0, sub(row), :] = left * value
                products[k, 1, sub(row), :] = left * (twice - sums[row])
                products[k, 2, sub(row), :] = left * (twice - along)
                products[k, 3, sub(row), :] = (-0.5 * left) * skew
                products[k, 4, sub(row), :] = left * pltpu.roll(value, 4, 0)
        for k in range(count):
            index = step * count + k
            tile = index + offset
            cols = tile_columns(index)
            for kind in range(5):
                parts = [products[k, kind, pl.ds(s, SUBS, stride=SUBS), :] for s in range(SUBS)]
                sums = [(parts[4 * c] + parts[4 * c + 1]) + (parts[4 * c + 2] + parts[4 * c + 3]) for c in range(2)]
                if kind < 4:
                    for c in range(2):
                        out_ref[2 * kind + c, :, cols] = sums[c] + data_ref[tile, 2 * kind + c]
                else:
                    out_ref[8, :, cols] = (sums[0] + sums[1]) + data_ref[tile, 8]
        return carry

    lax.fori_loop(0, kept // count, body, 0)


def finish_kernel(tiles, factor, part_ref, z_ref, up_ref, down_ref, out_ref, fixed, sem):
    kept = out_ref.shape[2] // LANES
    offset = lax.axis_index("probe") * (tiles - kept)
    count = max(n for n in range(1, 9) if kept % n == 0)
    early = [
        pltpu.make_async_copy(part_ref.at[pl.ds(0, 4)], out_ref.at[pl.ds(0, 4)], sem.at[0]),
        pltpu.make_async_copy(part_ref.at[pl.ds(8, 1)], out_ref.at[pl.ds(8, 1)], sem.at[1]),
    ]
    for copy in early:
        copy.start()

    def body(step, carry):
        edges = masks()
        row = lax.broadcasted_iota(jnp.int32, (SUBS, LANES), 0)
        for k in range(count):
            index = step * count + k
            tile = index + offset
            cols = tile_columns(index)
            adds = []
            for ref, z_row, sign in ((up_ref, 0, 0.5), (down_ref, SUBS - 1, -0.5)):
                before, here, after = window_tiles(lambda at: ref[at], tile, 1, tiles)
                left, right = beside(before, here, after, edges)
                z = factor * z_ref[tile, sub(z_row), :]
                pair = []
                for term in (-z * here, (sign * z) * (right - left)):
                    term = term + pltpu.roll(term, 1, 0)
                    pair.append(term + pltpu.roll(term, 2, 0))
                adds.append(pair)
            for kind in range(2):
                for c in range(2):
                    at = 4 * c + 3
                    channel = 2 * kind + c
                    top = jnp.broadcast_to(adds[0][kind][at : at + 1, :], (SUBS, LANES))
                    bottom = jnp.broadcast_to(adds[1][kind][at : at + 1, :], (SUBS, LANES))
                    more = jnp.where(row == 0, top, jnp.where(row == SUBS - 1, bottom, 0.0))
                    fixed[channel, :, cols] = part_ref[4 + channel, :, cols] + more
        return carry

    lax.fori_loop(0, kept // count, body, 0)
    late = pltpu.make_async_copy(fixed, out_ref.at[pl.ds(4, 4)], sem.at[2])
    late.start()
    late.wait()
    for copy in early:
        copy.wait()


def per_device(observations, coefficients, probes):
    weights = cheb_weights(CHEB, lower_edge, upper_edge)
    f32 = jnp.float32
    columns = probes.shape[3]
    share = columns // lax.axis_size("probe")
    width = share + LANES
    tiles = width // LANES
    kept = share // LANES
    rows = lax.axis_size("row")
    down_pairs = [(i, i + 1) for i in range(rows - 1)]
    up_pairs = [(i + 1, i) for i in range(rows - 1)]

    def to_next(edge):
        return lax.ppermute(edge, "row", down_pairs)

    def to_previous(edge):
        return lax.ppermute(edge, "row", up_pairs)

    def call(kernel, name, vregs, operands, outs, scratch=(), in_specs=None, out_specs=None):
        return pl.pallas_call(
            kernel,
            out_shape=outs,
            in_specs=in_specs or [vmem_spec()] * len(operands),
            out_specs=out_specs or jax.tree.map(lambda _: vmem_spec(), outs),
            scratch_shapes=scratch,
            compiler_params=params(),
            cost_estimate=cost(vregs),
            name=name,
        )(*operands)

    theirs, own, seen, window = call(
        functools.partial(load_kernel, width),
        "load",
        100,
        [
            pltpu.with_memory_space_constraint(array, pltpu.HBM)
            for array in (probes, observations, coefficients)
        ],
        [
            pltpu.VMEM((2, 2, SUBS, width), f32),
            pltpu.VMEM((2, 2, SUBS, width), f32),
            pltpu.VMEM((2, SUBS, width), f32),
            pltpu.VMEM((9, SUBS, width), f32),
        ],
        [pltpu.SemaphoreType.DMA((4,))],
        [pl.BlockSpec(memory_space=pltpu.HBM)] * 3,
    )
    other = lax.ppermute(theirs, "probe", [(0, 1), (1, 0)])
    pairs = -(-tiles // 2)
    more = (tiles + pairs, SUBS, LANES)
    expanded, more_top, more_bottom = call(
        prep_kernel,
        "prep",
        5 * 8 * tiles,
        (window, seen),
        [pltpu.VMEM((5, tiles, SUBS * SUBS, LANES), f32), pltpu.VMEM(more, f32), pltpu.VMEM(more, f32)],
        [pltpu.VMEM((tiles, SUBS * SUBS, LANES), f32), pltpu.VMEM((pairs, SUBS * SUBS, LANES), f32)],
    )
    own, expanded = lax.optimization_barrier((own, expanded))
    message = (2 * tiles + more[0], SUBS, LANES)
    z, top, bottom = call(
        layout_kernel,
        "layout",
        8 * tiles,
        (own, other, more_top, more_bottom),
        [pltpu.VMEM((tiles, SUBS * SUBS, LANES), f32), pltpu.VMEM(message, f32), pltpu.VMEM(message, f32)],
    )

    first_up, first_down = to_next(bottom), to_previous(top)
    up, down = first_up, first_down
    rounds = CHEB // 2
    inner = once = rims = None
    for index in range(rounds):
        first_round, last_round = index == 0, index == rounds - 1
        high = CHEB - 1 - 2 * index
        if first_round:
            steps = ((weights[high], weights[CHEB]), (weights[high - 1] - weights[CHEB], 1.0))
        else:
            steps = ((weights[high], 1.0), (weights[high - 1], 0.5 if last_round else 1.0))
        operands = [z, expanded]
        if not first_round:
            operands += [top, inner, bottom, once[1]]
        inner_once, inner_twice = call(
            functools.partial(middle_kernel, steps, tiles, first_round),
            "middle",
            10 * tiles,
            operands,
            [pltpu.VMEM((tiles, 6 * SUBS, LANES), f32), pltpu.VMEM((tiles, 4 * SUBS, LANES), f32)],
        )
        results = []
        for upper in (True, False):
            halo, z_halo = (up, first_up) if upper else (down, first_down)
            operands = [halo, z_halo, z, expanded, inner_once]
            outs = [pltpu.VMEM((tiles, 2 * SUBS, LANES), f32), pltpu.VMEM((2 * tiles, SUBS, LANES), f32)]
            if first_round:
                outs.append(pltpu.VMEM((5, tiles, SUBS, LANES), f32))
            else:
                operands += [rims[0 if upper else 1], top if upper else bottom, once[0 if upper else 2]]
            if last_round:
                outs.append(pltpu.VMEM((tiles, SUBS, LANES), f32))
            results.append(
                call(
                    functools.partial(edge_kernel, upper, steps, tiles, first_round, last_round),
                    "upper" if upper else "lower",
                    4 * tiles,
                    operands,
                    outs,
                )
            )
        over, under = results
        once = (over[0], inner_once, under[0])
        top, inner, bottom = over[1], inner_twice, under[1]
        if first_round:
            rims = (over[2], under[2])
        if last_round:
            down, up = to_previous(over[-1]), to_next(under[-1])
        else:
            down, up = to_previous(top), to_next(bottom)

    data = call(
        functools.partial(data_kernel, tiles),
        "data",
        9 * tiles,
        (seen, first_up, first_down),
        pltpu.VMEM((tiles, 9, SUBS, LANES), f32),
    )
    factor = 0.5 / (probes.shape[0] * lax.axis_size("probe"))
    count = max(n for n in range(1, 5) if kept % n == 0)
    part = call(
        functools.partial(gradient_kernel, tiles, factor),
        "gradient",
        24 * tiles,
        (z, top, inner, bottom, data),
        pltpu.VMEM((9, SUBS, share), f32),
        [pltpu.VMEM((count, 5, SUBS * SUBS, LANES), f32)],
    )
    return call(
        functools.partial(finish_kernel, tiles, factor),
        "finish",
        8 * tiles,
        (part, z, up, down),
        jax.ShapeDtypeStruct((9, SUBS, share), f32),
        [pltpu.VMEM((4, SUBS, share), f32), pltpu.SemaphoreType.DMA((3,))],
        None,
        pl.BlockSpec(memory_space=pltpu.HBM),
    )


def solution(mesh):
    in_specs = (P("group", "row", None), P("group", "row", None), P("probe", "group", "row", None))
    out_specs = P("group", "row", "probe")
    return jax.shard_map(
        per_device, mesh=mesh, in_specs=in_specs, out_specs=out_specs, check_vma=False
    )
```

```python
import functools
import math

import jax
import jax.numpy as jnp
from jax import lax
from jax.experimental import pallas as pl
from jax.experimental.pallas import tpu as pltpu
from jax.sharding import PartitionSpec as P

CHEB = 6
LANES = 128
SUBS = 8

lower_edge = 0.25
upper_edge = 12.0


def cheb_weights(degree, low_end, high_end):
    count = degree + 1
    values = []
    for order in range(count):
        accum = 0.0
        for node in range(count):
            angle = math.pi * (node + 0.5) / count
            point = 0.5 * (high_end - low_end) * math.cos(angle) + 0.5 * (high_end + low_end)
            accum += math.cos(order * angle) / point
        accum = accum * 2.0 / count
        if order == 0:
            accum = accum * 0.5
        values.append(accum)
    return values


def vmem_spec():
    return pl.BlockSpec(memory_space=pltpu.VMEM)


def params():
    return pltpu.CompilerParams(vmem_limit_bytes=40 * 1024 * 1024)


def cost(vregs):
    return pl.CostEstimate(flops=vregs * 1024 * 20, bytes_accessed=vregs * 4096 * 4, transcendentals=0)


def masks():
    lane = lax.broadcasted_iota(jnp.int32, (SUBS, LANES), 1)
    return lane == 0, lane == LANES - 1


def window_tiles(load, first, count, total):
    before = jnp.where(first > 0, load(jnp.maximum(first - 1, 0)), 0.0)
    after = jnp.where(first + count < total, load(jnp.minimum(first + count, total - 1)), 0.0)
    return [before] + [load(first + k) for k in range(count)] + [after]


def beside(before, here, after, edges):
    left = pltpu.roll(jnp.where(edges[1], before, here), 1, 1)
    right = pltpu.roll(jnp.where(edges[0], after, here), LANES - 1, 1)
    return left, right


def sub(row):
    return pl.ds(row * SUBS, SUBS)


def upside_down():
    return 1 - lax.axis_index("row") % 2


def place(row, flip):
    return row + flip * (SUBS - 1 - 2 * row)


def placed(row, flip):
    return pl.ds(pl.multiple_of(place(row, flip) * SUBS, SUBS), SUBS)


def tile_columns(tile):
    return pl.ds(pl.multiple_of(tile * LANES, LANES), LANES)


def chunk_of(tiles):
    return max(count for count in range(1, 12) if tiles % count == 0)


def load_kernel(width, probes_ref, observed_ref, coefficients_ref, theirs_ref, own_ref, seen_ref, window_ref, sem):
    core = lax.axis_index("probe")
    move = probes_ref.shape[3] - width
    mine = pl.ds(pl.multiple_of(core * move, LANES), width)
    other = pl.ds(pl.multiple_of((1 - core) * move, LANES), width)
    copies = [
        pltpu.make_async_copy(probes_ref.at[:, :, :, other], theirs_ref, sem.at[0]),
        pltpu.make_async_copy(probes_ref.at[:, :, :, mine], own_ref, sem.at[1]),
        pltpu.make_async_copy(coefficients_ref.at[:, :, mine], window_ref, sem.at[2]),
        pltpu.make_async_copy(observed_ref.at[:, :, mine], seen_ref, sem.at[3]),
    ]
    for copy in copies:
        copy.start()
    for copy in copies:
        copy.wait()


def prep_kernel(window_ref, expanded_ref):
    tiles = expanded_ref.shape[1]
    chunk = chunk_of(tiles)
    scale = 4.0 / (upper_edge - lower_edge)
    shift = 2.0 * (upper_edge + lower_edge) / (upper_edge - lower_edge)
    tilt = (upside_down().astype(jnp.float32) - 0.5) * scale

    def body(step, carry):
        for k in range(chunk):
            tile = step * chunk + k
            cols = tile_columns(tile)
            kappa, across, along, skew = [
                [window_ref[2 * kind + c, :, cols] for c in range(2)] for kind in range(4)
            ]
            coupling = scale * window_ref[8, :, cols]
            for c in range(2):
                values = (
                    scale * (kappa[c] + 2.0 * (across[c] + along[c])) - shift,
                    -scale * across[c],
                    -scale * along[c],
                    tilt * skew[c],
                    coupling,
                )
                for kind, value in enumerate(values):
                    for probe in range(4):
                        expanded_ref[kind, tile, pl.ds(4 * c + probe, SUBS, stride=SUBS), :] = value
        return carry

    lax.fori_loop(0, tiles // chunk, body, 0)


def layout_kernel(own_ref, other_ref, seen_ref, z_ref, top_ref, bottom_ref, natural):
    tiles = z_ref.shape[0]
    chunk = chunk_of(tiles)
    flip = upside_down()

    def body(step, carry):
        for k in range(chunk):
            tile = step * chunk + k
            cols = tile_columns(tile)
            for c in range(2):
                for probe in range(2):
                    natural[tile, pl.ds(4 * c + probe, SUBS, stride=SUBS), :] = own_ref[probe, c, :, cols]
                    natural[tile, pl.ds(4 * c + 2 + probe, SUBS, stride=SUBS), :] = other_ref[probe, c, :, cols]
        for k in range(chunk):
            tile = step * chunk + k
            for row in range(SUBS):
                value = natural[tile, placed(row, flip), :]
                z_ref[tile, sub(row), :] = value
                if row == 0:
                    top_ref[tile] = value
                if row == SUBS - 1:
                    bottom_ref[tile] = value
        return carry

    lax.fori_loop(0, tiles // chunk, body, 0)
    for c in range(2):
        for tile in range(tiles):
            index = c * tiles + tile
            cols = pl.ds(tile * LANES, LANES)
            at = (tiles + index // SUBS, pl.ds(index % SUBS, 1))
            first, last = seen_ref[c, 0:1, cols], seen_ref[c, SUBS - 1 : SUBS, cols]
            top_ref[at[0], at[1], :] = jnp.where(flip == 1, last, first)
            bottom_ref[at[0], at[1], :] = jnp.where(flip == 1, first, last)


def step_kernel(upper, constants, offset, other_row, tiles, *refs):
    weight, scale, subtract = constants
    own_ref, other_ref, halo_ref, z_ref, coefficients_ref = refs[:5]
    rest = refs[5:]
    before_ref = None
    if subtract:
        before_ref, rest = rest[0], rest[1:]
    out_ref, edge_ref = rest
    first_row = 0 if upper else 4
    chunk = chunk_of(tiles)

    flip = upside_down()

    def load(row):
        if row == (-1 if upper else 4):
            return lambda tile: halo_ref[tile]
        if row == (4 if upper else -1):
            return lambda tile: other_ref[tile, sub(other_row), :]
        return lambda tile: own_ref[tile, sub(offset + row), :]

    def body(step, carry):
        edges = masks()
        first = step * chunk
        for k in range(chunk):
            tile = first + k
            values, sums, slopes = [], [], []
            for row in range(-1, 5):
                loader = load(row)
                here = loader(tile)
                if k == 0:
                    before = jnp.where(first > 0, loader(jnp.maximum(first - 1, 0)), 0.0)
                else:
                    before = loader(tile - 1)
                if k == chunk - 1:
                    last = first + chunk < tiles
                    after = jnp.where(last, loader(jnp.minimum(first + chunk, tiles - 1)), 0.0)
                else:
                    after = loader(tile + 1)
                left, right = beside(before, here, after, edges)
                values.append(here)
                sums.append(left + right)
                slopes.append(right - left)
            for row in range(4):
                rows = sub(first_row + row)
                at = placed(first_row + row, flip)
                coefs = [coefficients_ref[kind, tile, at, :] for kind in range(5)]
                total = (
                    coefs[0] * values[row + 1]
                    + coefs[1] * sums[row + 1]
                    + coefs[2] * (values[row] + values[row + 2])
                    + coefs[3] * (slopes[row + 2] - slopes[row])
                    + coefs[4] * pltpu.roll(values[row + 1], 4, 0)
                )
                if scale != 1.0:
                    total = scale * total
                total = total + weight * z_ref[tile, rows, :]
                if subtract:
                    total = total - before_ref[tile, sub(row), :]
                out_ref[tile, sub(row), :] = total
                if row == (0 if upper else 3):
                    edge_ref[tile] = total
        return carry

    lax.fori_loop(0, tiles // chunk, body, 0)


def data_kernel(tiles, seen_ref, up_ref, down_ref, out_ref):
    chunk = chunk_of(tiles)

    flip = upside_down()

    def halo(near, far, c, tile):
        index = c * tiles + tile
        at = (tiles + index // SUBS, pl.ds(index % SUBS, 1), slice(None))
        return jnp.broadcast_to(jnp.where(flip == 1, far[at], near[at]), (SUBS, LANES))

    def body(step, carry):
        edges = masks()
        row = lax.broadcasted_iota(jnp.int32, (SUBS, LANES), 0)
        first = step * chunk
        kept = [[], []]
        for c in range(2):
            values = window_tiles(lambda tile: seen_ref[c, :, tile_columns(tile)], first, chunk, tiles)
            ups = window_tiles(lambda tile: halo(up_ref, down_ref, c, tile), first, chunk, tiles)
            downs = window_tiles(lambda tile: halo(down_ref, up_ref, c, tile), first, chunk, tiles)
            aboves = [jnp.where(row == 0, u, pltpu.roll(v, 1, 0)) for u, v in zip(ups, values)]
            belows = [jnp.where(row == SUBS - 1, d, pltpu.roll(v, SUBS - 1, 0)) for d, v in zip(downs, values)]
            tilts = [b - a for a, b in zip(aboves, belows)]
            for k in range(chunk):
                tile = first + k
                value = values[k + 1]
                left, right = beside(values[k], value, values[k + 2], edges)
                low, high = beside(tilts[k], tilts[k + 1], tilts[k + 2], edges)
                half = -0.5 * value
                out_ref[tile, c] = half * value
                out_ref[tile, 2 + c] = half * (2.0 * value - (left + right))
                out_ref[tile, 4 + c] = half * (2.0 * value - (aboves[k + 1] + belows[k + 1]))
                out_ref[tile, 6 + c] = (-0.5 * half) * (high - low)
                kept[c].append(value)
        for k in range(chunk):
            out_ref[first + k, 8] = -(kept[0][k] * kept[1][k])
        return carry

    lax.fori_loop(0, tiles // chunk, body, 0)


def gradient_kernel(tiles, factor, z_ref, top_ref, bottom_ref, data_ref, out_ref, products):
    kept = out_ref.shape[2] // LANES
    offset = lax.axis_index("probe") * (tiles - kept)
    count = products.shape[0]
    flip = upside_down()
    tilt = flip.astype(jnp.float32) - 0.5

    def load(row):
        if row < 4:
            return lambda tile: top_ref[tile, sub(row), :]
        return lambda tile: bottom_ref[tile, sub(row - 4), :]

    def body(step, carry):
        edges = masks()
        for k in range(count):
            index = step * count + k
            tile = index + offset
            values, sums, slopes = [], [], []
            for row in range(SUBS):
                loader = load(row)
                before, here, after = window_tiles(loader, tile, 1, tiles)
                left, right = beside(before, here, after, edges)
                values.append(here)
                sums.append(left + right)
                slopes.append(right - left)
            for row in range(SUBS):
                left = factor * z_ref[tile, sub(row), :]
                value = values[row]
                at = placed(row, flip)
                twice = 2.0 * value
                if row == 0:
                    along, skew = values[1], slopes[1]
                elif row == SUBS - 1:
                    along, skew = values[row - 1], -slopes[row - 1]
                else:
                    along, skew = values[row - 1] + values[row + 1], slopes[row + 1] - slopes[row - 1]
                products[k, 0, at, :] = left * value
                products[k, 1, at, :] = left * (twice - sums[row])
                products[k, 2, at, :] = left * (twice - along)
                products[k, 3, at, :] = (tilt * left) * skew
                products[k, 4, at, :] = left * pltpu.roll(value, 4, 0)
        for k in range(count):
            index = step * count + k
            tile = index + offset
            cols = tile_columns(index)
            for kind in range(5):
                parts = [products[k, kind, pl.ds(s, SUBS, stride=SUBS), :] for s in range(SUBS)]
                sums = [(parts[4 * c] + parts[4 * c + 1]) + (parts[4 * c + 2] + parts[4 * c + 3]) for c in range(2)]
                if kind < 4:
                    for c in range(2):
                        out_ref[2 * kind + c, :, cols] = sums[c] + data_ref[tile, 2 * kind + c]
                else:
                    out_ref[8, :, cols] = (sums[0] + sums[1]) + data_ref[tile, 8]
        return carry

    lax.fori_loop(0, kept // count, body, 0)


def finish_kernel(tiles, factor, part_ref, z_ref, up_ref, down_ref, out_ref, fixed, sem):
    kept = out_ref.shape[2] // LANES
    offset = lax.axis_index("probe") * (tiles - kept)
    count = max(n for n in range(1, 9) if kept % n == 0)
    early = [
        pltpu.make_async_copy(part_ref.at[pl.ds(0, 4)], out_ref.at[pl.ds(0, 4)], sem.at[0]),
        pltpu.make_async_copy(part_ref.at[pl.ds(8, 1)], out_ref.at[pl.ds(8, 1)], sem.at[1]),
    ]
    for copy in early:
        copy.start()
    flip = upside_down()
    tilt = 0.5 - flip.astype(jnp.float32)

    def body(step, carry):
        edges = masks()
        row = place(lax.broadcasted_iota(jnp.int32, (SUBS, LANES), 0), flip)
        for k in range(count):
            index = step * count + k
            tile = index + offset
            cols = tile_columns(index)
            adds = []
            for ref, z_row, sign in ((up_ref, 0, tilt), (down_ref, SUBS - 1, -tilt)):
                before, here, after = window_tiles(lambda at: ref[at], tile, 1, tiles)
                left, right = beside(before, here, after, edges)
                z = factor * z_ref[tile, sub(z_row), :]
                pair = []
                for term in (-z * here, (sign * z) * (right - left)):
                    term = term + pltpu.roll(term, 1, 0)
                    pair.append(term + pltpu.roll(term, 2, 0))
                adds.append(pair)
            for kind in range(2):
                for c in range(2):
                    at = 4 * c + 3
                    channel = 2 * kind + c
                    top = jnp.broadcast_to(adds[0][kind][at : at + 1, :], (SUBS, LANES))
                    bottom = jnp.broadcast_to(adds[1][kind][at : at + 1, :], (SUBS, LANES))
                    more = jnp.where(row == 0, top, jnp.where(row == SUBS - 1, bottom, 0.0))
                    fixed[channel, :, cols] = part_ref[4 + channel, :, cols] + more
        return carry

    lax.fori_loop(0, kept // count, body, 0)
    late = pltpu.make_async_copy(fixed, out_ref.at[pl.ds(4, 4)], sem.at[2])
    late.start()
    late.wait()
    for copy in early:
        copy.wait()


def per_device(observations, coefficients, probes):
    weights = cheb_weights(CHEB, lower_edge, upper_edge)
    f32 = jnp.float32
    columns = probes.shape[3]
    share = columns // lax.axis_size("probe")
    width = share + LANES
    tiles = width // LANES
    kept = share // LANES
    seen_tiles = -(-2 * tiles // SUBS)
    rows = lax.axis_size("row")
    near_pairs = [pair for i in range(0, rows - 1, 2) for pair in ((i, i + 1), (i + 1, i))]
    far_pairs = [pair for i in range(1, rows - 1, 2) for pair in ((i, i + 1), (i + 1, i))]

    def near(edge):
        return lax.ppermute(edge, "row", near_pairs)

    def far(edge):
        return lax.ppermute(edge, "row", far_pairs)

    def call(kernel, name, vregs, operands, outs, scratch=(), in_specs=None, out_specs=None):
        return pl.pallas_call(
            kernel,
            out_shape=outs,
            in_specs=in_specs or [vmem_spec()] * len(operands),
            out_specs=out_specs or jax.tree.map(lambda _: vmem_spec(), outs),
            scratch_shapes=scratch,
            compiler_params=params(),
            cost_estimate=cost(vregs),
            name=name,
        )(*operands)

    theirs, own, seen, window = call(
        functools.partial(load_kernel, width),
        "load",
        100,
        [
            pltpu.with_memory_space_constraint(array, pltpu.HBM)
            for array in (probes, observations, coefficients)
        ],
        [
            pltpu.VMEM((2, 2, SUBS, width), f32),
            pltpu.VMEM((2, 2, SUBS, width), f32),
            pltpu.VMEM((2, SUBS, width), f32),
            pltpu.VMEM((9, SUBS, width), f32),
        ],
        [pltpu.SemaphoreType.DMA((4,))],
        [pl.BlockSpec(memory_space=pltpu.HBM)] * 3,
    )
    other = lax.ppermute(theirs, "probe", [(0, 1), (1, 0)])
    expanded = call(
        prep_kernel, "prep", 5 * 8 * tiles, (window,), pltpu.VMEM((5, tiles, SUBS * SUBS, LANES), f32)
    )
    own, expanded = lax.optimization_barrier((own, expanded))
    message = (tiles + seen_tiles, SUBS, LANES)
    z, top, bottom = call(
        layout_kernel,
        "layout",
        8 * tiles,
        (own, other, seen),
        [pltpu.VMEM((tiles, SUBS * SUBS, LANES), f32), pltpu.VMEM(message, f32), pltpu.VMEM(message, f32)],
        [pltpu.VMEM((tiles, SUBS * SUBS, LANES), f32)],
    )

    def half(upper, constants, own, other_half, halo, before):
        shared = own is z
        offset = (0 if upper else 4) if shared else 0
        other_row = (4 if upper else 3) if shared else (0 if upper else 3)
        operands = [own, other_half, halo, z, expanded]
        if constants[2]:
            operands.append(before)
        return call(
            functools.partial(step_kernel, upper, constants, offset, other_row, tiles),
            "upper" if upper else "lower",
            4 * tiles,
            operands,
            [pltpu.VMEM((tiles, 4 * SUBS, LANES), f32), pltpu.VMEM((tiles, SUBS, LANES), f32)],
        )

    first_up, first_down = near(top), far(bottom)
    up, down = first_up, first_down
    now = (z, z)
    before = (None, None)
    for order in range(CHEB - 1, -1, -1):
        if order == CHEB - 1:
            constants = (weights[order], weights[CHEB], False)
        elif order == CHEB - 2:
            constants = (weights[order] - weights[CHEB], 1.0, False)
        elif order > 0:
            constants = (weights[order], 1.0, True)
        else:
            constants = (weights[0], 0.5, True)
        upper, top = half(True, constants, now[0], now[1], up, before[0])
        next_up = near(top)
        lower, bottom = half(False, constants, now[1], now[0], down, before[1])
        next_down = far(bottom)
        before, now = now, (upper, lower)
        up, down = next_up, next_down

    data = call(
        functools.partial(data_kernel, tiles),
        "data",
        9 * tiles,
        (seen, first_up, first_down),
        pltpu.VMEM((tiles, 9, SUBS, LANES), f32),
    )
    factor = 0.5 / (probes.shape[0] * lax.axis_size("probe"))
    count = max(n for n in range(1, 5) if kept % n == 0)
    part = call(
        functools.partial(gradient_kernel, tiles, factor),
        "gradient",
        24 * tiles,
        (z, now[0], now[1], data),
        pltpu.VMEM((9, SUBS, share), f32),
        [pltpu.VMEM((count, 5, SUBS * SUBS, LANES), f32)],
    )
    return call(
        functools.partial(finish_kernel, tiles, factor),
        "finish",
        8 * tiles,
        (part, z, up, down),
        jax.ShapeDtypeStruct((9, SUBS, share), f32),
        [pltpu.VMEM((4, SUBS, share), f32), pltpu.SemaphoreType.DMA((3,))],
        None,
        pl.BlockSpec(memory_space=pltpu.HBM),
    )


def solution(mesh):
    in_specs = (P("group", "row", None), P("group", "row", None), P("probe", "group", "row", None))
    out_specs = P("group", "row", "probe")
    return jax.shard_map(
        per_device, mesh=mesh, in_specs=in_specs, out_specs=out_specs, check_vma=False
    )
```

```python
import functools
import math

import jax
import jax.numpy as jnp
from jax import lax
from jax.experimental import pallas as pl
from jax.experimental.pallas import tpu as pltpu
from jax.sharding import PartitionSpec as P

CHEB = 6
LANES = 128
SUBS = 8

lower_edge = 0.25
upper_edge = 12.0


def cheb_weights(degree, low_end, high_end):
    count = degree + 1
    values = []
    for order in range(count):
        accum = 0.0
        for node in range(count):
            angle = math.pi * (node + 0.5) / count
            point = 0.5 * (high_end - low_end) * math.cos(angle) + 0.5 * (high_end + low_end)
            accum += math.cos(order * angle) / point
        accum = accum * 2.0 / count
        if order == 0:
            accum = accum * 0.5
        values.append(accum)
    return values


def vmem_spec():
    return pl.BlockSpec(memory_space=pltpu.VMEM)


def params():
    return pltpu.CompilerParams(vmem_limit_bytes=40 * 1024 * 1024)


def cost(vregs):
    return pl.CostEstimate(flops=vregs * 1024 * 20, bytes_accessed=vregs * 4096 * 4, transcendentals=0)


def masks():
    lane = lax.broadcasted_iota(jnp.int32, (SUBS, LANES), 1)
    return lane == 0, lane == LANES - 1


def window_tiles(load, first, count, total):
    before = jnp.where(first > 0, load(jnp.maximum(first - 1, 0)), 0.0)
    after = jnp.where(first + count < total, load(jnp.minimum(first + count, total - 1)), 0.0)
    return [before] + [load(first + k) for k in range(count)] + [after]


def beside(before, here, after, edges):
    left = pltpu.roll(jnp.where(edges[1], before, here), 1, 1)
    right = pltpu.roll(jnp.where(edges[0], after, here), LANES - 1, 1)
    return left, right


def sub(row):
    return pl.ds(row * SUBS, SUBS)


def upside_down():
    return 1 - lax.axis_index("row") % 2


def place(row, flip):
    return row + flip * (SUBS - 1 - 2 * row)


def placed(row, flip):
    at = place(row, flip) * SUBS
    return pl.ds(at if isinstance(at, int) else pl.multiple_of(at, SUBS), SUBS)


def tilt_sign():
    return 1.0 - 2.0 * upside_down().astype(jnp.float32)


def tile_columns(tile):
    return pl.ds(pl.multiple_of(tile * LANES, LANES), LANES)


def chunk_of(tiles):
    return max(count for count in range(1, 12) if tiles % count == 0)


def load_kernel(width, probes_ref, observed_ref, coefficients_ref, theirs_ref, own_ref, seen_ref, window_ref, sem):
    core = lax.axis_index("probe")
    move = probes_ref.shape[3] - width
    mine = pl.ds(pl.multiple_of(core * move, LANES), width)
    other = pl.ds(pl.multiple_of((1 - core) * move, LANES), width)
    copies = [
        pltpu.make_async_copy(probes_ref.at[:, :, :, other], theirs_ref, sem.at[0]),
        pltpu.make_async_copy(probes_ref.at[:, :, :, mine], own_ref, sem.at[1]),
        pltpu.make_async_copy(coefficients_ref.at[:, :, mine], window_ref, sem.at[2]),
        pltpu.make_async_copy(observed_ref.at[:, :, mine], seen_ref, sem.at[3]),
    ]
    for copy in copies:
        copy.start()
    for copy in copies:
        copy.wait()


def combine(kappa, across, along, skew, coupling, sign):
    scale = 4.0 / (upper_edge - lower_edge)
    shift = 2.0 * (upper_edge + lower_edge) / (upper_edge - lower_edge)
    return (
        scale * (kappa + 2.0 * (across + along)) - shift,
        -scale * across,
        -scale * along,
        (-0.5 * scale * sign) * skew,
        scale * coupling,
    )


def prep_kernel(window_ref, seen_ref, expanded_ref, near_ref, far_ref, eight, rest, observed):
    tiles = expanded_ref.shape[1]
    chunk = chunk_of(tiles)
    flip = upside_down()
    sign = tilt_sign()
    rest[...] = jnp.zeros_like(rest)
    observed[...] = jnp.zeros_like(observed)

    def body(step, carry):
        for k in range(chunk):
            tile = step * chunk + k
            cols = tile_columns(tile)
            raw = [window_ref[channel, :, cols] for channel in range(9)]
            for c in range(2):
                values = combine(raw[c], raw[2 + c], raw[4 + c], raw[6 + c], raw[8], sign)
                for kind, value in enumerate(values):
                    for probe in range(4):
                        expanded_ref[kind, tile, pl.ds(4 * c + probe, SUBS, stride=SUBS), :] = value
            for channel in range(8):
                eight[tile, pl.ds(channel, SUBS, stride=SUBS), :] = raw[channel]
        return carry

    lax.fori_loop(0, tiles // chunk, body, 0)
    for tile in range(tiles):
        cols = pl.ds(tile * LANES, LANES)
        rest[tile // 8, pl.ds(tile % 8, SUBS, stride=SUBS), :] = window_ref[8, :, cols]
        for c in range(2):
            observed[tile // 4, pl.ds(2 * (tile % 4) + c, SUBS, stride=SUBS), :] = seen_ref[c, :, cols]
    first, last = placed(0, flip), placed(SUBS - 1, flip)
    for tile in range(tiles):
        far_ref[tile] = eight[tile, last, :]
    for index in range(rest.shape[0]):
        far_ref[tiles + index] = rest[index, last, :]
    for index in range(observed.shape[0]):
        near_ref[index] = observed[index, first, :]
        far_ref[tiles + rest.shape[0] + index] = observed[index, last, :]


def layout_kernel(own_ref, other_ref, more_near_ref, more_far_ref, z_ref, near_ref, far_ref, natural):
    tiles = z_ref.shape[0]
    chunk = chunk_of(tiles)
    flip = upside_down()

    def body(step, carry):
        for k in range(chunk):
            tile = step * chunk + k
            cols = tile_columns(tile)
            for c in range(2):
                for probe in range(2):
                    natural[tile, pl.ds(4 * c + probe, SUBS, stride=SUBS), :] = own_ref[probe, c, :, cols]
                    natural[tile, pl.ds(4 * c + 2 + probe, SUBS, stride=SUBS), :] = other_ref[probe, c, :, cols]
        for k in range(chunk):
            tile = step * chunk + k
            for row in range(SUBS):
                value = natural[tile, placed(row, flip), :]
                z_ref[tile, sub(row), :] = value
                if row == 0:
                    near_ref[tile] = value
                if row >= SUBS - 2:
                    far_ref[2 * tile + row - SUBS + 2] = value
        return carry

    lax.fori_loop(0, tiles // chunk, body, 0)
    for index in range(more_near_ref.shape[0]):
        near_ref[tiles + index] = more_near_ref[index]
    for index in range(more_far_ref.shape[0]):
        far_ref[2 * tiles + index] = more_far_ref[index]


def rim(halo_ref, rim_ref, tiles):
    chunk = chunk_of(tiles)
    sign = tilt_sign()

    def spread(index, row):
        return jnp.broadcast_to(halo_ref[index, pl.ds(row, 1), :], (SUBS, LANES))

    def body(step, carry):
        low = lax.broadcasted_iota(jnp.int32, (SUBS, LANES), 0) < 4
        for k in range(chunk):
            tile = step * chunk + k
            pairs = [
                jnp.where(low, spread(2 * tiles + tile, 2 * kind), spread(2 * tiles + tile, 2 * kind + 1))
                for kind in range(4)
            ]
            coupling = spread(3 * tiles + tile // 8, tile % 8)
            for kind, value in enumerate(combine(*pairs, coupling, sign)):
                rim_ref[kind, tile] = value
        return carry

    lax.fori_loop(0, tiles // chunk, body, 0)


def sweep(tiles, low, count, load, factor, z_row, before, constants, store):
    weight, scale = constants
    chunk = chunk_of(tiles)

    def body(step, carry):
        edges = masks()
        first = step * chunk
        for k in range(chunk):
            tile = first + k
            values, sums, slopes = [], [], []
            for row in range(low - 1, low + count + 1):
                here = load(row, tile)
                if k == 0:
                    last = jnp.where(first > 0, load(row, jnp.maximum(first - 1, 0)), 0.0)
                else:
                    last = load(row, tile - 1)
                if k == chunk - 1:
                    more = first + chunk < tiles
                    after = jnp.where(more, load(row, jnp.minimum(first + chunk, tiles - 1)), 0.0)
                else:
                    after = load(row, tile + 1)
                left, right = beside(last, here, after, edges)
                values.append(here)
                sums.append(left + right)
                slopes.append(right - left)
            for at in range(count):
                row = low + at
                total = (
                    factor(0, row, tile) * values[at + 1]
                    + factor(1, row, tile) * sums[at + 1]
                    + factor(2, row, tile) * (values[at] + values[at + 2])
                    + factor(3, row, tile) * (slopes[at + 2] - slopes[at])
                    + factor(4, row, tile) * pltpu.roll(values[at + 1], 4, 0)
                )
                if scale != 1.0:
                    total = scale * total
                total = total + weight * z_row(row, tile)
                if before is not None:
                    total = total - before(row, tile)
                store(row, tile, total)
        return carry

    lax.fori_loop(0, tiles // chunk, body, 0)


def middle_kernel(steps, tiles, first_round, *refs):
    if first_round:
        z_ref, expanded_ref, once_ref, twice_ref = refs
    else:
        z_ref, expanded_ref, top_ref, second_ref, inner_ref, bottom_ref, older_ref, once_ref, twice_ref = refs
    flip = upside_down()

    def now(row, tile):
        if first_round:
            return z_ref[tile, sub(row), :]
        if row < 2:
            return (top_ref, second_ref)[row][tile]
        if row < 6:
            return inner_ref[tile, sub(row - 2), :]
        return bottom_ref[2 * tile + row - 6]

    def factor(kind, row, tile):
        return expanded_ref[kind, tile, placed(row, flip), :]

    def z_row(row, tile):
        return z_ref[tile, sub(row), :]

    def once(row, tile):
        return once_ref[tile, sub(row - 1), :]

    def store_once(row, tile, value):
        once_ref[tile, sub(row - 1), :] = value

    def store_twice(row, tile, value):
        twice_ref[tile, sub(row - 2), :] = value

    older = None if first_round else (lambda row, tile: older_ref[tile, sub(row - 1), :])
    sweep(tiles, 1, 6, now, factor, z_row, older, steps[0], store_once)
    sweep(tiles, 2, 4, once, factor, z_row, None if first_round else now, steps[1], store_twice)


def near_once_kernel(constants, tiles, first_round, *refs):
    if first_round:
        halo_ref, z_ref, expanded_ref, out_ref = refs
    else:
        halo_ref, z_ref, expanded_ref, top_ref, second_ref, older_ref, out_ref = refs
    flip = upside_down()

    def now(row, tile):
        if row < 0:
            return halo_ref[tile]
        if first_round:
            return z_ref[tile, sub(row), :]
        return (top_ref, second_ref)[row][tile]

    def factor(kind, row, tile):
        return expanded_ref[kind, tile, placed(row, flip), :]

    def store(row, tile, value):
        out_ref[tile] = value

    older = None if first_round else (lambda row, tile: older_ref[tile])
    sweep(tiles, 0, 1, now, factor, lambda row, tile: z_ref[tile, sub(row), :], older, constants, store)


def near_twice_kernel(constants, tiles, first_round, *refs):
    if first_round:
        halo_ref, z_ref, expanded_ref, once_ref, inner_ref, out_ref, second_out_ref = refs
    else:
        halo_ref, z_ref, expanded_ref, once_ref, inner_ref, top_ref, second_ref, out_ref, second_out_ref = refs
    flip = upside_down()

    def once(row, tile):
        if row < 0:
            return halo_ref[tile]
        if row == 0:
            return once_ref[tile]
        return inner_ref[tile, sub(row - 1), :]

    def factor(kind, row, tile):
        return expanded_ref[kind, tile, placed(row, flip), :]

    def store(row, tile, value):
        (out_ref, second_out_ref)[row][tile] = value

    older = None if first_round else (lambda row, tile: (top_ref, second_ref)[row][tile])
    sweep(tiles, 0, 2, once, factor, lambda row, tile: z_ref[tile, sub(row), :], older, constants, store)


def far_kernel(steps, tiles, first_round, last_round, *refs):
    halo_ref, z_halo_ref, z_ref, expanded_ref, inner_ref = refs[:5]
    refs = refs[5:]
    if first_round:
        once_ref, twice_ref, rim_ref = refs[:3]
        rim(halo_ref, rim_ref, tiles)
    else:
        rim_ref, bottom_ref, older_ref, once_ref, twice_ref = refs[:5]
    row_ref = refs[-1]
    flip = upside_down()

    def now(row, tile):
        if row > 7:
            return halo_ref[2 * tile + 9 - row]
        if first_round:
            return z_ref[tile, sub(row), :]
        return bottom_ref[2 * tile + row - 6]

    def factor(kind, row, tile):
        if row > 7:
            return rim_ref[kind, tile]
        return expanded_ref[kind, tile, placed(row, flip), :]

    def z_row(row, tile):
        if row > 7:
            return z_halo_ref[2 * tile + 1]
        return z_ref[tile, sub(row), :]

    def once(row, tile):
        if row <= 6:
            return inner_ref[tile, sub(row - 1), :]
        return once_ref[tile, sub(row - 7), :]

    def store_once(row, tile, value):
        once_ref[tile, sub(row - 7), :] = value

    def store_twice(row, tile, value):
        twice_ref[2 * tile + row - 6] = value
        if last_round and row == 7:
            row_ref[tile] = value

    older = None if first_round else (lambda row, tile: older_ref[tile, sub(row - 7), :])
    sweep(tiles, 7, 2, now, factor, z_row, older, steps[0], store_once)
    sweep(tiles, 6, 2, once, factor, z_row, None if first_round else now, steps[1], store_twice)


def data_kernel(tiles, seen_ref, near_ref, far_ref, out_ref):
    chunk = chunk_of(tiles)

    flip = upside_down()
    far_base = far_ref.shape[0] - (near_ref.shape[0] - tiles)

    def halo(above, c, tile):
        at = pl.ds(2 * (tile % 4) + c, 1)
        near, far = near_ref[tiles + tile // 4, at, :], far_ref[far_base + tile // 4, at, :]
        row = jnp.where(flip == 1, far, near) if above else jnp.where(flip == 1, near, far)
        return jnp.broadcast_to(row, (SUBS, LANES))

    def body(step, carry):
        edges = masks()
        row = lax.broadcasted_iota(jnp.int32, (SUBS, LANES), 0)
        first = step * chunk
        kept = [[], []]
        for c in range(2):
            values = window_tiles(lambda tile: seen_ref[c, :, tile_columns(tile)], first, chunk, tiles)
            ups = window_tiles(lambda tile: halo(True, c, tile), first, chunk, tiles)
            downs = window_tiles(lambda tile: halo(False, c, tile), first, chunk, tiles)
            aboves = [jnp.where(row == 0, u, pltpu.roll(v, 1, 0)) for u, v in zip(ups, values)]
            belows = [jnp.where(row == SUBS - 1, d, pltpu.roll(v, SUBS - 1, 0)) for d, v in zip(downs, values)]
            tilts = [b - a for a, b in zip(aboves, belows)]
            for k in range(chunk):
                tile = first + k
                value = values[k + 1]
                left, right = beside(values[k], value, values[k + 2], edges)
                low, high = beside(tilts[k], tilts[k + 1], tilts[k + 2], edges)
                half = -0.5 * value
                out_ref[tile, c] = half * value
                out_ref[tile, 2 + c] = half * (2.0 * value - (left + right))
                out_ref[tile, 4 + c] = half * (2.0 * value - (aboves[k + 1] + belows[k + 1]))
                out_ref[tile, 6 + c] = (-0.5 * half) * (high - low)
                kept[c].append(value)
        for k in range(chunk):
            out_ref[first + k, 8] = -(kept[0][k] * kept[1][k])
        return carry

    lax.fori_loop(0, tiles // chunk, body, 0)


def gradient_kernel(tiles, factor, z_ref, top_ref, second_ref, inner_ref, bottom_ref, data_ref, out_ref, products):
    kept = out_ref.shape[2] // LANES
    offset = lax.axis_index("probe") * (tiles - kept)
    count = products.shape[0]

    def load(row):
        if row < 2:
            return lambda tile: (top_ref, second_ref)[row][tile]
        if row < 6:
            return lambda tile: inner_ref[tile, sub(row - 2), :]
        return lambda tile: bottom_ref[2 * tile + row - 6]

    def body(flip, step, carry):
        edges = masks()
        for k in range(count):
            index = step * count + k
            tile = index + offset
            values, sums, slopes = [], [], []
            for row in range(SUBS):
                loader = load(row)
                before, here, after = window_tiles(loader, tile, 1, tiles)
                left, right = beside(before, here, after, edges)
                values.append(here)
                sums.append(left + right)
                slopes.append(right - left)
            for row in range(SUBS):
                left = factor * z_ref[tile, sub(row), :]
                value = values[row]
                at = placed(row, flip)
                twice = 2.0 * value
                if row == 0:
                    along, skew = values[1], slopes[1]
                elif row == SUBS - 1:
                    along, skew = values[row - 1], -slopes[row - 1]
                else:
                    along, skew = values[row - 1] + values[row + 1], slopes[row + 1] - slopes[row - 1]
                products[k, 0, at, :] = left * value
                products[k, 1, at, :] = left * (twice - sums[row])
                products[k, 2, at, :] = left * (twice - along)
                products[k, 3, at, :] = ((flip - 0.5) * left) * skew
                products[k, 4, at, :] = left * pltpu.roll(value, 4, 0)
        for k in range(count):
            index = step * count + k
            tile = index + offset
            cols = tile_columns(index)
            for kind in range(5):
                parts = [products[k, kind, pl.ds(s, SUBS, stride=SUBS), :] for s in range(SUBS)]
                sums = [(parts[4 * c] + parts[4 * c + 1]) + (parts[4 * c + 2] + parts[4 * c + 3]) for c in range(2)]
                if kind < 4:
                    for c in range(2):
                        out_ref[2 * kind + c, :, cols] = sums[c] + data_ref[tile, 2 * kind + c]
                else:
                    out_ref[8, :, cols] = (sums[0] + sums[1]) + data_ref[tile, 8]
        return carry

    for flip in range(2):

        @pl.when(upside_down() == flip)
        def _():
            lax.fori_loop(0, kept // count, functools.partial(body, flip), 0)


def finish_kernel(tiles, factor, part_ref, z_ref, up_ref, down_ref, out_ref, fixed, sem):
    kept = out_ref.shape[2] // LANES
    offset = lax.axis_index("probe") * (tiles - kept)
    count = max(n for n in range(1, 9) if kept % n == 0)
    early = [
        pltpu.make_async_copy(part_ref.at[pl.ds(0, 4)], out_ref.at[pl.ds(0, 4)], sem.at[0]),
        pltpu.make_async_copy(part_ref.at[pl.ds(8, 1)], out_ref.at[pl.ds(8, 1)], sem.at[1]),
    ]
    for copy in early:
        copy.start()
    flip = upside_down()
    sign = 0.5 * tilt_sign()

    def body(step, carry):
        edges = masks()
        row = place(lax.broadcasted_iota(jnp.int32, (SUBS, LANES), 0), flip)
        for k in range(count):
            index = step * count + k
            tile = index + offset
            cols = tile_columns(index)
            adds = []
            for ref, z_row, slant in ((up_ref, 0, sign), (down_ref, SUBS - 1, -sign)):
                before, here, after = window_tiles(lambda at: ref[at], tile, 1, tiles)
                left, right = beside(before, here, after, edges)
                z = factor * z_ref[tile, sub(z_row), :]
                pair = []
                for term in (-z * here, (slant * z) * (right - left)):
                    term = term + pltpu.roll(term, 1, 0)
                    pair.append(term + pltpu.roll(term, 2, 0))
                adds.append(pair)
            for kind in range(2):
                for c in range(2):
                    at = 4 * c + 3
                    channel = 2 * kind + c
                    top = jnp.broadcast_to(adds[0][kind][at : at + 1, :], (SUBS, LANES))
                    bottom = jnp.broadcast_to(adds[1][kind][at : at + 1, :], (SUBS, LANES))
                    more = jnp.where(row == 0, top, jnp.where(row == SUBS - 1, bottom, 0.0))
                    fixed[channel, :, cols] = part_ref[4 + channel, :, cols] + more
        return carry

    lax.fori_loop(0, kept // count, body, 0)
    late = pltpu.make_async_copy(fixed, out_ref.at[pl.ds(4, 4)], sem.at[2])
    late.start()
    late.wait()
    for copy in early:
        copy.wait()


def per_device(observations, coefficients, probes):
    weights = cheb_weights(CHEB, lower_edge, upper_edge)
    f32 = jnp.float32
    columns = probes.shape[3]
    share = columns // lax.axis_size("probe")
    width = share + LANES
    tiles = width // LANES
    kept = share // LANES
    rows = lax.axis_size("row")
    near_pairs = [pair for i in range(0, rows - 1, 2) for pair in ((i, i + 1), (i + 1, i))]
    far_pairs = [pair for i in range(1, rows - 1, 2) for pair in ((i, i + 1), (i + 1, i))]

    def near(edge):
        return lax.ppermute(edge, "row", near_pairs)

    def far(edge):
        return lax.ppermute(edge, "row", far_pairs)

    def call(kernel, name, vregs, operands, outs, scratch=(), in_specs=None, out_specs=None):
        return pl.pallas_call(
            kernel,
            out_shape=outs,
            in_specs=in_specs or [vmem_spec()] * len(operands),
            out_specs=out_specs or jax.tree.map(lambda _: vmem_spec(), outs),
            scratch_shapes=scratch,
            compiler_params=params(),
            cost_estimate=cost(vregs),
            name=name,
        )(*operands)

    theirs, own, seen, window = call(
        functools.partial(load_kernel, width),
        "load",
        100,
        [
            pltpu.with_memory_space_constraint(array, pltpu.HBM)
            for array in (probes, observations, coefficients)
        ],
        [
            pltpu.VMEM((2, 2, SUBS, width), f32),
            pltpu.VMEM((2, 2, SUBS, width), f32),
            pltpu.VMEM((2, SUBS, width), f32),
            pltpu.VMEM((9, SUBS, width), f32),
        ],
        [pltpu.SemaphoreType.DMA((4,))],
        [pl.BlockSpec(memory_space=pltpu.HBM)] * 3,
    )
    other = lax.ppermute(theirs, "probe", [(0, 1), (1, 0)])
    eights, fours = -(-tiles // 8), -(-tiles // 4)
    expanded, more_near, more_far = call(
        prep_kernel,
        "prep",
        5 * 8 * tiles,
        (window, seen),
        [
            pltpu.VMEM((5, tiles, SUBS * SUBS, LANES), f32),
            pltpu.VMEM((fours, SUBS, LANES), f32),
            pltpu.VMEM((tiles + eights + fours, SUBS, LANES), f32),
        ],
        [pltpu.VMEM((count, SUBS * SUBS, LANES), f32) for count in (tiles, eights, fours)],
    )
    own, expanded = lax.optimization_barrier((own, expanded))
    z, top, bottom = call(
        layout_kernel,
        "layout",
        8 * tiles,
        (own, other, more_near, more_far),
        [
            pltpu.VMEM((tiles, SUBS * SUBS, LANES), f32),
            pltpu.VMEM((tiles + fours, SUBS, LANES), f32),
            pltpu.VMEM((3 * tiles + eights + fours, SUBS, LANES), f32),
        ],
        [pltpu.VMEM((tiles, SUBS * SUBS, LANES), f32)],
    )

    def rows_of(count):
        return pltpu.VMEM((tiles, count * SUBS, LANES), f32)

    first_up, first_down = near(top), far(bottom)
    up, down = first_up, first_down
    data = call(
        functools.partial(data_kernel, tiles),
        "data",
        9 * tiles,
        (seen, first_up, first_down),
        pltpu.VMEM((tiles, 9, SUBS, LANES), f32),
    )
    rounds = CHEB // 2
    second = inner = once = rim_factors = None
    for index in range(rounds):
        first_round, last_round = index == 0, index == rounds - 1
        high = CHEB - 1 - 2 * index
        if first_round:
            steps = ((weights[high], weights[CHEB]), (weights[high - 1] - weights[CHEB], 1.0))
        else:
            steps = ((weights[high], 1.0), (weights[high - 1], 0.5 if last_round else 1.0))
        if index == 1:
            inner, data = lax.optimization_barrier((inner, data))
        near_once = call(
            functools.partial(near_once_kernel, steps[0], tiles, first_round),
            "near_once",
            tiles,
            [up, z, expanded] + ([] if first_round else [top, second, once[0]]),
            rows_of(1),
        )
        up = near(near_once)
        inner_once, inner_twice = call(
            functools.partial(middle_kernel, steps, tiles, first_round),
            "middle",
            10 * tiles,
            [z, expanded] + ([] if first_round else [top, second, inner, bottom, once[1]]),
            [rows_of(6), rows_of(4)],
        )
        outs = [rows_of(2), pltpu.VMEM((2 * tiles, SUBS, LANES), f32)]
        if first_round:
            outs.append(pltpu.VMEM((5, tiles, SUBS, LANES), f32))
        if last_round:
            outs.append(rows_of(1))
        under = call(
            functools.partial(far_kernel, steps, tiles, first_round, last_round),
            "far",
            4 * tiles,
            [down, first_down, z, expanded, inner_once] + ([] if first_round else [rim_factors, bottom, once[2]]),
            outs,
        )
        over = call(
            functools.partial(near_twice_kernel, steps[1], tiles, first_round),
            "near_twice",
            2 * tiles,
            [up, z, expanded, near_once, inner_once] + ([] if first_round else [top, second]),
            [rows_of(1), rows_of(1)],
        )
        once = (near_once, inner_once, under[0])
        top, second, inner, bottom = over[0], over[1], inner_twice, under[1]
        if first_round:
            rim_factors = under[2]
        up, down = near(top), far(under[-1] if last_round else bottom)

    factor = 0.5 / (probes.shape[0] * lax.axis_size("probe"))
    count = max(n for n in range(1, 5) if kept % n == 0)
    part = call(
        functools.partial(gradient_kernel, tiles, factor),
        "gradient",
        24 * tiles,
        (z, top, second, inner, bottom, data),
        pltpu.VMEM((9, SUBS, share), f32),
        [pltpu.VMEM((count, 5, SUBS * SUBS, LANES), f32)],
    )
    return call(
        functools.partial(finish_kernel, tiles, factor),
        "finish",
        8 * tiles,
        (part, z, up, down),
        jax.ShapeDtypeStruct((9, SUBS, share), f32),
        [pltpu.VMEM((4, SUBS, share), f32), pltpu.SemaphoreType.DMA((3,))],
        None,
        pl.BlockSpec(memory_space=pltpu.HBM),
    )


def solution(mesh):
    in_specs = (P("group", "row", None), P("group", "row", None), P("probe", "group", "row", None))
    out_specs = P("group", "row", "probe")
    return jax.shard_map(
        per_device, mesh=mesh, in_specs=in_specs, out_specs=out_specs, check_vma=False
    )
```

```python
import functools
import math

import jax
import jax.numpy as jnp
from jax import lax
from jax.experimental import pallas as pl
from jax.experimental.pallas import tpu as pltpu
from jax.sharding import PartitionSpec as P

CHEB = 6
LANES = 128
SUBS = 8

lower_edge = 0.25
upper_edge = 12.0


def cheb_weights(degree, low_end, high_end):
    count = degree + 1
    values = []
    for order in range(count):
        accum = 0.0
        for node in range(count):
            angle = math.pi * (node + 0.5) / count
            point = 0.5 * (high_end - low_end) * math.cos(angle) + 0.5 * (high_end + low_end)
            accum += math.cos(order * angle) / point
        accum = accum * 2.0 / count
        if order == 0:
            accum = accum * 0.5
        values.append(accum)
    return values


def vmem_spec():
    return pl.BlockSpec(memory_space=pltpu.VMEM)


def params():
    return pltpu.CompilerParams(vmem_limit_bytes=40 * 1024 * 1024)


def cost(vregs):
    return pl.CostEstimate(flops=vregs * 1024 * 20, bytes_accessed=vregs * 4096 * 4, transcendentals=0)


def masks():
    lane = lax.broadcasted_iota(jnp.int32, (SUBS, LANES), 1)
    return lane == 0, lane == LANES - 1


def window_tiles(load, first, count, total):
    before = jnp.where(first > 0, load(jnp.maximum(first - 1, 0)), 0.0)
    after = jnp.where(first + count < total, load(jnp.minimum(first + count, total - 1)), 0.0)
    return [before] + [load(first + k) for k in range(count)] + [after]


def beside(before, here, after, edges):
    left = pltpu.roll(jnp.where(edges[1], before, here), 1, 1)
    right = pltpu.roll(jnp.where(edges[0], after, here), LANES - 1, 1)
    return left, right


def sub(row):
    return pl.ds(row * SUBS, SUBS)


def tile_columns(tile):
    return pl.ds(pl.multiple_of(tile * LANES, LANES), LANES)


def chunk_of(tiles):
    return max(count for count in range(1, 12) if tiles % count == 0)


def load_kernel(width, probes_ref, observed_ref, coefficients_ref, theirs_ref, own_ref, seen_ref, window_ref, sem):
    core = lax.axis_index("probe")
    move = probes_ref.shape[3] - width
    mine = pl.ds(pl.multiple_of(core * move, LANES), width)
    other = pl.ds(pl.multiple_of((1 - core) * move, LANES), width)
    copies = [
        pltpu.make_async_copy(probes_ref.at[:, :, :, other], theirs_ref, sem.at[0]),
        pltpu.make_async_copy(probes_ref.at[:, :, :, mine], own_ref, sem.at[1]),
        pltpu.make_async_copy(coefficients_ref.at[:, :, mine], window_ref, sem.at[2]),
        pltpu.make_async_copy(observed_ref.at[:, :, mine], seen_ref, sem.at[3]),
    ]
    for copy in copies:
        copy.start()
    for copy in copies:
        copy.wait()


def combine(kappa, across, along, skew, coupling):
    scale = 4.0 / (upper_edge - lower_edge)
    shift = 2.0 * (upper_edge + lower_edge) / (upper_edge - lower_edge)
    return (
        scale * (kappa + 2.0 * (across + along)) - shift,
        -scale * across,
        -scale * along,
        -0.5 * scale * skew,
        scale * coupling,
    )


def prep_kernel(window_ref, seen_ref, expanded_ref, top_ref, bottom_ref, eight, rest, observed):
    tiles = expanded_ref.shape[1]
    chunk = chunk_of(tiles)
    rest[...] = jnp.zeros_like(rest)
    observed[...] = jnp.zeros_like(observed)

    def body(step, carry):
        for k in range(chunk):
            tile = step * chunk + k
            cols = tile_columns(tile)
            raw = [window_ref[channel, :, cols] for channel in range(9)]
            for c in range(2):
                values = combine(raw[c], raw[2 + c], raw[4 + c], raw[6 + c], raw[8])
                for kind, value in enumerate(values):
                    for probe in range(4):
                        expanded_ref[kind, tile, pl.ds(4 * c + probe, SUBS, stride=SUBS), :] = value
            for channel in range(8):
                eight[tile, pl.ds(channel, SUBS, stride=SUBS), :] = raw[channel]
            top_ref[tile] = eight[tile, sub(0), :]
            bottom_ref[tile] = eight[tile, sub(SUBS - 1), :]
        return carry

    lax.fori_loop(0, tiles // chunk, body, 0)
    for tile in range(tiles):
        cols = pl.ds(tile * LANES, LANES)
        rest[tile // 8, pl.ds(tile % 8, SUBS, stride=SUBS), :] = window_ref[8, :, cols]
        for c in range(2):
            observed[tile // 4, pl.ds(2 * (tile % 4) + c, SUBS, stride=SUBS), :] = seen_ref[c, :, cols]
    base = tiles
    for source in (rest, observed):
        for index in range(source.shape[0]):
            top_ref[base + index] = source[index, sub(0), :]
            bottom_ref[base + index] = source[index, sub(SUBS - 1), :]
        base += source.shape[0]


def layout_kernel(own_ref, other_ref, z_ref, top_ref, bottom_ref):
    tiles = z_ref.shape[0]
    chunk = chunk_of(tiles)

    def body(step, carry):
        for k in range(chunk):
            tile = step * chunk + k
            cols = tile_columns(tile)
            for c in range(2):
                for probe in range(2):
                    z_ref[tile, pl.ds(4 * c + probe, SUBS, stride=SUBS), :] = own_ref[probe, c, :, cols]
                    z_ref[tile, pl.ds(4 * c + 2 + probe, SUBS, stride=SUBS), :] = other_ref[probe, c, :, cols]
            top_ref[tile] = z_ref[tile, sub(0), :]
            bottom_ref[tile] = z_ref[tile, sub(SUBS - 1), :]
        return carry

    lax.fori_loop(0, tiles // chunk, body, 0)


def rim(edge_ref, rim_ref, tiles):
    chunk = chunk_of(tiles)

    def spread(index, row):
        return jnp.broadcast_to(edge_ref[index, pl.ds(row, 1), :], (SUBS, LANES))

    def body(step, carry):
        low = lax.broadcasted_iota(jnp.int32, (SUBS, LANES), 0) < 4
        for k in range(chunk):
            tile = step * chunk + k
            pairs = [jnp.where(low, spread(tile, 2 * kind), spread(tile, 2 * kind + 1)) for kind in range(4)]
            coupling = spread(tiles + tile // 8, tile % 8)
            for kind, value in enumerate(combine(*pairs, coupling)):
                rim_ref[kind, tile] = value
        return carry

    lax.fori_loop(0, tiles // chunk, body, 0)


def sweep(tiles, low, count, load, factor, z_row, before, constants, store):
    weight, scale = constants
    chunk = chunk_of(tiles)

    def body(step, carry):
        edges = masks()
        first = step * chunk
        for k in range(chunk):
            tile = first + k
            values, sums, slopes = [], [], []
            for row in range(low - 1, low + count + 1):
                here = load(row, tile)
                if k == 0:
                    last = jnp.where(first > 0, load(row, jnp.maximum(first - 1, 0)), 0.0)
                else:
                    last = load(row, tile - 1)
                if k == chunk - 1:
                    more = first + chunk < tiles
                    after = jnp.where(more, load(row, jnp.minimum(first + chunk, tiles - 1)), 0.0)
                else:
                    after = load(row, tile + 1)
                left, right = beside(last, here, after, edges)
                values.append(here)
                sums.append(left + right)
                slopes.append(right - left)
            for at in range(count):
                row = low + at
                total = (
                    factor(0, row, tile) * values[at + 1]
                    + factor(1, row, tile) * sums[at + 1]
                    + factor(2, row, tile) * (values[at] + values[at + 2])
                    + factor(3, row, tile) * (slopes[at + 2] - slopes[at])
                    + factor(4, row, tile) * pltpu.roll(values[at + 1], 4, 0)
                )
                if scale != 1.0:
                    total = scale * total
                total = total + weight * z_row(row, tile)
                if before is not None:
                    total = total - before(row, tile)
                store(row, tile, total)
        return carry

    lax.fori_loop(0, tiles // chunk, body, 0)


def first_kernel(part, constants, tiles, *refs):
    halo_ref = None
    if part != 1:
        halo_ref, refs = refs[0], refs[1:]
    z_ref, expanded_ref, out_ref = refs
    low, count = ((0, 2), (2, 4), (6, 2))[part]

    def now(row, tile):
        if row < 0 or row > 7:
            return halo_ref[tile]
        return z_ref[tile, sub(row), :]

    def store(row, tile, value):
        if part == 1:
            out_ref[tile, sub(row - low), :] = value
        else:
            out_ref[2 * tile + row - low] = value

    def factor(kind, row, tile):
        return expanded_ref[kind, tile, sub(row), :]

    sweep(tiles, low, count, now, factor, lambda row, tile: z_ref[tile, sub(row), :], None, constants, store)


def inner_rows(top_ref, inner_ref, bottom_ref):
    def now(row, tile):
        if row < 2:
            return top_ref[2 * tile + row]
        if row < 6:
            return inner_ref[tile, sub(row - 2), :]
        return bottom_ref[2 * tile + row - 6]

    return now


def middle_kernel(steps, tiles, *refs):
    z_ref, expanded_ref, top_ref, inner_ref, bottom_ref = refs[:5]
    once_ref, twice_ref = refs[-2:]
    now = inner_rows(top_ref, inner_ref, bottom_ref)

    def factor(kind, row, tile):
        return expanded_ref[kind, tile, sub(row), :]

    def z_row(row, tile):
        return z_ref[tile, sub(row), :]

    def once(row, tile):
        return once_ref[tile, sub(row - 1), :]

    def store_once(row, tile, value):
        once_ref[tile, sub(row - 1), :] = value

    def store_twice(row, tile, value):
        twice_ref[tile, sub(row - 2), :] = value

    older = None
    if len(refs) > 7:
        older = lambda row, tile: refs[5][tile, sub(row - 1), :]
    sweep(tiles, 1, 6, now, factor, z_row, older, steps[0], store_once)
    sweep(tiles, 2, 4, once, factor, z_row, now, steps[1], store_twice)


def edge_product(upper, constants, tiles, halo_ref, z_halo_ref, z_ref, expanded_ref, rim_ref, edge_ref, older_ref, once_ref):
    base = 0 if upper else 6
    low = -1 if upper else 7

    def now(row, tile):
        if row < 0 or row > 7:
            return halo_ref[2 * tile + (row + 2 if upper else row - 8)]
        return edge_ref[2 * tile + row - base]

    def factor(kind, row, tile):
        if row < 0 or row > 7:
            return rim_ref[kind, tile]
        return expanded_ref[kind, tile, sub(row), :]

    def z_row(row, tile):
        if row < 0 or row > 7:
            return z_halo_ref[tile]
        return z_ref[tile, sub(row), :]

    def store(row, tile, value):
        once_ref[tile, sub(row - low), :] = value

    older = None if older_ref is None else (lambda row, tile: older_ref[tile, sub(row - low), :])
    sweep(tiles, low, 2, now, factor, z_row, older, constants, store)
    return now, factor, z_row


def edge_kernel(upper, steps, tiles, *refs):
    halo_ref, z_halo_ref, z_ref, expanded_ref, rim_ref, edge_ref, inner_ref = refs[:7]
    once_ref, twice_ref = refs[-2:]
    older_ref = refs[7] if len(refs) > 9 else None
    now, factor, z_row = edge_product(
        upper, steps[0], tiles, halo_ref, z_halo_ref, z_ref, expanded_ref, rim_ref, edge_ref, older_ref, once_ref
    )
    base = 0 if upper else 6
    low = -1 if upper else 7

    def once(row, tile):
        if 1 <= row <= 6:
            return inner_ref[tile, sub(row - 1), :]
        return once_ref[tile, sub(row - low), :]

    def store_twice(row, tile, value):
        twice_ref[2 * tile + row - base] = value

    sweep(tiles, base, 2, once, factor, z_row, now, steps[1], store_twice)


def gradient_rows(low, count, tile, slot, load, z_ref, factor, tiles, products):
    edges = masks()
    values, sums, slopes = [], [], []
    for row in range(low - 1, low + count + 1):
        before, here, after = window_tiles(lambda at: load(row, at), tile, 1, tiles)
        left, right = beside(before, here, after, edges)
        values.append(here)
        sums.append(left + right)
        slopes.append(right - left)
    for at in range(count):
        row = low + at
        left = factor * z_ref[tile, sub(row), :]
        value = values[at + 1]
        twice = 2.0 * value
        products[slot, 0, sub(row), :] = left * value
        products[slot, 1, sub(row), :] = left * (twice - sums[at + 1])
        products[slot, 2, sub(row), :] = left * (twice - (values[at] + values[at + 2]))
        products[slot, 3, sub(row), :] = (-0.5 * left) * (slopes[at + 2] - slopes[at])
        products[slot, 4, sub(row), :] = left * pltpu.roll(value, 4, 0)


def gradient_sums(slot, products, start, store):
    for kind in range(5):
        parts = [products[slot, kind, pl.ds(s, SUBS, stride=SUBS), :] for s in range(SUBS)]
        sums = [(parts[4 * c] + parts[4 * c + 1]) + (parts[4 * c + 2] + parts[4 * c + 3]) for c in range(2)]
        if kind < 4:
            for c in range(2):
                store(2 * kind + c, sums[c] + start(2 * kind + c))
        else:
            store(8, (sums[0] + sums[1]) + start(8))


def gradient_kernel(constants, tiles, factor, *refs):
    z_ref, expanded_ref, top_ref, inner_ref, bottom_ref, older_ref, data_ref, series_ref, out_ref, products = refs
    now = inner_rows(top_ref, inner_ref, bottom_ref)

    def coefficient(kind, row, tile):
        return expanded_ref[kind, tile, sub(row), :]

    def store(row, tile, value):
        series_ref[tile, sub(row - 1), :] = value

    def series(row, tile):
        return series_ref[tile, sub(row - 1), :]

    sweep(
        tiles,
        1,
        6,
        now,
        coefficient,
        lambda row, tile: z_ref[tile, sub(row), :],
        lambda row, tile: older_ref[tile, sub(row - 1), :],
        constants,
        store,
    )
    kept = out_ref.shape[2] // LANES
    offset = lax.axis_index("probe") * (tiles - kept)
    count = products.shape[0]
    products[...] = jnp.zeros_like(products)

    def body(step, carry):
        for k in range(count):
            gradient_rows(2, 4, step * count + k + offset, k, series, z_ref, factor, tiles, products)
        for k in range(count):
            index = step * count + k
            cols = tile_columns(index)

            def put(channel, value):
                out_ref[channel, :, cols] = value

            gradient_sums(k, products, lambda channel: data_ref[index + offset, channel], put)
        return carry

    lax.fori_loop(0, kept // count, body, 0)


def end_kernel(upper, constants, tiles, factor, *refs):
    halo_ref, z_halo_ref, z_ref, expanded_ref, rim_ref, edge_ref, inner_ref, older_ref, part_ref = refs[:9]
    if upper:
        out_ref, once_ref, products = refs[9:]
        target = out_ref
    else:
        out_ref, once_ref, products, target, sem = refs[9:]
    edge_product(
        upper, constants, tiles, halo_ref, z_halo_ref, z_ref, expanded_ref, rim_ref, edge_ref, older_ref, once_ref
    )
    low = -1 if upper else 7

    def series(row, tile):
        if 1 <= row <= 6:
            return inner_ref[tile, sub(row - 1), :]
        return once_ref[tile, sub(row - low), :]

    kept = target.shape[2] // LANES
    offset = lax.axis_index("probe") * (tiles - kept)
    count = products.shape[0]
    products[...] = jnp.zeros_like(products)

    def body(step, carry):
        for k in range(count):
            tile = step * count + k + offset
            gradient_rows(0 if upper else 6, 2, tile, k, series, z_ref, factor, tiles, products)
        for k in range(count):
            cols = tile_columns(step * count + k)

            def put(channel, value):
                target[channel, :, cols] = value

            gradient_sums(k, products, lambda channel: part_ref[channel, :, cols], put)
        return carry

    steps = kept // count
    if upper:
        lax.fori_loop(0, steps, body, 0)
        return
    groups = sem.shape[0]
    copies = []
    for group in range(groups):
        lax.fori_loop(group * steps // groups, (group + 1) * steps // groups, body, 0)
        cols = pl.ds(group * kept // groups * LANES, kept // groups * LANES)
        copies.append(pltpu.make_async_copy(target.at[:, :, cols], out_ref.at[:, :, cols], sem.at[group]))
        copies[-1].start()
    for copy in copies:
        copy.wait()


def border_kernel(tiles, seen_ref, up_ref, down_ref, out_ref, rim_up_ref, rim_down_ref):
    rim(up_ref, rim_up_ref, tiles)
    rim(down_ref, rim_down_ref, tiles)
    chunk = chunk_of(tiles)

    base = tiles + -(-tiles // 8)

    def halo(ref, c, tile):
        row = ref[base + tile // 4, pl.ds(2 * (tile % 4) + c, 1), :]
        return jnp.broadcast_to(row, (SUBS, LANES))

    def body(step, carry):
        edges = masks()
        row = lax.broadcasted_iota(jnp.int32, (SUBS, LANES), 0)
        first = step * chunk
        kept = [[], []]
        for c in range(2):
            values = window_tiles(lambda tile: seen_ref[c, :, tile_columns(tile)], first, chunk, tiles)
            ups = window_tiles(lambda tile: halo(up_ref, c, tile), first, chunk, tiles)
            downs = window_tiles(lambda tile: halo(down_ref, c, tile), first, chunk, tiles)
            aboves = [jnp.where(row == 0, u, pltpu.roll(v, 1, 0)) for u, v in zip(ups, values)]
            belows = [jnp.where(row == SUBS - 1, d, pltpu.roll(v, SUBS - 1, 0)) for d, v in zip(downs, values)]
            tilts = [b - a for a, b in zip(aboves, belows)]
            for k in range(chunk):
                tile = first + k
                value = values[k + 1]
                left, right = beside(values[k], value, values[k + 2], edges)
                low, high = beside(tilts[k], tilts[k + 1], tilts[k + 2], edges)
                half = -0.5 * value
                out_ref[tile, c] = half * value
                out_ref[tile, 2 + c] = half * (2.0 * value - (left + right))
                out_ref[tile, 4 + c] = half * (2.0 * value - (aboves[k + 1] + belows[k + 1]))
                out_ref[tile, 6 + c] = (-0.5 * half) * (high - low)
                kept[c].append(value)
        for k in range(chunk):
            out_ref[first + k, 8] = -(kept[0][k] * kept[1][k])
        return carry

    lax.fori_loop(0, tiles // chunk, body, 0)


def per_device(observations, coefficients, probes):
    weights = cheb_weights(CHEB, lower_edge, upper_edge)
    f32 = jnp.float32
    columns = probes.shape[3]
    share = columns // lax.axis_size("probe")
    width = share + LANES
    tiles = width // LANES
    kept = share // LANES
    rows = lax.axis_size("row")
    down_pairs = [(i, i + 1) for i in range(rows - 1)]
    up_pairs = [(i + 1, i) for i in range(rows - 1)]

    def to_next(edge):
        return lax.ppermute(edge, "row", down_pairs)

    def to_previous(edge):
        return lax.ppermute(edge, "row", up_pairs)

    def call(kernel, name, vregs, operands, outs, scratch=(), in_specs=None, out_specs=None):
        return pl.pallas_call(
            kernel,
            out_shape=outs,
            in_specs=in_specs or [vmem_spec()] * len(operands),
            out_specs=out_specs or jax.tree.map(lambda _: vmem_spec(), outs),
            scratch_shapes=scratch,
            compiler_params=params(),
            cost_estimate=cost(vregs),
            name=name,
        )(*operands)

    theirs, own, seen, window = call(
        functools.partial(load_kernel, width),
        "load",
        100,
        [
            pltpu.with_memory_space_constraint(array, pltpu.HBM)
            for array in (probes, observations, coefficients)
        ],
        [
            pltpu.VMEM((2, 2, SUBS, width), f32),
            pltpu.VMEM((2, 2, SUBS, width), f32),
            pltpu.VMEM((2, SUBS, width), f32),
            pltpu.VMEM((9, SUBS, width), f32),
        ],
        [pltpu.SemaphoreType.DMA((4,))],
        [pl.BlockSpec(memory_space=pltpu.HBM)] * 3,
    )
    other = lax.ppermute(theirs, "probe", [(0, 1), (1, 0)])
    eights, fours = -(-tiles // 8), -(-tiles // 4)
    edge_shape = pltpu.VMEM((tiles + eights + fours, SUBS, LANES), f32)
    expanded, edge_top, edge_bottom = call(
        prep_kernel,
        "prep",
        5 * 8 * tiles,
        (window, seen),
        [pltpu.VMEM((5, tiles, SUBS * SUBS, LANES), f32), edge_shape, edge_shape],
        [pltpu.VMEM((count, SUBS * SUBS, LANES), f32) for count in (tiles, eights, fours)],
    )
    edges_down, edges_up = to_previous(edge_top), to_next(edge_bottom)
    own, expanded = lax.optimization_barrier((own, expanded))
    def rows_of(count):
        return pltpu.VMEM((tiles, count * SUBS, LANES), f32)

    z, top, bottom = call(
        layout_kernel,
        "layout",
        8 * tiles,
        (own, other),
        [rows_of(SUBS), rows_of(1), rows_of(1)],
    )
    z_down, z_up = to_previous(top), to_next(bottom)
    edge_rows = pltpu.VMEM((2 * tiles, SUBS, LANES), f32)
    constants = (weights[CHEB - 1], weights[CHEB])

    def first(part, halos, out):
        return call(
            functools.partial(first_kernel, part, constants, tiles),
            "first",
            (2 + part % 2 * 2) * tiles,
            [*halos, z, expanded],
            out,
        )

    rim_shape = pltpu.VMEM((5, tiles, SUBS, LANES), f32)
    data, rim_up, rim_down = call(
        functools.partial(border_kernel, tiles),
        "border",
        9 * tiles,
        (seen, edges_up, edges_down),
        [pltpu.VMEM((tiles, 9, SUBS, LANES), f32), rim_shape, rim_shape],
    )
    expanded, data = lax.optimization_barrier((expanded, data))
    inner = first(1, [], rows_of(4))
    bottom = first(2, [z_down], edge_rows)
    up = to_next(bottom)
    top = first(0, [z_up], edge_rows)
    down = to_previous(top)
    once = None
    for order in range(CHEB - 2, 0, -2):
        opening = weights[order] - (weights[CHEB] if order == CHEB - 2 else 0.0)
        steps = ((opening, 1.0), (weights[order - 1], 1.0))
        inner_once, inner_twice = call(
            functools.partial(middle_kernel, steps, tiles),
            "middle",
            10 * tiles,
            [z, expanded, top, inner, bottom] + ([once[1]] if once else []),
            [rows_of(6), rows_of(4)],
        )

        def edge(upper):
            operands = [up if upper else down, z_up if upper else z_down, z, expanded, rim_up if upper else rim_down]
            operands += [top if upper else bottom, inner_once]
            return call(
                functools.partial(edge_kernel, upper, steps, tiles),
                "upper" if upper else "lower",
                4 * tiles,
                operands + ([once[0 if upper else 2]] if once else []),
                [rows_of(2), edge_rows],
            )

        over, under = edge(True), edge(False)
        once = (over[0], inner_once, under[0])
        top, inner, bottom = over[1], inner_twice, under[1]
        down, up = to_previous(top), to_next(bottom)

    factor = 0.5 / (probes.shape[0] * lax.axis_size("probe"))
    count = max(n for n in range(1, 5) if kept % n == 0)
    constants = (weights[0], 0.5)
    products = pltpu.VMEM((count, 5, SUBS * SUBS, LANES), f32)
    whole = (9, SUBS, share)
    series, part = call(
        functools.partial(gradient_kernel, constants, tiles, factor),
        "gradient",
        24 * tiles,
        (z, expanded, top, inner, bottom, once[1], data),
        [rows_of(6), pltpu.VMEM(whole, f32)],
        [products],
    )
    part = call(
        functools.partial(end_kernel, True, constants, tiles, factor),
        "upper_end",
        8 * tiles,
        (up, z_up, z, expanded, rim_up, top, series, once[0], part),
        pltpu.VMEM(whole, f32),
        [rows_of(2), products],
    )
    groups = max(n for n in range(1, 5) if kept // count % n == 0)
    return call(
        functools.partial(end_kernel, False, constants, tiles, factor),
        "lower_end",
        8 * tiles,
        (down, z_down, z, expanded, rim_down, bottom, series, once[2], part),
        jax.ShapeDtypeStruct(whole, f32),
        [rows_of(2), products, pltpu.VMEM(whole, f32), pltpu.SemaphoreType.DMA((groups,))],
        None,
        pl.BlockSpec(memory_space=pltpu.HBM),
    )


def solution(mesh):
    in_specs = (P("group", "row", None), P("group", "row", None), P("probe", "group", "row", None))
    out_specs = P("group", "row", "probe")
    return jax.shard_map(
        per_device, mesh=mesh, in_specs=in_specs, out_specs=out_specs, check_vma=False
    )
```

```python
import functools
import math

import jax
import jax.numpy as jnp
from jax import lax
from jax.experimental import pallas as pl
from jax.experimental.pallas import tpu as pltpu
from jax.sharding import PartitionSpec as P

CHEB = 6
LANES = 128
SUBS = 8

lower_edge = 0.25
upper_edge = 12.0


def cheb_weights(degree, low_end, high_end):
    count = degree + 1
    values = []
    for order in range(count):
        accum = 0.0
        for node in range(count):
            angle = math.pi * (node + 0.5) / count
            point = 0.5 * (high_end - low_end) * math.cos(angle) + 0.5 * (high_end + low_end)
            accum += math.cos(order * angle) / point
        accum = accum * 2.0 / count
        if order == 0:
            accum = accum * 0.5
        values.append(accum)
    return values


def vmem_spec():
    return pl.BlockSpec(memory_space=pltpu.VMEM)


def params():
    return pltpu.CompilerParams(vmem_limit_bytes=40 * 1024 * 1024)


def cost(vregs):
    return pl.CostEstimate(flops=vregs * 1024 * 20, bytes_accessed=vregs * 4096 * 4, transcendentals=0)


def masks():
    lane = lax.broadcasted_iota(jnp.int32, (SUBS, LANES), 1)
    return lane == 0, lane == LANES - 1


def window_tiles(load, first, count, total):
    before = jnp.where(first > 0, load(jnp.maximum(first - 1, 0)), 0.0)
    after = jnp.where(first + count < total, load(jnp.minimum(first + count, total - 1)), 0.0)
    return [before] + [load(first + k) for k in range(count)] + [after]


def beside(before, here, after, edges):
    left = pltpu.roll(jnp.where(edges[1], before, here), 1, 1)
    right = pltpu.roll(jnp.where(edges[0], after, here), LANES - 1, 1)
    return left, right


def sub(row):
    return pl.ds(row * SUBS, SUBS)


def tile_columns(tile):
    return pl.ds(pl.multiple_of(tile * LANES, LANES), LANES)


def chunk_of(tiles):
    return max(count for count in range(1, 12) if tiles % count == 0)


def load_kernel(width, probes_ref, observed_ref, coefficients_ref, *refs):
    theirs_ref, own_ref, seen_ref, window_ref, top_ref, bottom_ref, eight, rest, observed, sem = refs
    core = lax.axis_index("probe")
    move = probes_ref.shape[3] - width
    mine = pl.ds(pl.multiple_of(core * move, LANES), width)
    other = pl.ds(pl.multiple_of((1 - core) * move, LANES), width)
    copies = [
        pltpu.make_async_copy(coefficients_ref.at[:, :, mine], window_ref, sem.at[0]),
        pltpu.make_async_copy(observed_ref.at[:, :, mine], seen_ref, sem.at[1]),
        pltpu.make_async_copy(probes_ref.at[:, :, :, other], theirs_ref, sem.at[2]),
        pltpu.make_async_copy(probes_ref.at[:, :, :, mine], own_ref, sem.at[3]),
    ]
    for copy in copies:
        copy.start()
    rest[...] = jnp.zeros_like(rest)
    observed[...] = jnp.zeros_like(observed)
    copies[0].wait()
    copies[1].wait()
    tiles = width // LANES
    for tile in range(tiles):
        cols = pl.ds(tile * LANES, LANES)
        for channel in range(8):
            eight[tile, pl.ds(channel, SUBS, stride=SUBS), :] = window_ref[channel, :, cols]
        rest[tile // 8, pl.ds(tile % 8, SUBS, stride=SUBS), :] = window_ref[8, :, cols]
        for c in range(2):
            observed[tile // 4, pl.ds(2 * (tile % 4) + c, SUBS, stride=SUBS), :] = seen_ref[c, :, cols]
    base = 0
    for source in (eight, rest, observed):
        for index in range(source.shape[0]):
            top_ref[base + index] = source[index, sub(0), :]
            bottom_ref[base + index] = source[index, sub(SUBS - 1), :]
        base += source.shape[0]
    copies[2].wait()
    copies[3].wait()


def combine(kappa, across, along, skew, coupling):
    scale = 4.0 / (upper_edge - lower_edge)
    shift = 2.0 * (upper_edge + lower_edge) / (upper_edge - lower_edge)
    return (
        scale * (kappa + 2.0 * (across + along)) - shift,
        -scale * across,
        -scale * along,
        -0.5 * scale * skew,
        scale * coupling,
    )


def prep_kernel(window_ref, expanded_ref):
    tiles = expanded_ref.shape[1]
    chunk = chunk_of(tiles)

    def body(step, carry):
        for k in range(chunk):
            tile = step * chunk + k
            cols = tile_columns(tile)
            raw = [window_ref[channel, :, cols] for channel in range(9)]
            for c in range(2):
                values = combine(raw[c], raw[2 + c], raw[4 + c], raw[6 + c], raw[8])
                for kind, value in enumerate(values):
                    for probe in range(4):
                        expanded_ref[kind, tile, pl.ds(4 * c + probe, SUBS, stride=SUBS), :] = value
        return carry

    lax.fori_loop(0, tiles // chunk, body, 0)


def layout_kernel(own_ref, other_ref, z_ref, top_ref, bottom_ref):
    tiles = z_ref.shape[0]
    chunk = chunk_of(tiles)

    def body(step, carry):
        for k in range(chunk):
            tile = step * chunk + k
            cols = tile_columns(tile)
            for c in range(2):
                for probe in range(2):
                    z_ref[tile, pl.ds(4 * c + probe, SUBS, stride=SUBS), :] = own_ref[probe, c, :, cols]
                    z_ref[tile, pl.ds(4 * c + 2 + probe, SUBS, stride=SUBS), :] = other_ref[probe, c, :, cols]
            top_ref[tile] = z_ref[tile, sub(0), :]
            bottom_ref[tile] = z_ref[tile, sub(SUBS - 1), :]
        return carry

    lax.fori_loop(0, tiles // chunk, body, 0)


def rim(edge_ref, rim_ref, tiles):
    chunk = chunk_of(tiles)

    def spread(index, row):
        return jnp.broadcast_to(edge_ref[index, pl.ds(row, 1), :], (SUBS, LANES))

    def body(step, carry):
        low = lax.broadcasted_iota(jnp.int32, (SUBS, LANES), 0) < 4
        for k in range(chunk):
            tile = step * chunk + k
            pairs = [jnp.where(low, spread(tile, 2 * kind), spread(tile, 2 * kind + 1)) for kind in range(4)]
            coupling = spread(tiles + tile // 8, tile % 8)
            for kind, value in enumerate(combine(*pairs, coupling)):
                rim_ref[kind, tile] = value
        return carry

    lax.fori_loop(0, tiles // chunk, body, 0)


def sweep(tiles, low, count, load, factor, z_row, before, constants, store):
    weight, scale = constants
    chunk = chunk_of(tiles)

    def body(step, carry):
        edges = masks()
        first = step * chunk
        for k in range(chunk):
            tile = first + k
            values, sums, slopes = [], [], []
            for row in range(low - 1, low + count + 1):
                here = load(row, tile)
                if k == 0:
                    last = jnp.where(first > 0, load(row, jnp.maximum(first - 1, 0)), 0.0)
                else:
                    last = load(row, tile - 1)
                if k == chunk - 1:
                    more = first + chunk < tiles
                    after = jnp.where(more, load(row, jnp.minimum(first + chunk, tiles - 1)), 0.0)
                else:
                    after = load(row, tile + 1)
                left, right = beside(last, here, after, edges)
                values.append(here)
                sums.append(left + right)
                slopes.append(right - left)
            for at in range(count):
                row = low + at
                total = (
                    factor(0, row, tile) * values[at + 1]
                    + factor(1, row, tile) * sums[at + 1]
                    + factor(2, row, tile) * (values[at] + values[at + 2])
                    + factor(3, row, tile) * (slopes[at + 2] - slopes[at])
                    + factor(4, row, tile) * pltpu.roll(values[at + 1], 4, 0)
                )
                if scale != 1.0:
                    total = scale * total
                total = total + weight * z_row(row, tile)
                if before is not None:
                    total = total - before(row, tile)
                store(row, tile, total)
        return carry

    lax.fori_loop(0, tiles // chunk, body, 0)


def first_kernel(part, constants, tiles, *refs):
    halo_ref = None
    if part != 1:
        halo_ref, refs = refs[0], refs[1:]
    z_ref, expanded_ref, out_ref = refs
    low, count = ((0, 2), (2, 4), (6, 2))[part]

    def now(row, tile):
        if row < 0 or row > 7:
            return halo_ref[tile]
        return z_ref[tile, sub(row), :]

    def store(row, tile, value):
        if part == 1:
            out_ref[tile, sub(row - low), :] = value
        else:
            out_ref[2 * tile + row - low] = value

    def factor(kind, row, tile):
        return expanded_ref[kind, tile, sub(row), :]

    sweep(tiles, low, count, now, factor, lambda row, tile: z_ref[tile, sub(row), :], None, constants, store)


def inner_rows(top_ref, inner_ref, bottom_ref):
    def now(row, tile):
        if row < 2:
            return top_ref[2 * tile + row]
        if row < 6:
            return inner_ref[tile, sub(row - 2), :]
        return bottom_ref[2 * tile + row - 6]

    return now


def middle_kernel(steps, tiles, *refs):
    z_ref, expanded_ref, top_ref, inner_ref, bottom_ref = refs[:5]
    once_ref, twice_ref = refs[-2:]
    now = inner_rows(top_ref, inner_ref, bottom_ref)

    def factor(kind, row, tile):
        return expanded_ref[kind, tile, sub(row), :]

    def z_row(row, tile):
        return z_ref[tile, sub(row), :]

    def once(row, tile):
        return once_ref[tile, sub(row - 1), :]

    def store_once(row, tile, value):
        once_ref[tile, sub(row - 1), :] = value

    def store_twice(row, tile, value):
        twice_ref[tile, sub(row - 2), :] = value

    older = None
    if len(refs) > 7:
        older = lambda row, tile: refs[5][tile, sub(row - 1), :]
    sweep(tiles, 1, 6, now, factor, z_row, older, steps[0], store_once)
    sweep(tiles, 2, 4, once, factor, z_row, now, steps[1], store_twice)


def edge_product(upper, constants, tiles, halo_ref, z_halo_ref, z_ref, expanded_ref, rim_ref, edge_ref, older_ref, once_ref):
    base = 0 if upper else 6
    low = -1 if upper else 7

    def now(row, tile):
        if row < 0 or row > 7:
            return halo_ref[2 * tile + (row + 2 if upper else row - 8)]
        return edge_ref[2 * tile + row - base]

    def factor(kind, row, tile):
        if row < 0 or row > 7:
            return rim_ref[kind, tile]
        return expanded_ref[kind, tile, sub(row), :]

    def z_row(row, tile):
        if row < 0 or row > 7:
            return z_halo_ref[tile]
        return z_ref[tile, sub(row), :]

    def store(row, tile, value):
        once_ref[tile, sub(row - low), :] = value

    older = None if older_ref is None else (lambda row, tile: older_ref[tile, sub(row - low), :])
    sweep(tiles, low, 2, now, factor, z_row, older, constants, store)
    return now, factor, z_row


def edge_kernel(upper, steps, tiles, *refs):
    halo_ref, z_halo_ref, z_ref, expanded_ref, rim_ref, edge_ref, inner_ref = refs[:7]
    once_ref, twice_ref = refs[-2:]
    older_ref = refs[7] if len(refs) > 9 else None
    now, factor, z_row = edge_product(
        upper, steps[0], tiles, halo_ref, z_halo_ref, z_ref, expanded_ref, rim_ref, edge_ref, older_ref, once_ref
    )
    base = 0 if upper else 6
    low = -1 if upper else 7

    def once(row, tile):
        if 1 <= row <= 6:
            return inner_ref[tile, sub(row - 1), :]
        return once_ref[tile, sub(row - low), :]

    def store_twice(row, tile, value):
        twice_ref[2 * tile + row - base] = value

    sweep(tiles, base, 2, once, factor, z_row, now, steps[1], store_twice)


def gradient_rows(low, count, tile, slot, load, z_ref, factor, tiles, products):
    edges = masks()
    values, sums, slopes = [], [], []
    for row in range(low - 1, low + count + 1):
        before, here, after = window_tiles(lambda at: load(row, at), tile, 1, tiles)
        left, right = beside(before, here, after, edges)
        values.append(here)
        sums.append(left + right)
        slopes.append(right - left)
    for at in range(count):
        row = low + at
        left = factor * z_ref[tile, sub(row), :]
        value = values[at + 1]
        twice = 2.0 * value
        products[slot, 0, sub(row), :] = left * value
        products[slot, 1, sub(row), :] = left * (twice - sums[at + 1])
        products[slot, 2, sub(row), :] = left * (twice - (values[at] + values[at + 2]))
        products[slot, 3, sub(row), :] = (-0.5 * left) * (slopes[at + 2] - slopes[at])
        products[slot, 4, sub(row), :] = left * pltpu.roll(value, 4, 0)


def gradient_sums(slot, products, start, store):
    for kind in range(5):
        parts = [products[slot, kind, pl.ds(s, SUBS, stride=SUBS), :] for s in range(SUBS)]
        sums = [(parts[4 * c] + parts[4 * c + 1]) + (parts[4 * c + 2] + parts[4 * c + 3]) for c in range(2)]
        if kind < 4:
            for c in range(2):
                store(2 * kind + c, sums[c] + start(2 * kind + c))
        else:
            store(8, (sums[0] + sums[1]) + start(8))


def gradient_kernel(constants, tiles, factor, *refs):
    z_ref, expanded_ref, top_ref, inner_ref, bottom_ref, older_ref, data_ref, series_ref, out_ref, products = refs
    now = inner_rows(top_ref, inner_ref, bottom_ref)

    def coefficient(kind, row, tile):
        return expanded_ref[kind, tile, sub(row), :]

    def store(row, tile, value):
        series_ref[tile, sub(row - 1), :] = value

    def series(row, tile):
        return series_ref[tile, sub(row - 1), :]

    sweep(
        tiles,
        1,
        6,
        now,
        coefficient,
        lambda row, tile: z_ref[tile, sub(row), :],
        lambda row, tile: older_ref[tile, sub(row - 1), :],
        constants,
        store,
    )
    kept = out_ref.shape[2] // LANES
    offset = lax.axis_index("probe") * (tiles - kept)
    count = products.shape[0]
    products[...] = jnp.zeros_like(products)

    def body(step, carry):
        for k in range(count):
            gradient_rows(2, 4, step * count + k + offset, k, series, z_ref, factor, tiles, products)
        for k in range(count):
            index = step * count + k
            cols = tile_columns(index)

            def put(channel, value):
                out_ref[channel, :, cols] = value

            gradient_sums(k, products, lambda channel: data_ref[index + offset, channel], put)
        return carry

    lax.fori_loop(0, kept // count, body, 0)


def end_kernel(upper, constants, tiles, *refs):
    edge_product(upper, constants, tiles, *refs)


def finish_kernel(tiles, factor, z_ref, over_ref, inner_ref, under_ref, part_ref, out_ref, products, target, sem):
    def series(row, tile):
        if row < 1:
            return over_ref[tile, sub(row + 1), :]
        if row > 6:
            return under_ref[tile, sub(row - 7), :]
        return inner_ref[tile, sub(row - 1), :]

    kept = target.shape[2] // LANES
    offset = lax.axis_index("probe") * (tiles - kept)
    count = products.shape[0]
    products[...] = jnp.zeros_like(products)

    def body(step, carry):
        for k in range(count):
            tile = step * count + k + offset
            for low in (0, 6):
                gradient_rows(low, 2, tile, k, series, z_ref, factor, tiles, products)
        for k in range(count):
            cols = tile_columns(step * count + k)

            def put(channel, value):
                target[channel, :, cols] = value

            gradient_sums(k, products, lambda channel: part_ref[channel, :, cols], put)
        return carry

    steps = kept // count
    groups = sem.shape[0]
    copies = []
    for group in range(groups):
        lax.fori_loop(group * steps // groups, (group + 1) * steps // groups, body, 0)
        cols = pl.ds(group * kept // groups * LANES, kept // groups * LANES)
        copies.append(pltpu.make_async_copy(target.at[:, :, cols], out_ref.at[:, :, cols], sem.at[group]))
        copies[-1].start()
    for copy in copies:
        copy.wait()


def border_kernel(tiles, seen_ref, up_ref, down_ref, out_ref, rim_up_ref, rim_down_ref):
    rim(up_ref, rim_up_ref, tiles)
    rim(down_ref, rim_down_ref, tiles)
    chunk = chunk_of(tiles)

    base = tiles + -(-tiles // 8)

    def halo(ref, c, tile):
        row = ref[base + tile // 4, pl.ds(2 * (tile % 4) + c, 1), :]
        return jnp.broadcast_to(row, (SUBS, LANES))

    def body(step, carry):
        edges = masks()
        row = lax.broadcasted_iota(jnp.int32, (SUBS, LANES), 0)
        first = step * chunk
        kept = [[], []]
        for c in range(2):
            values = window_tiles(lambda tile: seen_ref[c, :, tile_columns(tile)], first, chunk, tiles)
            ups = window_tiles(lambda tile: halo(up_ref, c, tile), first, chunk, tiles)
            downs = window_tiles(lambda tile: halo(down_ref, c, tile), first, chunk, tiles)
            aboves = [jnp.where(row == 0, u, pltpu.roll(v, 1, 0)) for u, v in zip(ups, values)]
            belows = [jnp.where(row == SUBS - 1, d, pltpu.roll(v, SUBS - 1, 0)) for d, v in zip(downs, values)]
            tilts = [b - a for a, b in zip(aboves, belows)]
            for k in range(chunk):
                tile = first + k
                value = values[k + 1]
                left, right = beside(values[k], value, values[k + 2], edges)
                low, high = beside(tilts[k], tilts[k + 1], tilts[k + 2], edges)
                half = -0.5 * value
                out_ref[tile, c] = half * value
                out_ref[tile, 2 + c] = half * (2.0 * value - (left + right))
                out_ref[tile, 4 + c] = half * (2.0 * value - (aboves[k + 1] + belows[k + 1]))
                out_ref[tile, 6 + c] = (-0.5 * half) * (high - low)
                kept[c].append(value)
        for k in range(chunk):
            out_ref[first + k, 8] = -(kept[0][k] * kept[1][k])
        return carry

    lax.fori_loop(0, tiles // chunk, body, 0)


def per_device(observations, coefficients, probes):
    weights = cheb_weights(CHEB, lower_edge, upper_edge)
    f32 = jnp.float32
    columns = probes.shape[3]
    share = columns // lax.axis_size("probe")
    width = share + LANES
    tiles = width // LANES
    kept = share // LANES
    rows = lax.axis_size("row")
    down_pairs = [(i, i + 1) for i in range(rows - 1)]
    up_pairs = [(i + 1, i) for i in range(rows - 1)]

    def to_next(edge):
        return lax.ppermute(edge, "row", down_pairs)

    def to_previous(edge):
        return lax.ppermute(edge, "row", up_pairs)

    def call(kernel, name, vregs, operands, outs, scratch=(), in_specs=None, out_specs=None):
        return pl.pallas_call(
            kernel,
            out_shape=outs,
            in_specs=in_specs or [vmem_spec()] * len(operands),
            out_specs=out_specs or jax.tree.map(lambda _: vmem_spec(), outs),
            scratch_shapes=scratch,
            compiler_params=params(),
            cost_estimate=cost(vregs),
            name=name,
        )(*operands)

    eights, fours = -(-tiles // 8), -(-tiles // 4)
    edge_shape = pltpu.VMEM((tiles + eights + fours, SUBS, LANES), f32)
    theirs, own, seen, window, edge_top, edge_bottom = call(
        functools.partial(load_kernel, width),
        "load",
        100,
        [
            pltpu.with_memory_space_constraint(array, pltpu.HBM)
            for array in (probes, observations, coefficients)
        ],
        [
            pltpu.VMEM((2, 2, SUBS, width), f32),
            pltpu.VMEM((2, 2, SUBS, width), f32),
            pltpu.VMEM((2, SUBS, width), f32),
            pltpu.VMEM((9, SUBS, width), f32),
            edge_shape,
            edge_shape,
        ],
        [pltpu.VMEM((count, SUBS * SUBS, LANES), f32) for count in (tiles, eights, fours)]
        + [pltpu.SemaphoreType.DMA((4,))],
        [pl.BlockSpec(memory_space=pltpu.HBM)] * 3,
    )
    other = lax.ppermute(theirs, "probe", [(0, 1), (1, 0)])
    edges_down, edges_up = to_previous(edge_top), to_next(edge_bottom)
    expanded = call(
        prep_kernel, "prep", 5 * 8 * tiles, (window,), pltpu.VMEM((5, tiles, SUBS * SUBS, LANES), f32)
    )
    own, expanded = lax.optimization_barrier((own, expanded))
    def rows_of(count):
        return pltpu.VMEM((tiles, count * SUBS, LANES), f32)

    z, top, bottom = call(
        layout_kernel,
        "layout",
        8 * tiles,
        (own, other),
        [rows_of(SUBS), rows_of(1), rows_of(1)],
    )
    z_down, z_up = to_previous(top), to_next(bottom)
    edge_rows = pltpu.VMEM((2 * tiles, SUBS, LANES), f32)
    constants = (weights[CHEB - 1], weights[CHEB])

    def first(part, halos, out):
        return call(
            functools.partial(first_kernel, part, constants, tiles),
            "first",
            (2 + part % 2 * 2) * tiles,
            [*halos, z, expanded],
            out,
        )

    rim_shape = pltpu.VMEM((5, tiles, SUBS, LANES), f32)
    data, rim_up, rim_down = call(
        functools.partial(border_kernel, tiles),
        "border",
        9 * tiles,
        (seen, edges_up, edges_down),
        [pltpu.VMEM((tiles, 9, SUBS, LANES), f32), rim_shape, rim_shape],
    )
    expanded, data = lax.optimization_barrier((expanded, data))
    inner = first(1, [], rows_of(4))
    bottom = first(2, [z_down], edge_rows)
    up = to_next(bottom)
    top = first(0, [z_up], edge_rows)
    down = to_previous(top)
    once = None
    for order in range(CHEB - 2, 0, -2):
        opening = weights[order] - (weights[CHEB] if order == CHEB - 2 else 0.0)
        steps = ((opening, 1.0), (weights[order - 1], 1.0))
        inner_once, inner_twice = call(
            functools.partial(middle_kernel, steps, tiles),
            "middle",
            10 * tiles,
            [z, expanded, top, inner, bottom] + ([once[1]] if once else []),
            [rows_of(6), rows_of(4)],
        )

        def edge(upper):
            operands = [up if upper else down, z_up if upper else z_down, z, expanded, rim_up if upper else rim_down]
            operands += [top if upper else bottom, inner_once]
            return call(
                functools.partial(edge_kernel, upper, steps, tiles),
                "upper" if upper else "lower",
                4 * tiles,
                operands + ([once[0 if upper else 2]] if once else []),
                [rows_of(2), edge_rows],
            )

        over, under = edge(True), edge(False)
        once = (over[0], inner_once, under[0])
        top, inner, bottom = over[1], inner_twice, under[1]
        down, up = to_previous(top), to_next(bottom)

    factor = 0.5 / (probes.shape[0] * lax.axis_size("probe"))
    count = max(n for n in range(1, 5) if kept % n == 0)
    constants = (weights[0], 0.5)
    products = pltpu.VMEM((count, 5, SUBS * SUBS, LANES), f32)
    whole = (9, SUBS, share)
    series, part = call(
        functools.partial(gradient_kernel, constants, tiles, factor),
        "gradient",
        24 * tiles,
        (z, expanded, top, inner, bottom, once[1], data),
        [rows_of(6), pltpu.VMEM(whole, f32)],
        [products],
    )
    ends = [
        call(
            functools.partial(end_kernel, upper, constants, tiles),
            "upper_end" if upper else "lower_end",
            2 * tiles,
            operands,
            rows_of(2),
        )
        for upper, operands in (
            (True, (up, z_up, z, expanded, rim_up, top, once[0])),
            (False, (down, z_down, z, expanded, rim_down, bottom, once[2])),
        )
    ]
    groups = max(n for n in range(1, 5) if kept // count % n == 0)
    return call(
        functools.partial(finish_kernel, tiles, factor),
        "finish",
        16 * tiles,
        (z, ends[0], series, ends[1], part),
        jax.ShapeDtypeStruct(whole, f32),
        [products, pltpu.VMEM(whole, f32), pltpu.SemaphoreType.DMA((groups,))],
        None,
        pl.BlockSpec(memory_space=pltpu.HBM),
    )


def solution(mesh):
    in_specs = (P("group", "row", None), P("group", "row", None), P("probe", "group", "row", None))
    out_specs = P("group", "row", "probe")
    return jax.shard_map(
        per_device, mesh=mesh, in_specs=in_specs, out_specs=out_specs, check_vma=False
    )
```

```python
import functools
import math

import jax
import jax.numpy as jnp
from jax import lax
from jax.experimental import pallas as pl
from jax.experimental.pallas import tpu as pltpu
from jax.sharding import PartitionSpec as P

CHEB = 6
LANES = 128
SUBS = 8

lower_edge = 0.25
upper_edge = 12.0


def cheb_weights(degree, low_end, high_end):
    count = degree + 1
    values = []
    for order in range(count):
        accum = 0.0
        for node in range(count):
            angle = math.pi * (node + 0.5) / count
            point = 0.5 * (high_end - low_end) * math.cos(angle) + 0.5 * (high_end + low_end)
            accum += math.cos(order * angle) / point
        accum = accum * 2.0 / count
        if order == 0:
            accum = accum * 0.5
        values.append(accum)
    return values


def vmem_spec():
    return pl.BlockSpec(memory_space=pltpu.VMEM)


def params():
    return pltpu.CompilerParams(vmem_limit_bytes=40 * 1024 * 1024)


def cost(vregs):
    return pl.CostEstimate(flops=vregs * 1024 * 20, bytes_accessed=vregs * 4096 * 4, transcendentals=0)


def masks():
    lane = lax.broadcasted_iota(jnp.int32, (SUBS, LANES), 1)
    return lane == 0, lane == LANES - 1


def window_tiles(load, first, count, total):
    before = jnp.where(first > 0, load(jnp.maximum(first - 1, 0)), 0.0)
    after = jnp.where(first + count < total, load(jnp.minimum(first + count, total - 1)), 0.0)
    return [before] + [load(first + k) for k in range(count)] + [after]


def beside(before, here, after, edges):
    left = pltpu.roll(jnp.where(edges[1], before, here), 1, 1)
    right = pltpu.roll(jnp.where(edges[0], after, here), LANES - 1, 1)
    return left, right


def sub(row):
    return pl.ds(row * SUBS, SUBS)


def upside_down():
    return 1 - lax.axis_index("row") % 2


def place(row, flip):
    return row + flip * (SUBS - 1 - 2 * row)


def placed(row, flip):
    at = place(row, flip) * SUBS
    return pl.ds(at if isinstance(at, int) else pl.multiple_of(at, SUBS), SUBS)


def tile_columns(tile):
    return pl.ds(pl.multiple_of(tile * LANES, LANES), LANES)


def chunk_of(tiles):
    return max(count for count in range(1, 12) if tiles % count == 0)


def load_kernel(width, probes_ref, observed_ref, coefficients_ref, *refs):
    theirs_ref, own_ref, seen_ref, window_ref, top_ref, bottom_ref, eight, rest, observed, sem = refs
    core = lax.axis_index("probe")
    move = probes_ref.shape[3] - width
    mine = pl.ds(pl.multiple_of(core * move, LANES), width)
    other = pl.ds(pl.multiple_of((1 - core) * move, LANES), width)
    copies = [
        pltpu.make_async_copy(coefficients_ref.at[:, :, mine], window_ref, sem.at[0]),
        pltpu.make_async_copy(observed_ref.at[:, :, mine], seen_ref, sem.at[1]),
        pltpu.make_async_copy(probes_ref.at[:, :, :, other], theirs_ref, sem.at[2]),
        pltpu.make_async_copy(probes_ref.at[:, :, :, mine], own_ref, sem.at[3]),
    ]
    for copy in copies:
        copy.start()
    rest[...] = jnp.zeros_like(rest)
    observed[...] = jnp.zeros_like(observed)
    copies[0].wait()
    copies[1].wait()
    tiles = width // LANES
    for tile in range(tiles):
        cols = pl.ds(tile * LANES, LANES)
        for channel in range(8):
            eight[tile, pl.ds(channel, SUBS, stride=SUBS), :] = window_ref[channel, :, cols]
        rest[tile // 8, pl.ds(tile % 8, SUBS, stride=SUBS), :] = window_ref[8, :, cols]
        for c in range(2):
            observed[tile // 4, pl.ds(2 * (tile % 4) + c, SUBS, stride=SUBS), :] = seen_ref[c, :, cols]
    flip = upside_down()
    first, last = placed(0, flip), placed(SUBS - 1, flip)
    base = 0
    for source in (eight, rest, observed):
        for index in range(source.shape[0]):
            top_ref[base + index] = source[index, first, :]
            bottom_ref[base + index] = source[index, last, :]
        base += source.shape[0]
    copies[2].wait()
    copies[3].wait()


def combine(kappa, across, along, skew, coupling, sign):
    scale = 4.0 / (upper_edge - lower_edge)
    shift = 2.0 * (upper_edge + lower_edge) / (upper_edge - lower_edge)
    return (
        scale * (kappa + 2.0 * (across + along)) - shift,
        -scale * across,
        -scale * along,
        (-0.5 * scale * sign) * skew,
        scale * coupling,
    )


def prep_kernel(window_ref, expanded_ref):
    tiles = expanded_ref.shape[1]
    chunk = chunk_of(tiles)
    sign = 1.0 - 2.0 * upside_down().astype(jnp.float32)

    def body(step, carry):
        for k in range(chunk):
            tile = step * chunk + k
            cols = tile_columns(tile)
            raw = [window_ref[channel, :, cols] for channel in range(9)]
            for c in range(2):
                values = combine(raw[c], raw[2 + c], raw[4 + c], raw[6 + c], raw[8], sign)
                for kind, value in enumerate(values):
                    for probe in range(4):
                        expanded_ref[kind, tile, pl.ds(4 * c + probe, SUBS, stride=SUBS), :] = value
        return carry

    lax.fori_loop(0, tiles // chunk, body, 0)


def layout_kernel(own_ref, other_ref, z_ref, top_ref, bottom_ref, natural):
    tiles = z_ref.shape[0]
    chunk = chunk_of(tiles)
    flip = upside_down()

    def body(step, carry):
        for k in range(chunk):
            tile = step * chunk + k
            cols = tile_columns(tile)
            for c in range(2):
                for probe in range(2):
                    natural[tile, pl.ds(4 * c + probe, SUBS, stride=SUBS), :] = own_ref[probe, c, :, cols]
                    natural[tile, pl.ds(4 * c + 2 + probe, SUBS, stride=SUBS), :] = other_ref[probe, c, :, cols]
        for k in range(chunk):
            tile = step * chunk + k
            for row in range(SUBS):
                value = natural[tile, placed(row, flip), :]
                z_ref[tile, sub(row), :] = value
                if row == 0:
                    top_ref[tile] = value
                if row == SUBS - 1:
                    bottom_ref[tile] = value
        return carry

    lax.fori_loop(0, tiles // chunk, body, 0)


def rim(edge_ref, rim_ref, tiles):
    chunk = chunk_of(tiles)

    sign = 1.0 - 2.0 * upside_down().astype(jnp.float32)

    def spread(index, row):
        return jnp.broadcast_to(edge_ref[index, pl.ds(row, 1), :], (SUBS, LANES))

    def body(step, carry):
        low = lax.broadcasted_iota(jnp.int32, (SUBS, LANES), 0) < 4
        for k in range(chunk):
            tile = step * chunk + k
            pairs = [jnp.where(low, spread(tile, 2 * kind), spread(tile, 2 * kind + 1)) for kind in range(4)]
            coupling = spread(tiles + tile // 8, tile % 8)
            for kind, value in enumerate(combine(*pairs, coupling, sign)):
                rim_ref[kind, tile] = value
        return carry

    lax.fori_loop(0, tiles // chunk, body, 0)


def sweep(tiles, low, count, load, factor, z_row, before, constants, store):
    weight, scale = constants
    chunk = chunk_of(tiles)

    def body(step, carry):
        edges = masks()
        first = step * chunk
        for k in range(chunk):
            tile = first + k
            values, sums, slopes = [], [], []
            for row in range(low - 1, low + count + 1):
                here = load(row, tile)
                if k == 0:
                    last = jnp.where(first > 0, load(row, jnp.maximum(first - 1, 0)), 0.0)
                else:
                    last = load(row, tile - 1)
                if k == chunk - 1:
                    more = first + chunk < tiles
                    after = jnp.where(more, load(row, jnp.minimum(first + chunk, tiles - 1)), 0.0)
                else:
                    after = load(row, tile + 1)
                left, right = beside(last, here, after, edges)
                values.append(here)
                sums.append(left + right)
                slopes.append(right - left)
            for at in range(count):
                row = low + at
                total = (
                    factor(0, row, tile) * values[at + 1]
                    + factor(1, row, tile) * sums[at + 1]
                    + factor(2, row, tile) * (values[at] + values[at + 2])
                    + factor(3, row, tile) * (slopes[at + 2] - slopes[at])
                    + factor(4, row, tile) * pltpu.roll(values[at + 1], 4, 0)
                )
                if scale != 1.0:
                    total = scale * total
                total = total + weight * z_row(row, tile)
                if before is not None:
                    total = total - before(row, tile)
                store(row, tile, total)
        return carry

    lax.fori_loop(0, tiles // chunk, body, 0)


def first_kernel(part, constants, tiles, *refs):
    halo_ref = None
    if part != 1:
        halo_ref, refs = refs[0], refs[1:]
    z_ref, expanded_ref, out_ref = refs
    low, count = ((0, 2), (2, 4), (6, 2))[part]
    flip = upside_down()

    def now(row, tile):
        if row < 0 or row > 7:
            return halo_ref[tile]
        return z_ref[tile, sub(row), :]

    def store(row, tile, value):
        if part == 1:
            out_ref[tile, sub(row - low), :] = value
        else:
            out_ref[2 * tile + row - low] = value

    def factor(kind, row, tile):
        return expanded_ref[kind, tile, placed(row, flip), :]

    sweep(tiles, low, count, now, factor, lambda row, tile: z_ref[tile, sub(row), :], None, constants, store)


def inner_rows(top_ref, inner_ref, bottom_ref):
    def now(row, tile):
        if row < 2:
            return top_ref[2 * tile + row]
        if row < 6:
            return inner_ref[tile, sub(row - 2), :]
        return bottom_ref[2 * tile + row - 6]

    return now


def middle_kernel(steps, tiles, *refs):
    z_ref, expanded_ref, top_ref, inner_ref, bottom_ref = refs[:5]
    once_ref, twice_ref = refs[-2:]
    now = inner_rows(top_ref, inner_ref, bottom_ref)
    flip = upside_down()

    def factor(kind, row, tile):
        return expanded_ref[kind, tile, placed(row, flip), :]

    def z_row(row, tile):
        return z_ref[tile, sub(row), :]

    def once(row, tile):
        return once_ref[tile, sub(row - 1), :]

    def store_once(row, tile, value):
        once_ref[tile, sub(row - 1), :] = value

    def store_twice(row, tile, value):
        twice_ref[tile, sub(row - 2), :] = value

    older = None
    if len(refs) > 7:
        older = lambda row, tile: refs[5][tile, sub(row - 1), :]
    sweep(tiles, 1, 6, now, factor, z_row, older, steps[0], store_once)
    sweep(tiles, 2, 4, once, factor, z_row, now, steps[1], store_twice)


def edge_product(upper, constants, tiles, halo_ref, z_halo_ref, z_ref, expanded_ref, rim_ref, edge_ref, older_ref, once_ref):
    base = 0 if upper else 6
    flip = upside_down()
    low = -1 if upper else 7

    def now(row, tile):
        if row < 0 or row > 7:
            return halo_ref[2 * tile + (-1 - row if upper else 9 - row)]
        return edge_ref[2 * tile + row - base]

    def factor(kind, row, tile):
        if row < 0 or row > 7:
            return rim_ref[kind, tile]
        return expanded_ref[kind, tile, placed(row, flip), :]

    def z_row(row, tile):
        if row < 0 or row > 7:
            return z_halo_ref[tile]
        return z_ref[tile, sub(row), :]

    def store(row, tile, value):
        once_ref[tile, sub(row - low), :] = value

    older = None if older_ref is None else (lambda row, tile: older_ref[tile, sub(row - low), :])
    sweep(tiles, low, 2, now, factor, z_row, older, constants, store)
    return now, factor, z_row


def edge_kernel(upper, steps, tiles, *refs):
    halo_ref, z_halo_ref, z_ref, expanded_ref, rim_ref, edge_ref, inner_ref = refs[:7]
    once_ref, twice_ref = refs[-2:]
    older_ref = refs[7] if len(refs) > 9 else None
    now, factor, z_row = edge_product(
        upper, steps[0], tiles, halo_ref, z_halo_ref, z_ref, expanded_ref, rim_ref, edge_ref, older_ref, once_ref
    )
    base = 0 if upper else 6
    low = -1 if upper else 7

    def once(row, tile):
        if 1 <= row <= 6:
            return inner_ref[tile, sub(row - 1), :]
        return once_ref[tile, sub(row - low), :]

    def store_twice(row, tile, value):
        twice_ref[2 * tile + row - base] = value

    sweep(tiles, base, 2, once, factor, z_row, now, steps[1], store_twice)


def gradient_rows(low, count, tile, slot, load, z_ref, factor, tiles, products, flip):
    edges = masks()
    values, sums, slopes = [], [], []
    for row in range(low - 1, low + count + 1):
        before, here, after = window_tiles(lambda at: load(row, at), tile, 1, tiles)
        left, right = beside(before, here, after, edges)
        values.append(here)
        sums.append(left + right)
        slopes.append(right - left)
    for at in range(count):
        row = low + at
        left = factor * z_ref[tile, sub(row), :]
        value = values[at + 1]
        twice = 2.0 * value
        rows = placed(row, flip)
        products[slot, 0, rows, :] = left * value
        products[slot, 1, rows, :] = left * (twice - sums[at + 1])
        products[slot, 2, rows, :] = left * (twice - (values[at] + values[at + 2]))
        products[slot, 3, rows, :] = ((flip - 0.5) * left) * (slopes[at + 2] - slopes[at])
        products[slot, 4, rows, :] = left * pltpu.roll(value, 4, 0)


def gradient_sums(slot, products, start, store):
    for kind in range(5):
        parts = [products[slot, kind, pl.ds(s, SUBS, stride=SUBS), :] for s in range(SUBS)]
        sums = [(parts[4 * c] + parts[4 * c + 1]) + (parts[4 * c + 2] + parts[4 * c + 3]) for c in range(2)]
        if kind < 4:
            for c in range(2):
                store(2 * kind + c, sums[c] + start(2 * kind + c))
        else:
            store(8, (sums[0] + sums[1]) + start(8))


def gradient_kernel(constants, tiles, factor, *refs):
    z_ref, expanded_ref, top_ref, inner_ref, bottom_ref, older_ref, data_ref, series_ref, out_ref, products = refs
    now = inner_rows(top_ref, inner_ref, bottom_ref)
    flip = upside_down()

    def coefficient(kind, row, tile):
        return expanded_ref[kind, tile, placed(row, flip), :]

    def store(row, tile, value):
        series_ref[tile, sub(row - 1), :] = value

    def series(row, tile):
        return series_ref[tile, sub(row - 1), :]

    sweep(
        tiles,
        1,
        6,
        now,
        coefficient,
        lambda row, tile: z_ref[tile, sub(row), :],
        lambda row, tile: older_ref[tile, sub(row - 1), :],
        constants,
        store,
    )
    kept = out_ref.shape[2] // LANES
    offset = lax.axis_index("probe") * (tiles - kept)
    count = products.shape[0]
    products[...] = jnp.zeros_like(products)

    def body(turned, step, carry):
        for k in range(count):
            gradient_rows(2, 4, step * count + k + offset, k, series, z_ref, factor, tiles, products, turned)
        for k in range(count):
            index = step * count + k
            cols = tile_columns(index)

            def put(channel, value):
                out_ref[channel, :, cols] = value

            gradient_sums(k, products, lambda channel: data_ref[index + offset, channel], put)
        return carry

    for turned in range(2):

        @pl.when(flip == turned)
        def _():
            lax.fori_loop(0, kept // count, functools.partial(body, turned), 0)


def end_kernel(upper, constants, tiles, *refs):
    edge_product(upper, constants, tiles, *refs)


def finish_kernel(tiles, factor, z_ref, over_ref, inner_ref, under_ref, part_ref, out_ref, products, target, sem):
    def series(row, tile):
        if row < 1:
            return over_ref[tile, sub(row + 1), :]
        if row > 6:
            return under_ref[tile, sub(row - 7), :]
        return inner_ref[tile, sub(row - 1), :]

    kept = target.shape[2] // LANES
    offset = lax.axis_index("probe") * (tiles - kept)
    count = products.shape[0]
    products[...] = jnp.zeros_like(products)

    def body(turned, step, carry):
        for k in range(count):
            tile = step * count + k + offset
            for low in (0, 6):
                gradient_rows(low, 2, tile, k, series, z_ref, factor, tiles, products, turned)
        for k in range(count):
            cols = tile_columns(step * count + k)

            def put(channel, value):
                target[channel, :, cols] = value

            gradient_sums(k, products, lambda channel: part_ref[channel, :, cols], put)
        return carry

    steps = kept // count
    groups = sem.shape[0]

    def run(turned):
        copies = []
        for group in range(groups):
            span = (group * steps // groups, (group + 1) * steps // groups)
            lax.fori_loop(*span, functools.partial(body, turned), 0)
            cols = pl.ds(group * kept // groups * LANES, kept // groups * LANES)
            copies.append(pltpu.make_async_copy(target.at[:, :, cols], out_ref.at[:, :, cols], sem.at[group]))
            copies[-1].start()
        for copy in copies:
            copy.wait()

    for turned in range(2):
        pl.when(upside_down() == turned)(functools.partial(run, turned))


def border_kernel(tiles, seen_ref, up_ref, down_ref, out_ref, rim_up_ref, rim_down_ref):
    rim(up_ref, rim_up_ref, tiles)
    rim(down_ref, rim_down_ref, tiles)
    chunk = chunk_of(tiles)

    base = tiles + -(-tiles // 8)
    flip = upside_down()

    def halo(near, far, c, tile):
        at = (base + tile // 4, pl.ds(2 * (tile % 4) + c, 1), slice(None))
        row = jnp.where(flip == 1, far[at], near[at])
        return jnp.broadcast_to(row, (SUBS, LANES))

    def body(step, carry):
        edges = masks()
        row = lax.broadcasted_iota(jnp.int32, (SUBS, LANES), 0)
        first = step * chunk
        kept = [[], []]
        for c in range(2):
            values = window_tiles(lambda tile: seen_ref[c, :, tile_columns(tile)], first, chunk, tiles)
            ups = window_tiles(lambda tile: halo(up_ref, down_ref, c, tile), first, chunk, tiles)
            downs = window_tiles(lambda tile: halo(down_ref, up_ref, c, tile), first, chunk, tiles)
            aboves = [jnp.where(row == 0, u, pltpu.roll(v, 1, 0)) for u, v in zip(ups, values)]
            belows = [jnp.where(row == SUBS - 1, d, pltpu.roll(v, SUBS - 1, 0)) for d, v in zip(downs, values)]
            tilts = [b - a for a, b in zip(aboves, belows)]
            for k in range(chunk):
                tile = first + k
                value = values[k + 1]
                left, right = beside(values[k], value, values[k + 2], edges)
                low, high = beside(tilts[k], tilts[k + 1], tilts[k + 2], edges)
                half = -0.5 * value
                out_ref[tile, c] = half * value
                out_ref[tile, 2 + c] = half * (2.0 * value - (left + right))
                out_ref[tile, 4 + c] = half * (2.0 * value - (aboves[k + 1] + belows[k + 1]))
                out_ref[tile, 6 + c] = (-0.5 * half) * (high - low)
                kept[c].append(value)
        for k in range(chunk):
            out_ref[first + k, 8] = -(kept[0][k] * kept[1][k])
        return carry

    lax.fori_loop(0, tiles // chunk, body, 0)


def per_device(observations, coefficients, probes):
    weights = cheb_weights(CHEB, lower_edge, upper_edge)
    f32 = jnp.float32
    columns = probes.shape[3]
    share = columns // lax.axis_size("probe")
    width = share + LANES
    tiles = width // LANES
    kept = share // LANES
    rows = lax.axis_size("row")
    near_pairs = [pair for i in range(0, rows - 1, 2) for pair in ((i, i + 1), (i + 1, i))]
    far_pairs = [pair for i in range(1, rows - 1, 2) for pair in ((i, i + 1), (i + 1, i))]

    def near(edge):
        return lax.ppermute(edge, "row", near_pairs)

    def far(edge):
        return lax.ppermute(edge, "row", far_pairs)

    def call(kernel, name, vregs, operands, outs, scratch=(), in_specs=None, out_specs=None):
        return pl.pallas_call(
            kernel,
            out_shape=outs,
            in_specs=in_specs or [vmem_spec()] * len(operands),
            out_specs=out_specs or jax.tree.map(lambda _: vmem_spec(), outs),
            scratch_shapes=scratch,
            compiler_params=params(),
            cost_estimate=cost(vregs),
            name=name,
        )(*operands)

    eights, fours = -(-tiles // 8), -(-tiles // 4)
    edge_shape = pltpu.VMEM((tiles + eights + fours, SUBS, LANES), f32)
    theirs, own, seen, window, edge_top, edge_bottom = call(
        functools.partial(load_kernel, width),
        "load",
        100,
        [
            pltpu.with_memory_space_constraint(array, pltpu.HBM)
            for array in (probes, observations, coefficients)
        ],
        [
            pltpu.VMEM((2, 2, SUBS, width), f32),
            pltpu.VMEM((2, 2, SUBS, width), f32),
            pltpu.VMEM((2, SUBS, width), f32),
            pltpu.VMEM((9, SUBS, width), f32),
            edge_shape,
            edge_shape,
        ],
        [pltpu.VMEM((count, SUBS * SUBS, LANES), f32) for count in (tiles, eights, fours)]
        + [pltpu.SemaphoreType.DMA((4,))],
        [pl.BlockSpec(memory_space=pltpu.HBM)] * 3,
    )
    other = lax.ppermute(theirs, "probe", [(0, 1), (1, 0)])
    edges_up, edges_down = near(edge_top), far(edge_bottom)
    expanded = call(
        prep_kernel, "prep", 5 * 8 * tiles, (window,), pltpu.VMEM((5, tiles, SUBS * SUBS, LANES), f32)
    )
    own, expanded = lax.optimization_barrier((own, expanded))
    def rows_of(count):
        return pltpu.VMEM((tiles, count * SUBS, LANES), f32)

    z, top, bottom = call(
        layout_kernel,
        "layout",
        8 * tiles,
        (own, other),
        [rows_of(SUBS), rows_of(1), rows_of(1)],
        [rows_of(SUBS)],
    )
    z_up, z_down = near(top), far(bottom)
    edge_rows = pltpu.VMEM((2 * tiles, SUBS, LANES), f32)
    constants = (weights[CHEB - 1], weights[CHEB])

    def first(part, halos, out):
        return call(
            functools.partial(first_kernel, part, constants, tiles),
            "first",
            (2 + part % 2 * 2) * tiles,
            [*halos, z, expanded],
            out,
        )

    rim_shape = pltpu.VMEM((5, tiles, SUBS, LANES), f32)
    data, rim_up, rim_down = call(
        functools.partial(border_kernel, tiles),
        "border",
        9 * tiles,
        (seen, edges_up, edges_down),
        [pltpu.VMEM((tiles, 9, SUBS, LANES), f32), rim_shape, rim_shape],
    )
    expanded, data = lax.optimization_barrier((expanded, data))
    inner = first(1, [], rows_of(4))
    bottom = first(2, [z_down], edge_rows)
    down = far(bottom)
    top = first(0, [z_up], edge_rows)
    up = near(top)
    once = None
    for order in range(CHEB - 2, 0, -2):
        opening = weights[order] - (weights[CHEB] if order == CHEB - 2 else 0.0)
        steps = ((opening, 1.0), (weights[order - 1], 1.0))
        inner_once, inner_twice = call(
            functools.partial(middle_kernel, steps, tiles),
            "middle",
            10 * tiles,
            [z, expanded, top, inner, bottom] + ([once[1]] if once else []),
            [rows_of(6), rows_of(4)],
        )

        def edge(upper):
            operands = [up if upper else down, z_up if upper else z_down, z, expanded, rim_up if upper else rim_down]
            operands += [top if upper else bottom, inner_once]
            return call(
                functools.partial(edge_kernel, upper, steps, tiles),
                "upper" if upper else "lower",
                4 * tiles,
                operands + ([once[0 if upper else 2]] if once else []),
                [rows_of(2), edge_rows],
            )

        over, under = edge(True), edge(False)
        once = (over[0], inner_once, under[0])
        top, inner, bottom = over[1], inner_twice, under[1]
        up, down = near(top), far(bottom)

    factor = 0.5 / (probes.shape[0] * lax.axis_size("probe"))
    count = max(n for n in range(1, 5) if kept % n == 0)
    constants = (weights[0], 0.5)
    products = pltpu.VMEM((count, 5, SUBS * SUBS, LANES), f32)
    whole = (9, SUBS, share)
    series, part = call(
        functools.partial(gradient_kernel, constants, tiles, factor),
        "gradient",
        24 * tiles,
        (z, expanded, top, inner, bottom, once[1], data),
        [rows_of(6), pltpu.VMEM(whole, f32)],
        [products],
    )
    ends = [
        call(
            functools.partial(end_kernel, upper, constants, tiles),
            "upper_end" if upper else "lower_end",
            2 * tiles,
            operands,
            rows_of(2),
        )
        for upper, operands in (
            (True, (up, z_up, z, expanded, rim_up, top, once[0])),
            (False, (down, z_down, z, expanded, rim_down, bottom, once[2])),
        )
    ]
    groups = max(n for n in range(1, 5) if kept // count % n == 0)
    return call(
        functools.partial(finish_kernel, tiles, factor),
        "finish",
        16 * tiles,
        (z, ends[0], series, ends[1], part),
        jax.ShapeDtypeStruct(whole, f32),
        [products, pltpu.VMEM(whole, f32), pltpu.SemaphoreType.DMA((groups,))],
        None,
        pl.BlockSpec(memory_space=pltpu.HBM),
    )


def solution(mesh):
    in_specs = (P("group", "row", None), P("group", "row", None), P("probe", "group", "row", None))
    out_specs = P("group", "row", "probe")
    return jax.shard_map(
        per_device, mesh=mesh, in_specs=in_specs, out_specs=out_specs, check_vma=False
    )
```

```python
import functools
import math

import jax
import jax.numpy as jnp
from jax import lax
from jax.experimental import pallas as pl
from jax.experimental.pallas import tpu as pltpu
from jax.sharding import PartitionSpec as P

CHEB = 6
LANES = 128
SUBS = 8

lower_edge = 0.25
upper_edge = 12.0


def cheb_weights(degree, low_end, high_end):
    count = degree + 1
    values = []
    for order in range(count):
        accum = 0.0
        for node in range(count):
            angle = math.pi * (node + 0.5) / count
            point = 0.5 * (high_end - low_end) * math.cos(angle) + 0.5 * (high_end + low_end)
            accum += math.cos(order * angle) / point
        accum = accum * 2.0 / count
        if order == 0:
            accum = accum * 0.5
        values.append(accum)
    return values


def vmem_spec():
    return pl.BlockSpec(memory_space=pltpu.VMEM)


def params():
    return pltpu.CompilerParams(vmem_limit_bytes=40 * 1024 * 1024)


def cost(vregs):
    return pl.CostEstimate(flops=vregs * 1024 * 20, bytes_accessed=vregs * 4096 * 4, transcendentals=0)


def masks():
    lane = lax.broadcasted_iota(jnp.int32, (SUBS, LANES), 1)
    return lane == 0, lane == LANES - 1


def window_tiles(load, first, count, total):
    before = jnp.where(first > 0, load(jnp.maximum(first - 1, 0)), 0.0)
    after = jnp.where(first + count < total, load(jnp.minimum(first + count, total - 1)), 0.0)
    return [before] + [load(first + k) for k in range(count)] + [after]


def beside(before, here, after, edges):
    left = pltpu.roll(jnp.where(edges[1], before, here), 1, 1)
    right = pltpu.roll(jnp.where(edges[0], after, here), LANES - 1, 1)
    return left, right


def sub(row):
    return pl.ds(row * SUBS, SUBS)


def upside_down():
    return 1 - lax.axis_index("row") % 2


def place(row, flip):
    return row + flip * (SUBS - 1 - 2 * row)


def placed(row, flip):
    at = place(row, flip) * SUBS
    return pl.ds(at if isinstance(at, int) else pl.multiple_of(at, SUBS), SUBS)


def tile_columns(tile):
    return pl.ds(pl.multiple_of(tile * LANES, LANES), LANES)


def chunk_of(tiles):
    return max(count for count in range(1, 12) if tiles % count == 0)


def load_kernel(width, probes_ref, observed_ref, coefficients_ref, *refs):
    theirs_ref, own_ref, seen_ref, window_ref, top_ref, bottom_ref, eight, rest, observed, sem = refs
    core = lax.axis_index("probe")
    move = probes_ref.shape[3] - width
    mine = pl.ds(pl.multiple_of(core * move, LANES), width)
    other = pl.ds(pl.multiple_of((1 - core) * move, LANES), width)
    copies = [
        pltpu.make_async_copy(coefficients_ref.at[:, :, mine], window_ref, sem.at[0]),
        pltpu.make_async_copy(observed_ref.at[:, :, mine], seen_ref, sem.at[1]),
        pltpu.make_async_copy(probes_ref.at[:, :, :, other], theirs_ref, sem.at[2]),
        pltpu.make_async_copy(probes_ref.at[:, :, :, mine], own_ref, sem.at[3]),
    ]
    for copy in copies:
        copy.start()
    rest[...] = jnp.zeros_like(rest)
    observed[...] = jnp.zeros_like(observed)
    copies[0].wait()
    copies[1].wait()
    tiles = width // LANES
    for tile in range(tiles):
        cols = pl.ds(tile * LANES, LANES)
        for channel in range(8):
            eight[tile, pl.ds(channel, SUBS, stride=SUBS), :] = window_ref[channel, :, cols]
        rest[tile // 8, pl.ds(tile % 8, SUBS, stride=SUBS), :] = window_ref[8, :, cols]
        for c in range(2):
            observed[tile // 4, pl.ds(2 * (tile % 4) + c, SUBS, stride=SUBS), :] = seen_ref[c, :, cols]
    flip = upside_down()
    first, last = placed(0, flip), placed(SUBS - 1, flip)
    base = 0
    for source in (eight, rest, observed):
        for index in range(source.shape[0]):
            top_ref[base + index] = source[index, first, :]
            bottom_ref[base + index] = source[index, last, :]
        base += source.shape[0]
    copies[2].wait()
    copies[3].wait()


def combine(kappa, across, along, skew, coupling, sign):
    scale = 4.0 / (upper_edge - lower_edge)
    shift = 2.0 * (upper_edge + lower_edge) / (upper_edge - lower_edge)
    return (
        scale * (kappa + 2.0 * (across + along)) - shift,
        -scale * across,
        -scale * along,
        (-0.5 * scale * sign) * skew,
        scale * coupling,
    )


def prep_kernel(window_ref, expanded_ref):
    tiles = expanded_ref.shape[1]
    chunk = chunk_of(tiles)
    sign = 1.0 - 2.0 * upside_down().astype(jnp.float32)

    def body(step, carry):
        for k in range(chunk):
            tile = step * chunk + k
            cols = tile_columns(tile)
            raw = [window_ref[channel, :, cols] for channel in range(9)]
            for c in range(2):
                values = combine(raw[c], raw[2 + c], raw[4 + c], raw[6 + c], raw[8], sign)
                for kind, value in enumerate(values):
                    for probe in range(4):
                        expanded_ref[kind, tile, pl.ds(4 * c + probe, SUBS, stride=SUBS), :] = value
        return carry

    lax.fori_loop(0, tiles // chunk, body, 0)


def layout_kernel(own_ref, other_ref, z_ref, top_ref, bottom_ref, natural):
    tiles = z_ref.shape[0]
    chunk = chunk_of(tiles)
    flip = upside_down()

    def body(step, carry):
        for k in range(chunk):
            tile = step * chunk + k
            cols = tile_columns(tile)
            for c in range(2):
                for probe in range(2):
                    natural[tile, pl.ds(4 * c + probe, SUBS, stride=SUBS), :] = own_ref[probe, c, :, cols]
                    natural[tile, pl.ds(4 * c + 2 + probe, SUBS, stride=SUBS), :] = other_ref[probe, c, :, cols]
        for k in range(chunk):
            tile = step * chunk + k
            for row in range(SUBS):
                value = natural[tile, placed(row, flip), :]
                z_ref[tile, sub(row), :] = value
                if row == 0:
                    top_ref[tile] = value
                if row == SUBS - 1:
                    bottom_ref[tile] = value
        return carry

    lax.fori_loop(0, tiles // chunk, body, 0)


def rim(edge_ref, rim_ref, tiles):
    chunk = chunk_of(tiles)

    sign = 1.0 - 2.0 * upside_down().astype(jnp.float32)

    def spread(index, row):
        return jnp.broadcast_to(edge_ref[index, pl.ds(row, 1), :], (SUBS, LANES))

    def body(step, carry):
        low = lax.broadcasted_iota(jnp.int32, (SUBS, LANES), 0) < 4
        for k in range(chunk):
            tile = step * chunk + k
            pairs = [jnp.where(low, spread(tile, 2 * kind), spread(tile, 2 * kind + 1)) for kind in range(4)]
            coupling = spread(tiles + tile // 8, tile % 8)
            for kind, value in enumerate(combine(*pairs, coupling, sign)):
                rim_ref[kind, tile] = value
        return carry

    lax.fori_loop(0, tiles // chunk, body, 0)


def sweep(tiles, low, count, load, factor, z_row, before, constants, store):
    weight, scale = constants
    chunk = tiles if count <= 2 else chunk_of(tiles)

    def body(step, carry):
        edges = masks()
        first = step * chunk
        for k in range(chunk):
            tile = first + k
            values, sums, slopes = [], [], []
            for row in range(low - 1, low + count + 1):
                here = load(row, tile)
                if k == 0 and chunk == tiles:
                    last = jnp.zeros_like(here)
                elif k == 0:
                    last = jnp.where(first > 0, load(row, jnp.maximum(first - 1, 0)), 0.0)
                else:
                    last = load(row, tile - 1)
                if k == chunk - 1 and chunk == tiles:
                    after = jnp.zeros_like(here)
                elif k == chunk - 1:
                    more = first + chunk < tiles
                    after = jnp.where(more, load(row, jnp.minimum(first + chunk, tiles - 1)), 0.0)
                else:
                    after = load(row, tile + 1)
                left, right = beside(last, here, after, edges)
                values.append(here)
                sums.append(left + right)
                slopes.append(right - left)
            for at in range(count):
                row = low + at
                total = (
                    factor(0, row, tile) * values[at + 1]
                    + factor(1, row, tile) * sums[at + 1]
                    + factor(2, row, tile) * (values[at] + values[at + 2])
                    + factor(3, row, tile) * (slopes[at + 2] - slopes[at])
                    + factor(4, row, tile) * pltpu.roll(values[at + 1], 4, 0)
                )
                if scale != 1.0:
                    total = scale * total
                total = total + weight * z_row(row, tile)
                if before is not None:
                    total = total - before(row, tile)
                store(row, tile, total)
        return carry

    if chunk == tiles:
        body(0, 0)
    else:
        lax.fori_loop(0, tiles // chunk, body, 0)


def first_kernel(part, constants, tiles, *refs):
    halo_ref = None
    if part != 1:
        halo_ref, refs = refs[0], refs[1:]
    z_ref, expanded_ref, out_ref = refs
    low, count = ((0, 2), (2, 4), (6, 2))[part]
    flip = upside_down()

    def now(row, tile):
        if row < 0 or row > 7:
            return halo_ref[tile]
        return z_ref[tile, sub(row), :]

    def store(row, tile, value):
        if part == 1:
            out_ref[tile, sub(row - low), :] = value
        else:
            out_ref[2 * tile + row - low] = value

    def factor(kind, row, tile):
        return expanded_ref[kind, tile, placed(row, flip), :]

    sweep(tiles, low, count, now, factor, lambda row, tile: z_ref[tile, sub(row), :], None, constants, store)


def inner_rows(top_ref, inner_ref, bottom_ref):
    def now(row, tile):
        if row < 2:
            return top_ref[2 * tile + row]
        if row < 6:
            return inner_ref[tile, sub(row - 2), :]
        return bottom_ref[2 * tile + row - 6]

    return now


def middle_kernel(steps, tiles, *refs):
    z_ref, expanded_ref, top_ref, inner_ref, bottom_ref = refs[:5]
    once_ref, twice_ref = refs[-2:]
    now = inner_rows(top_ref, inner_ref, bottom_ref)
    flip = upside_down()

    def factor(kind, row, tile):
        return expanded_ref[kind, tile, placed(row, flip), :]

    def z_row(row, tile):
        return z_ref[tile, sub(row), :]

    def once(row, tile):
        return once_ref[tile, sub(row - 1), :]

    def store_once(row, tile, value):
        once_ref[tile, sub(row - 1), :] = value

    def store_twice(row, tile, value):
        twice_ref[tile, sub(row - 2), :] = value

    older = None
    if len(refs) > 7:
        older = lambda row, tile: refs[5][tile, sub(row - 1), :]
    sweep(tiles, 1, 6, now, factor, z_row, older, steps[0], store_once)
    sweep(tiles, 2, 4, once, factor, z_row, now, steps[1], store_twice)


def edge_product(upper, constants, tiles, halo_ref, z_halo_ref, z_ref, expanded_ref, rim_ref, edge_ref, older_ref, once_ref):
    base = 0 if upper else 6
    flip = upside_down()
    low = -1 if upper else 7

    def now(row, tile):
        if row < 0 or row > 7:
            return halo_ref[2 * tile + (-1 - row if upper else 9 - row)]
        return edge_ref[2 * tile + row - base]

    def factor(kind, row, tile):
        if row < 0 or row > 7:
            return rim_ref[kind, tile]
        return expanded_ref[kind, tile, placed(row, flip), :]

    def z_row(row, tile):
        if row < 0 or row > 7:
            return z_halo_ref[tile]
        return z_ref[tile, sub(row), :]

    def store(row, tile, value):
        once_ref[tile, sub(row - low), :] = value

    older = None if older_ref is None else (lambda row, tile: older_ref[tile, sub(row - low), :])
    sweep(tiles, low, 2, now, factor, z_row, older, constants, store)
    return now, factor, z_row


def edge_kernel(upper, steps, tiles, *refs):
    halo_ref, z_halo_ref, z_ref, expanded_ref, rim_ref, edge_ref, inner_ref = refs[:7]
    once_ref, twice_ref = refs[-2:]
    older_ref = refs[7] if len(refs) > 9 else None
    now, factor, z_row = edge_product(
        upper, steps[0], tiles, halo_ref, z_halo_ref, z_ref, expanded_ref, rim_ref, edge_ref, older_ref, once_ref
    )
    base = 0 if upper else 6
    low = -1 if upper else 7

    def once(row, tile):
        if 1 <= row <= 6:
            return inner_ref[tile, sub(row - 1), :]
        return once_ref[tile, sub(row - low), :]

    def store_twice(row, tile, value):
        twice_ref[2 * tile + row - base] = value

    sweep(tiles, base, 2, once, factor, z_row, now, steps[1], store_twice)


def gradient_rows(low, count, tile, slot, load, z_ref, factor, tiles, products, flip):
    edges = masks()
    values, sums, slopes = [], [], []
    for row in range(low - 1, low + count + 1):
        before, here, after = window_tiles(lambda at: load(row, at), tile, 1, tiles)
        left, right = beside(before, here, after, edges)
        values.append(here)
        sums.append(left + right)
        slopes.append(right - left)
    for at in range(count):
        row = low + at
        left = factor * z_ref[tile, sub(row), :]
        value = values[at + 1]
        twice = 2.0 * value
        rows = placed(row, flip)
        products[slot, 0, rows, :] = left * value
        products[slot, 1, rows, :] = left * (twice - sums[at + 1])
        products[slot, 2, rows, :] = left * (twice - (values[at] + values[at + 2]))
        products[slot, 3, rows, :] = ((flip - 0.5) * left) * (slopes[at + 2] - slopes[at])
        products[slot, 4, rows, :] = left * pltpu.roll(value, 4, 0)


def gradient_sums(slot, products, start, store):
    for kind in range(5):
        parts = [products[slot, kind, pl.ds(s, SUBS, stride=SUBS), :] for s in range(SUBS)]
        sums = [(parts[4 * c] + parts[4 * c + 1]) + (parts[4 * c + 2] + parts[4 * c + 3]) for c in range(2)]
        if kind < 4:
            for c in range(2):
                store(2 * kind + c, sums[c] + start(2 * kind + c))
        else:
            store(8, (sums[0] + sums[1]) + start(8))


def gradient_kernel(constants, tiles, factor, *refs):
    z_ref, expanded_ref, top_ref, inner_ref, bottom_ref, older_ref, data_ref, series_ref, out_ref, products = refs
    now = inner_rows(top_ref, inner_ref, bottom_ref)
    flip = upside_down()

    def coefficient(kind, row, tile):
        return expanded_ref[kind, tile, placed(row, flip), :]

    def store(row, tile, value):
        series_ref[tile, sub(row - 1), :] = value

    def series(row, tile):
        return series_ref[tile, sub(row - 1), :]

    sweep(
        tiles,
        1,
        6,
        now,
        coefficient,
        lambda row, tile: z_ref[tile, sub(row), :],
        lambda row, tile: older_ref[tile, sub(row - 1), :],
        constants,
        store,
    )
    kept = out_ref.shape[2] // LANES
    offset = lax.axis_index("probe") * (tiles - kept)
    count = products.shape[0]
    products[...] = jnp.zeros_like(products)

    def body(turned, step, carry):
        for k in range(count):
            gradient_rows(2, 4, step * count + k + offset, k, series, z_ref, factor, tiles, products, turned)
        for k in range(count):
            index = step * count + k
            cols = tile_columns(index)

            def put(channel, value):
                out_ref[channel, :, cols] = value

            gradient_sums(k, products, lambda channel: data_ref[index + offset, channel], put)
        return carry

    for turned in range(2):

        @pl.when(flip == turned)
        def _():
            lax.fori_loop(0, kept // count, functools.partial(body, turned), 0)


def end_kernel(upper, constants, tiles, *refs):
    edge_product(upper, constants, tiles, *refs)


def finish_kernel(tiles, factor, z_ref, over_ref, inner_ref, under_ref, part_ref, out_ref, products, target, sem):
    def series(row, tile):
        if row < 1:
            return over_ref[tile, sub(row + 1), :]
        if row > 6:
            return under_ref[tile, sub(row - 7), :]
        return inner_ref[tile, sub(row - 1), :]

    kept = target.shape[2] // LANES
    offset = lax.axis_index("probe") * (tiles - kept)
    count = products.shape[0]
    products[...] = jnp.zeros_like(products)

    def body(turned, step, carry):
        for k in range(count):
            tile = step * count + k + offset
            for low in (0, 6):
                gradient_rows(low, 2, tile, k, series, z_ref, factor, tiles, products, turned)
        for k in range(count):
            cols = tile_columns(step * count + k)

            def put(channel, value):
                target[channel, :, cols] = value

            gradient_sums(k, products, lambda channel: part_ref[channel, :, cols], put)
        return carry

    steps = kept // count
    groups = sem.shape[0]

    def run(turned):
        copies = []
        for group in range(groups):
            span = (group * steps // groups, (group + 1) * steps // groups)
            lax.fori_loop(*span, functools.partial(body, turned), 0)
            cols = pl.ds(group * kept // groups * LANES, kept // groups * LANES)
            copies.append(pltpu.make_async_copy(target.at[:, :, cols], out_ref.at[:, :, cols], sem.at[group]))
            copies[-1].start()
        for copy in copies:
            copy.wait()

    for turned in range(2):
        pl.when(upside_down() == turned)(functools.partial(run, turned))


def border_kernel(tiles, seen_ref, up_ref, down_ref, out_ref, rim_up_ref, rim_down_ref):
    rim(up_ref, rim_up_ref, tiles)
    rim(down_ref, rim_down_ref, tiles)
    chunk = chunk_of(tiles)

    base = tiles + -(-tiles // 8)
    flip = upside_down()

    def halo(near, far, c, tile):
        at = (base + tile // 4, pl.ds(2 * (tile % 4) + c, 1), slice(None))
        row = jnp.where(flip == 1, far[at], near[at])
        return jnp.broadcast_to(row, (SUBS, LANES))

    def body(step, carry):
        edges = masks()
        row = lax.broadcasted_iota(jnp.int32, (SUBS, LANES), 0)
        first = step * chunk
        kept = [[], []]
        for c in range(2):
            values = window_tiles(lambda tile: seen_ref[c, :, tile_columns(tile)], first, chunk, tiles)
            ups = window_tiles(lambda tile: halo(up_ref, down_ref, c, tile), first, chunk, tiles)
            downs = window_tiles(lambda tile: halo(down_ref, up_ref, c, tile), first, chunk, tiles)
            aboves = [jnp.where(row == 0, u, pltpu.roll(v, 1, 0)) for u, v in zip(ups, values)]
            belows = [jnp.where(row == SUBS - 1, d, pltpu.roll(v, SUBS - 1, 0)) for d, v in zip(downs, values)]
            tilts = [b - a for a, b in zip(aboves, belows)]
            for k in range(chunk):
                tile = first + k
                value = values[k + 1]
                left, right = beside(values[k], value, values[k + 2], edges)
                low, high = beside(tilts[k], tilts[k + 1], tilts[k + 2], edges)
                half = -0.5 * value
                out_ref[tile, c] = half * value
                out_ref[tile, 2 + c] = half * (2.0 * value - (left + right))
                out_ref[tile, 4 + c] = half * (2.0 * value - (aboves[k + 1] + belows[k + 1]))
                out_ref[tile, 6 + c] = (-0.5 * half) * (high - low)
                kept[c].append(value)
        for k in range(chunk):
            out_ref[first + k, 8] = -(kept[0][k] * kept[1][k])
        return carry

    lax.fori_loop(0, tiles // chunk, body, 0)


def per_device(observations, coefficients, probes):
    weights = cheb_weights(CHEB, lower_edge, upper_edge)
    f32 = jnp.float32
    columns = probes.shape[3]
    share = columns // lax.axis_size("probe")
    width = share + LANES
    tiles = width // LANES
    kept = share // LANES
    rows = lax.axis_size("row")
    near_pairs = [pair for i in range(0, rows - 1, 2) for pair in ((i, i + 1), (i + 1, i))]
    far_pairs = [pair for i in range(1, rows - 1, 2) for pair in ((i, i + 1), (i + 1, i))]

    def near(edge):
        return lax.ppermute(edge, "row", near_pairs)

    def far(edge):
        return lax.ppermute(edge, "row", far_pairs)

    def call(kernel, name, vregs, operands, outs, scratch=(), in_specs=None, out_specs=None):
        return pl.pallas_call(
            kernel,
            out_shape=outs,
            in_specs=in_specs or [vmem_spec()] * len(operands),
            out_specs=out_specs or jax.tree.map(lambda _: vmem_spec(), outs),
            scratch_shapes=scratch,
            compiler_params=params(),
            cost_estimate=cost(vregs),
            name=name,
        )(*operands)

    eights, fours = -(-tiles // 8), -(-tiles // 4)
    edge_shape = pltpu.VMEM((tiles + eights + fours, SUBS, LANES), f32)
    theirs, own, seen, window, edge_top, edge_bottom = call(
        functools.partial(load_kernel, width),
        "load",
        100,
        [
            pltpu.with_memory_space_constraint(array, pltpu.HBM)
            for array in (probes, observations, coefficients)
        ],
        [
            pltpu.VMEM((2, 2, SUBS, width), f32),
            pltpu.VMEM((2, 2, SUBS, width), f32),
            pltpu.VMEM((2, SUBS, width), f32),
            pltpu.VMEM((9, SUBS, width), f32),
            edge_shape,
            edge_shape,
        ],
        [pltpu.VMEM((count, SUBS * SUBS, LANES), f32) for count in (tiles, eights, fours)]
        + [pltpu.SemaphoreType.DMA((4,))],
        [pl.BlockSpec(memory_space=pltpu.HBM)] * 3,
    )
    other = lax.ppermute(theirs, "probe", [(0, 1), (1, 0)])
    edges_up, edges_down = near(edge_top), far(edge_bottom)
    expanded = call(
        prep_kernel, "prep", 5 * 8 * tiles, (window,), pltpu.VMEM((5, tiles, SUBS * SUBS, LANES), f32)
    )
    own, expanded = lax.optimization_barrier((own, expanded))
    def rows_of(count):
        return pltpu.VMEM((tiles, count * SUBS, LANES), f32)

    z, top, bottom = call(
        layout_kernel,
        "layout",
        8 * tiles,
        (own, other),
        [rows_of(SUBS), rows_of(1), rows_of(1)],
        [rows_of(SUBS)],
    )
    z_up, z_down = near(top), far(bottom)
    edge_rows = pltpu.VMEM((2 * tiles, SUBS, LANES), f32)
    constants = (weights[CHEB - 1], weights[CHEB])

    def first(part, halos, out):
        return call(
            functools.partial(first_kernel, part, constants, tiles),
            "first",
            (2 + part % 2 * 2) * tiles,
            [*halos, z, expanded],
            out,
        )

    rim_shape = pltpu.VMEM((5, tiles, SUBS, LANES), f32)
    data, rim_up, rim_down = call(
        functools.partial(border_kernel, tiles),
        "border",
        9 * tiles,
        (seen, edges_up, edges_down),
        [pltpu.VMEM((tiles, 9, SUBS, LANES), f32), rim_shape, rim_shape],
    )
    expanded, data = lax.optimization_barrier((expanded, data))
    inner = first(1, [], rows_of(4))
    bottom = first(2, [z_down], edge_rows)
    _, near_halo = lax.optimization_barrier((bottom, z_up))
    down = far(bottom)
    top = first(0, [near_halo], edge_rows)
    up = near(top)
    once = None
    for order in range(CHEB - 2, 0, -2):
        opening = weights[order] - (weights[CHEB] if order == CHEB - 2 else 0.0)
        steps = ((opening, 1.0), (weights[order - 1], 1.0))
        inner_once, inner_twice = call(
            functools.partial(middle_kernel, steps, tiles),
            "middle",
            10 * tiles,
            [z, expanded, top, inner, bottom] + ([once[1]] if once else []),
            [rows_of(6), rows_of(4)],
        )

        def edge(upper):
            operands = [up if upper else down, z_up if upper else z_down, z, expanded, rim_up if upper else rim_down]
            operands += [top if upper else bottom, inner_once]
            return call(
                functools.partial(edge_kernel, upper, steps, tiles),
                "upper" if upper else "lower",
                4 * tiles,
                operands + ([once[0 if upper else 2]] if once else []),
                [rows_of(2), edge_rows],
            )

        under = edge(False)
        _, up = lax.optimization_barrier((under[1], up))
        over = edge(True)
        once = (over[0], inner_once, under[0])
        top, inner, bottom = over[1], inner_twice, under[1]
        down, up = far(bottom), near(top)

    factor = 0.5 / (probes.shape[0] * lax.axis_size("probe"))
    count = max(n for n in range(1, 5) if kept % n == 0)
    constants = (weights[0], 0.5)
    products = pltpu.VMEM((count, 5, SUBS * SUBS, LANES), f32)
    whole = (9, SUBS, share)
    series, part = call(
        functools.partial(gradient_kernel, constants, tiles, factor),
        "gradient",
        24 * tiles,
        (z, expanded, top, inner, bottom, once[1], data),
        [rows_of(6), pltpu.VMEM(whole, f32)],
        [products],
    )
    ends = [
        call(
            functools.partial(end_kernel, upper, constants, tiles),
            "upper_end" if upper else "lower_end",
            2 * tiles,
            operands,
            rows_of(2),
        )
        for upper, operands in (
            (True, (up, z_up, z, expanded, rim_up, top, once[0])),
            (False, (down, z_down, z, expanded, rim_down, bottom, once[2])),
        )
    ]
    groups = max(n for n in range(1, 5) if kept // count % n == 0)
    return call(
        functools.partial(finish_kernel, tiles, factor),
        "finish",
        16 * tiles,
        (z, ends[0], series, ends[1], part),
        jax.ShapeDtypeStruct(whole, f32),
        [products, pltpu.VMEM(whole, f32), pltpu.SemaphoreType.DMA((groups,))],
        None,
        pl.BlockSpec(memory_space=pltpu.HBM),
    )


def solution(mesh):
    in_specs = (P("group", "row", None), P("group", "row", None), P("probe", "group", "row", None))
    out_specs = P("group", "row", "probe")
    return jax.shard_map(
        per_device, mesh=mesh, in_specs=in_specs, out_specs=out_specs, check_vma=False
    )
```

```python
import functools
import math

import jax
import jax.numpy as jnp
from jax import lax
from jax.experimental import pallas as pl
from jax.experimental.pallas import tpu as pltpu
from jax.sharding import PartitionSpec as P

CHEB = 6
LANES = 128
SUBS = 8

lower_edge = 0.25
upper_edge = 12.0


def cheb_weights(degree, low_end, high_end):
    count = degree + 1
    values = []
    for order in range(count):
        accum = 0.0
        for node in range(count):
            angle = math.pi * (node + 0.5) / count
            point = 0.5 * (high_end - low_end) * math.cos(angle) + 0.5 * (high_end + low_end)
            accum += math.cos(order * angle) / point
        accum = accum * 2.0 / count
        if order == 0:
            accum = accum * 0.5
        values.append(accum)
    return values


def vmem_spec():
    return pl.BlockSpec(memory_space=pltpu.VMEM)


def params():
    return pltpu.CompilerParams(vmem_limit_bytes=40 * 1024 * 1024)


def cost(vregs):
    return pl.CostEstimate(flops=vregs * 1024 * 20, bytes_accessed=vregs * 4096 * 4, transcendentals=0)


def masks():
    lane = lax.broadcasted_iota(jnp.int32, (SUBS, LANES), 1)
    return lane == 0, lane == LANES - 1


def window_tiles(load, first, count, total):
    before = jnp.where(first > 0, load(jnp.maximum(first - 1, 0)), 0.0)
    after = jnp.where(first + count < total, load(jnp.minimum(first + count, total - 1)), 0.0)
    return [before] + [load(first + k) for k in range(count)] + [after]


def beside(before, here, after, edges):
    left = pltpu.roll(jnp.where(edges[1], before, here), 1, 1)
    right = pltpu.roll(jnp.where(edges[0], after, here), LANES - 1, 1)
    return left, right


def sub(row):
    return pl.ds(row * SUBS, SUBS)


def upside_down():
    return 1 - lax.axis_index("row") % 2


def place(row, flip):
    return row + flip * (SUBS - 1 - 2 * row)


def placed(row, flip):
    at = place(row, flip) * SUBS
    return pl.ds(at if isinstance(at, int) else pl.multiple_of(at, SUBS), SUBS)


def tile_columns(tile):
    return pl.ds(pl.multiple_of(tile * LANES, LANES), LANES)


def chunk_of(tiles):
    return max(count for count in range(1, 12) if tiles % count == 0)


def load_kernel(width, probes_ref, observed_ref, coefficients_ref, *refs):
    theirs_ref, own_ref, seen_ref, window_ref, top_ref, bottom_ref, eight, rest, observed, sem = refs
    core = lax.axis_index("probe")
    move = probes_ref.shape[3] - width
    mine = pl.ds(pl.multiple_of(core * move, LANES), width)
    other = pl.ds(pl.multiple_of((1 - core) * move, LANES), width)
    copies = [
        pltpu.make_async_copy(coefficients_ref.at[:, :, mine], window_ref, sem.at[0]),
        pltpu.make_async_copy(observed_ref.at[:, :, mine], seen_ref, sem.at[1]),
        pltpu.make_async_copy(probes_ref.at[:, :, :, other], theirs_ref, sem.at[2]),
        pltpu.make_async_copy(probes_ref.at[:, :, :, mine], own_ref, sem.at[3]),
    ]
    for copy in copies:
        copy.start()
    rest[...] = jnp.zeros_like(rest)
    observed[...] = jnp.zeros_like(observed)
    copies[0].wait()
    copies[1].wait()
    tiles = width // LANES
    for tile in range(tiles):
        cols = pl.ds(tile * LANES, LANES)
        for channel in range(8):
            eight[tile, pl.ds(channel, SUBS, stride=SUBS), :] = window_ref[channel, :, cols]
        rest[tile // 8, pl.ds(tile % 8, SUBS, stride=SUBS), :] = window_ref[8, :, cols]
        for c in range(2):
            observed[tile // 4, pl.ds(2 * (tile % 4) + c, SUBS, stride=SUBS), :] = seen_ref[c, :, cols]
    flip = upside_down()
    first, last = placed(0, flip), placed(SUBS - 1, flip)
    base = 0
    for source in (eight, rest, observed):
        for index in range(source.shape[0]):
            top_ref[base + index] = source[index, first, :]
            bottom_ref[base + index] = source[index, last, :]
        base += source.shape[0]
    copies[2].wait()
    copies[3].wait()


def combine(kappa, across, along, skew, coupling, sign):
    scale = 4.0 / (upper_edge - lower_edge)
    shift = 2.0 * (upper_edge + lower_edge) / (upper_edge - lower_edge)
    return (
        scale * (kappa + 2.0 * (across + along)) - shift,
        -scale * across,
        -scale * along,
        (-0.5 * scale * sign) * skew,
        scale * coupling,
    )


def prep_kernel(window_ref, expanded_ref):
    tiles = expanded_ref.shape[1]
    chunk = chunk_of(tiles)
    sign = 1.0 - 2.0 * upside_down().astype(jnp.float32)

    def body(step, carry):
        for k in range(chunk):
            tile = step * chunk + k
            cols = tile_columns(tile)
            raw = [window_ref[channel, :, cols] for channel in range(9)]
            for c in range(2):
                values = combine(raw[c], raw[2 + c], raw[4 + c], raw[6 + c], raw[8], sign)
                for kind, value in enumerate(values):
                    for probe in range(4):
                        expanded_ref[kind, tile, pl.ds(4 * c + probe, SUBS, stride=SUBS), :] = value
        return carry

    lax.fori_loop(0, tiles // chunk, body, 0)


def layout_kernel(own_ref, other_ref, z_ref, top_ref, bottom_ref, natural):
    tiles = z_ref.shape[0]
    chunk = chunk_of(tiles)
    flip = upside_down()

    def body(step, carry):
        for k in range(chunk):
            tile = step * chunk + k
            cols = tile_columns(tile)
            for c in range(2):
                for probe in range(2):
                    natural[tile, pl.ds(4 * c + probe, SUBS, stride=SUBS), :] = own_ref[probe, c, :, cols]
                    natural[tile, pl.ds(4 * c + 2 + probe, SUBS, stride=SUBS), :] = other_ref[probe, c, :, cols]
        for k in range(chunk):
            tile = step * chunk + k
            for row in range(SUBS):
                value = natural[tile, placed(row, flip), :]
                z_ref[tile, sub(row), :] = value
                if row == 0:
                    top_ref[tile] = value
                if row == SUBS - 1:
                    bottom_ref[tile] = value
        return carry

    lax.fori_loop(0, tiles // chunk, body, 0)


def rim(edge_ref, rim_ref, tiles):
    chunk = chunk_of(tiles)

    sign = 1.0 - 2.0 * upside_down().astype(jnp.float32)

    def spread(index, row):
        return jnp.broadcast_to(edge_ref[index, pl.ds(row, 1), :], (SUBS, LANES))

    def body(step, carry):
        low = lax.broadcasted_iota(jnp.int32, (SUBS, LANES), 0) < 4
        for k in range(chunk):
            tile = step * chunk + k
            pairs = [jnp.where(low, spread(tile, 2 * kind), spread(tile, 2 * kind + 1)) for kind in range(4)]
            coupling = spread(tiles + tile // 8, tile % 8)
            for kind, value in enumerate(combine(*pairs, coupling, sign)):
                rim_ref[kind, tile] = value
        return carry

    lax.fori_loop(0, tiles // chunk, body, 0)


def sweep(tiles, low, count, load, factor, z_row, before, constants, store):
    weight, scale = constants
    chunk = tiles if count <= 2 else chunk_of(tiles)

    def body(step, carry):
        edges = masks()
        first = step * chunk
        for k in range(chunk):
            tile = first + k
            values, sums, slopes = [], [], []
            for row in range(low - 1, low + count + 1):
                here = load(row, tile)
                if k == 0 and chunk == tiles:
                    last = jnp.zeros_like(here)
                elif k == 0:
                    last = jnp.where(first > 0, load(row, jnp.maximum(first - 1, 0)), 0.0)
                else:
                    last = load(row, tile - 1)
                if k == chunk - 1 and chunk == tiles:
                    after = jnp.zeros_like(here)
                elif k == chunk - 1:
                    more = first + chunk < tiles
                    after = jnp.where(more, load(row, jnp.minimum(first + chunk, tiles - 1)), 0.0)
                else:
                    after = load(row, tile + 1)
                left, right = beside(last, here, after, edges)
                values.append(here)
                sums.append(left + right)
                slopes.append(right - left)
            for at in range(count):
                row = low + at
                total = (
                    factor(0, row, tile) * values[at + 1]
                    + factor(1, row, tile) * sums[at + 1]
                    + factor(2, row, tile) * (values[at] + values[at + 2])
                    + factor(3, row, tile) * (slopes[at + 2] - slopes[at])
                    + factor(4, row, tile) * pltpu.roll(values[at + 1], 4, 0)
                )
                if scale != 1.0:
                    total = scale * total
                total = total + weight * z_row(row, tile)
                if before is not None:
                    total = total - before(row, tile)
                store(row, tile, total)
        return carry

    if chunk == tiles:
        body(0, 0)
    else:
        lax.fori_loop(0, tiles // chunk, body, 0)


def first_kernel(part, constants, tiles, *refs):
    halo_ref = None
    if part != 1:
        halo_ref, refs = refs[0], refs[1:]
    z_ref, expanded_ref, out_ref = refs
    low, count = ((0, 2), (2, 4), (6, 2))[part]
    flip = upside_down()

    def now(row, tile):
        if row < 0 or row > 7:
            return halo_ref[tile]
        return z_ref[tile, sub(row), :]

    def store(row, tile, value):
        if part == 1:
            out_ref[tile, sub(row - low), :] = value
        else:
            out_ref[2 * tile + row - low] = value

    def factor(kind, row, tile):
        return expanded_ref[kind, tile, placed(row, flip), :]

    sweep(tiles, low, count, now, factor, lambda row, tile: z_ref[tile, sub(row), :], None, constants, store)


def inner_rows(top_ref, inner_ref, bottom_ref):
    def now(row, tile):
        if row < 2:
            return top_ref[2 * tile + row]
        if row < 6:
            return inner_ref[tile, sub(row - 2), :]
        return bottom_ref[2 * tile + row - 6]

    return now


def middle_kernel(steps, tiles, *refs):
    z_ref, expanded_ref, top_ref, inner_ref, bottom_ref = refs[:5]
    once_ref, twice_ref = refs[-2:]
    now = inner_rows(top_ref, inner_ref, bottom_ref)
    flip = upside_down()

    def factor(kind, row, tile):
        return expanded_ref[kind, tile, placed(row, flip), :]

    def z_row(row, tile):
        return z_ref[tile, sub(row), :]

    def once(row, tile):
        return once_ref[tile, sub(row - 1), :]

    def store_once(row, tile, value):
        once_ref[tile, sub(row - 1), :] = value

    def store_twice(row, tile, value):
        twice_ref[tile, sub(row - 2), :] = value

    older = None
    if len(refs) > 7:
        older = lambda row, tile: refs[5][tile, sub(row - 1), :]
    sweep(tiles, 1, 6, now, factor, z_row, older, steps[0], store_once)
    sweep(tiles, 2, 4, once, factor, z_row, now, steps[1], store_twice)


def edge_product(upper, constants, tiles, halo_ref, z_halo_ref, z_ref, expanded_ref, rim_ref, edge_ref, older_ref, once_ref):
    base = 0 if upper else 6
    flip = upside_down()
    low = -1 if upper else 7

    def now(row, tile):
        if row < 0 or row > 7:
            return halo_ref[2 * tile + (-1 - row if upper else 9 - row)]
        return edge_ref[2 * tile + row - base]

    def factor(kind, row, tile):
        if row < 0 or row > 7:
            return rim_ref[kind, tile]
        return expanded_ref[kind, tile, placed(row, flip), :]

    def z_row(row, tile):
        if row < 0 or row > 7:
            return z_halo_ref[tile]
        return z_ref[tile, sub(row), :]

    def store(row, tile, value):
        once_ref[tile, sub(row - low), :] = value

    older = None if older_ref is None else (lambda row, tile: older_ref[tile, sub(row - low), :])
    sweep(tiles, low, 2, now, factor, z_row, older, constants, store)
    return now, factor, z_row


def edge_kernel(upper, steps, tiles, *refs):
    halo_ref, z_halo_ref, z_ref, expanded_ref, rim_ref, edge_ref, inner_ref = refs[:7]
    once_ref, twice_ref = refs[-2:]
    older_ref = refs[7] if len(refs) > 9 else None
    now, factor, z_row = edge_product(
        upper, steps[0], tiles, halo_ref, z_halo_ref, z_ref, expanded_ref, rim_ref, edge_ref, older_ref, once_ref
    )
    base = 0 if upper else 6
    low = -1 if upper else 7

    def once(row, tile):
        if 1 <= row <= 6:
            return inner_ref[tile, sub(row - 1), :]
        return once_ref[tile, sub(row - low), :]

    def store_twice(row, tile, value):
        twice_ref[2 * tile + row - base] = value

    sweep(tiles, base, 2, once, factor, z_row, now, steps[1], store_twice)


def gradient_rows(low, count, tile, slot, load, z_ref, factor, tiles, products, flip):
    edges = masks()
    values, sums, slopes = [], [], []
    for row in range(low - 1, low + count + 1):
        before, here, after = window_tiles(lambda at: load(row, at), tile, 1, tiles)
        left, right = beside(before, here, after, edges)
        values.append(here)
        sums.append(left + right)
        slopes.append(right - left)
    for at in range(count):
        row = low + at
        left = factor * z_ref[tile, sub(row), :]
        value = values[at + 1]
        twice = 2.0 * value
        rows = placed(row, flip)
        products[slot, 0, rows, :] = left * value
        products[slot, 1, rows, :] = left * (twice - sums[at + 1])
        products[slot, 2, rows, :] = left * (twice - (values[at] + values[at + 2]))
        products[slot, 3, rows, :] = ((flip - 0.5) * left) * (slopes[at + 2] - slopes[at])
        products[slot, 4, rows, :] = left * pltpu.roll(value, 4, 0)


def gradient_sums(slot, products, start, store):
    for kind in range(5):
        parts = [products[slot, kind, pl.ds(s, SUBS, stride=SUBS), :] for s in range(SUBS)]
        sums = [(parts[4 * c] + parts[4 * c + 1]) + (parts[4 * c + 2] + parts[4 * c + 3]) for c in range(2)]
        if kind < 4:
            for c in range(2):
                store(2 * kind + c, sums[c] + start(2 * kind + c))
        else:
            store(8, (sums[0] + sums[1]) + start(8))


def gradient_kernel(constants, tiles, factor, *refs):
    z_ref, expanded_ref, top_ref, inner_ref, bottom_ref, older_ref, data_ref, series_ref, out_ref, products = refs
    now = inner_rows(top_ref, inner_ref, bottom_ref)
    flip = upside_down()

    def coefficient(kind, row, tile):
        return expanded_ref[kind, tile, placed(row, flip), :]

    def store(row, tile, value):
        series_ref[tile, sub(row - 1), :] = value

    def series(row, tile):
        return series_ref[tile, sub(row - 1), :]

    sweep(
        tiles,
        1,
        6,
        now,
        coefficient,
        lambda row, tile: z_ref[tile, sub(row), :],
        lambda row, tile: older_ref[tile, sub(row - 1), :],
        constants,
        store,
    )
    kept = out_ref.shape[2] // LANES
    offset = lax.axis_index("probe") * (tiles - kept)
    count = products.shape[0]
    products[...] = jnp.zeros_like(products)

    def body(turned, step, carry):
        for k in range(count):
            gradient_rows(2, 4, step * count + k + offset, k, series, z_ref, factor, tiles, products, turned)
        for k in range(count):
            index = step * count + k
            cols = tile_columns(index)

            def put(channel, value):
                out_ref[channel, :, cols] = value

            gradient_sums(k, products, lambda channel: data_ref[index + offset, channel], put)
        return carry

    for turned in range(2):

        @pl.when(flip == turned)
        def _():
            lax.fori_loop(0, kept // count, functools.partial(body, turned), 0)


def end_kernel(upper, constants, tiles, *refs):
    edge_product(upper, constants, tiles, *refs)


def finish_kernel(tiles, factor, z_ref, over_ref, inner_ref, under_ref, part_ref, out_ref, products, target, sem):
    def series(row, tile):
        if row < 1:
            return over_ref[tile, sub(row + 1), :]
        if row > 6:
            return under_ref[tile, sub(row - 7), :]
        return inner_ref[tile, sub(row - 1), :]

    kept = target.shape[2] // LANES
    offset = lax.axis_index("probe") * (tiles - kept)
    count = products.shape[0]
    products[...] = jnp.zeros_like(products)

    def body(turned, step, carry):
        for k in range(count):
            tile = step * count + k + offset
            for low in (0, 6):
                gradient_rows(low, 2, tile, k, series, z_ref, factor, tiles, products, turned)
        for k in range(count):
            cols = tile_columns(step * count + k)

            def put(channel, value):
                target[channel, :, cols] = value

            gradient_sums(k, products, lambda channel: part_ref[channel, :, cols], put)
        return carry

    steps = kept // count
    groups = sem.shape[0]

    def run(turned):
        copies = []
        for group in range(groups):
            span = (group * steps // groups, (group + 1) * steps // groups)
            lax.fori_loop(*span, functools.partial(body, turned), 0)
            cols = pl.ds(group * kept // groups * LANES, kept // groups * LANES)
            copies.append(pltpu.make_async_copy(target.at[:, :, cols], out_ref.at[:, :, cols], sem.at[group]))
            copies[-1].start()
        for copy in copies:
            copy.wait()

    for turned in range(2):
        pl.when(upside_down() == turned)(functools.partial(run, turned))


def border_kernel(tiles, seen_ref, up_ref, down_ref, out_ref, rim_up_ref, rim_down_ref):
    rim(up_ref, rim_up_ref, tiles)
    rim(down_ref, rim_down_ref, tiles)
    chunk = chunk_of(tiles)

    base = tiles + -(-tiles // 8)
    flip = upside_down()

    def halo(near, far, c, tile):
        at = (base + tile // 4, pl.ds(2 * (tile % 4) + c, 1), slice(None))
        row = jnp.where(flip == 1, far[at], near[at])
        return jnp.broadcast_to(row, (SUBS, LANES))

    def body(step, carry):
        edges = masks()
        row = lax.broadcasted_iota(jnp.int32, (SUBS, LANES), 0)
        first = step * chunk
        kept = [[], []]
        for c in range(2):
            values = window_tiles(lambda tile: seen_ref[c, :, tile_columns(tile)], first, chunk, tiles)
            ups = window_tiles(lambda tile: halo(up_ref, down_ref, c, tile), first, chunk, tiles)
            downs = window_tiles(lambda tile: halo(down_ref, up_ref, c, tile), first, chunk, tiles)
            aboves = [jnp.where(row == 0, u, pltpu.roll(v, 1, 0)) for u, v in zip(ups, values)]
            belows = [jnp.where(row == SUBS - 1, d, pltpu.roll(v, SUBS - 1, 0)) for d, v in zip(downs, values)]
            tilts = [b - a for a, b in zip(aboves, belows)]
            for k in range(chunk):
                tile = first + k
                value = values[k + 1]
                left, right = beside(values[k], value, values[k + 2], edges)
                low, high = beside(tilts[k], tilts[k + 1], tilts[k + 2], edges)
                half = -0.5 * value
                out_ref[tile, c] = half * value
                out_ref[tile, 2 + c] = half * (2.0 * value - (left + right))
                out_ref[tile, 4 + c] = half * (2.0 * value - (aboves[k + 1] + belows[k + 1]))
                out_ref[tile, 6 + c] = (-0.5 * half) * (high - low)
                kept[c].append(value)
        for k in range(chunk):
            out_ref[first + k, 8] = -(kept[0][k] * kept[1][k])
        return carry

    lax.fori_loop(0, tiles // chunk, body, 0)


def per_device(observations, coefficients, probes):
    weights = cheb_weights(CHEB, lower_edge, upper_edge)
    f32 = jnp.float32
    columns = probes.shape[3]
    share = columns // lax.axis_size("probe")
    width = share + LANES
    tiles = width // LANES
    kept = share // LANES
    rows = lax.axis_size("row")
    near_pairs = [pair for i in range(0, rows - 1, 2) for pair in ((i, i + 1), (i + 1, i))]
    far_pairs = [pair for i in range(1, rows - 1, 2) for pair in ((i, i + 1), (i + 1, i))]

    def near(edge):
        return lax.ppermute(edge, "row", near_pairs)

    def far(edge):
        return lax.ppermute(edge, "row", far_pairs)

    def call(kernel, name, vregs, operands, outs, scratch=(), in_specs=None, out_specs=None):
        return pl.pallas_call(
            kernel,
            out_shape=outs,
            in_specs=in_specs or [vmem_spec()] * len(operands),
            out_specs=out_specs or jax.tree.map(lambda _: vmem_spec(), outs),
            scratch_shapes=scratch,
            compiler_params=params(),
            cost_estimate=cost(vregs),
            name=name,
        )(*operands)

    eights, fours = -(-tiles // 8), -(-tiles // 4)
    edge_shape = pltpu.VMEM((tiles + eights + fours, SUBS, LANES), f32)
    theirs, own, seen, window, edge_top, edge_bottom = call(
        functools.partial(load_kernel, width),
        "load",
        100,
        [
            pltpu.with_memory_space_constraint(array, pltpu.HBM)
            for array in (probes, observations, coefficients)
        ],
        [
            pltpu.VMEM((2, 2, SUBS, width), f32),
            pltpu.VMEM((2, 2, SUBS, width), f32),
            pltpu.VMEM((2, SUBS, width), f32),
            pltpu.VMEM((9, SUBS, width), f32),
            edge_shape,
            edge_shape,
        ],
        [pltpu.VMEM((count, SUBS * SUBS, LANES), f32) for count in (tiles, eights, fours)]
        + [pltpu.SemaphoreType.DMA((4,))],
        [pl.BlockSpec(memory_space=pltpu.HBM)] * 3,
    )
    other = lax.ppermute(theirs, "probe", [(0, 1), (1, 0)])
    edges_up, edges_down = near(edge_top), far(edge_bottom)
    expanded = call(
        prep_kernel, "prep", 5 * 8 * tiles, (window,), pltpu.VMEM((5, tiles, SUBS * SUBS, LANES), f32)
    )
    own, expanded = lax.optimization_barrier((own, expanded))
    def rows_of(count):
        return pltpu.VMEM((tiles, count * SUBS, LANES), f32)

    z, top, bottom = call(
        layout_kernel,
        "layout",
        8 * tiles,
        (own, other),
        [rows_of(SUBS), rows_of(1), rows_of(1)],
        [rows_of(SUBS)],
    )
    z_up, z_down = near(top), far(bottom)
    edge_rows = pltpu.VMEM((2 * tiles, SUBS, LANES), f32)
    constants = (weights[CHEB - 1], weights[CHEB])

    def first(part, halos, out):
        return call(
            functools.partial(first_kernel, part, constants, tiles),
            "first",
            (2 + part % 2 * 2) * tiles,
            [*halos, z, expanded],
            out,
        )

    expanded, edges_up, edges_down = lax.optimization_barrier((expanded, edges_up, edges_down))
    inner = first(1, [], rows_of(4))
    bottom = first(2, [z_down], edge_rows)
    _, near_halo = lax.optimization_barrier((bottom, z_up))
    down = far(bottom)
    top = first(0, [near_halo], edge_rows)
    up = near(top)
    _, seen = lax.optimization_barrier((top, seen))
    rim_shape = pltpu.VMEM((5, tiles, SUBS, LANES), f32)
    data, rim_up, rim_down = call(
        functools.partial(border_kernel, tiles),
        "border",
        9 * tiles,
        (seen, edges_up, edges_down),
        [pltpu.VMEM((tiles, 9, SUBS, LANES), f32), rim_shape, rim_shape],
    )
    once = None
    for order in range(CHEB - 2, 0, -2):
        opening = weights[order] - (weights[CHEB] if order == CHEB - 2 else 0.0)
        steps = ((opening, 1.0), (weights[order - 1], 1.0))
        inner_once, inner_twice = call(
            functools.partial(middle_kernel, steps, tiles),
            "middle",
            10 * tiles,
            [z, expanded, top, inner, bottom] + ([once[1]] if once else []),
            [rows_of(6), rows_of(4)],
        )

        def edge(upper):
            operands = [up if upper else down, z_up if upper else z_down, z, expanded, rim_up if upper else rim_down]
            operands += [top if upper else bottom, inner_once]
            return call(
                functools.partial(edge_kernel, upper, steps, tiles),
                "upper" if upper else "lower",
                4 * tiles,
                operands + ([once[0 if upper else 2]] if once else []),
                [rows_of(2), edge_rows],
            )

        under = edge(False)
        _, up = lax.optimization_barrier((under[1], up))
        over = edge(True)
        once = (over[0], inner_once, under[0])
        top, inner, bottom = over[1], inner_twice, under[1]
        down, up = far(bottom), near(top)

    factor = 0.5 / (probes.shape[0] * lax.axis_size("probe"))
    count = max(n for n in range(1, 5) if kept % n == 0)
    constants = (weights[0], 0.5)
    products = pltpu.VMEM((count, 5, SUBS * SUBS, LANES), f32)
    whole = (9, SUBS, share)
    series, part = call(
        functools.partial(gradient_kernel, constants, tiles, factor),
        "gradient",
        24 * tiles,
        (z, expanded, top, inner, bottom, once[1], data),
        [rows_of(6), pltpu.VMEM(whole, f32)],
        [products],
    )
    ends = [
        call(
            functools.partial(end_kernel, upper, constants, tiles),
            "upper_end" if upper else "lower_end",
            2 * tiles,
            operands,
            rows_of(2),
        )
        for upper, operands in (
            (True, (up, z_up, z, expanded, rim_up, top, once[0])),
            (False, (down, z_down, z, expanded, rim_down, bottom, once[2])),
        )
    ]
    wide = max(n for n in range(1, 9) if kept % n == 0)
    groups = max(n for n in range(1, 5) if kept // wide % n == 0)
    return call(
        functools.partial(finish_kernel, tiles, factor),
        "finish",
        16 * tiles,
        (z, ends[0], series, ends[1], part),
        jax.ShapeDtypeStruct(whole, f32),
        [pltpu.VMEM((wide, 5, SUBS * SUBS, LANES), f32), pltpu.VMEM(whole, f32), pltpu.SemaphoreType.DMA((groups,))],
        None,
        pl.BlockSpec(memory_space=pltpu.HBM),
    )


def solution(mesh):
    in_specs = (P("group", "row", None), P("group", "row", None), P("probe", "group", "row", None))
    out_specs = P("group", "row", "probe")
    return jax.shard_map(
        per_device, mesh=mesh, in_specs=in_specs, out_specs=out_specs, check_vma=False
    )
```

```python
import functools
import math

import jax
import jax.numpy as jnp
from jax import lax
from jax.experimental import pallas as pl
from jax.experimental.pallas import tpu as pltpu
from jax.sharding import PartitionSpec as P

CHEB = 6
LANES = 128
SUBS = 8

lower_edge = 0.25
upper_edge = 12.0


def cheb_weights(degree, low_end, high_end):
    count = degree + 1
    values = []
    for order in range(count):
        accum = 0.0
        for node in range(count):
            angle = math.pi * (node + 0.5) / count
            point = 0.5 * (high_end - low_end) * math.cos(angle) + 0.5 * (high_end + low_end)
            accum += math.cos(order * angle) / point
        accum = accum * 2.0 / count
        if order == 0:
            accum = accum * 0.5
        values.append(accum)
    return values


def vmem_spec():
    return pl.BlockSpec(memory_space=pltpu.VMEM)


def params():
    return pltpu.CompilerParams(vmem_limit_bytes=40 * 1024 * 1024)


def cost(vregs):
    return pl.CostEstimate(flops=vregs * 1024 * 20, bytes_accessed=vregs * 4096 * 4, transcendentals=0)


def masks():
    lane = lax.broadcasted_iota(jnp.int32, (SUBS, LANES), 1)
    return lane == 0, lane == LANES - 1


def window_tiles(load, first, count, total):
    before = jnp.where(first > 0, load(jnp.maximum(first - 1, 0)), 0.0)
    after = jnp.where(first + count < total, load(jnp.minimum(first + count, total - 1)), 0.0)
    return [before] + [load(first + k) for k in range(count)] + [after]


def beside(before, here, after, edges):
    left = pltpu.roll(jnp.where(edges[1], before, here), 1, 1)
    right = pltpu.roll(jnp.where(edges[0], after, here), LANES - 1, 1)
    return left, right


def sub(row):
    return pl.ds(row * SUBS, SUBS)


def upside_down():
    return 1 - lax.axis_index("row") % 2


def place(row, flip):
    return row + flip * (SUBS - 1 - 2 * row)


def placed(row, flip):
    at = place(row, flip) * SUBS
    return pl.ds(at if isinstance(at, int) else pl.multiple_of(at, SUBS), SUBS)


def tile_columns(tile):
    return pl.ds(pl.multiple_of(tile * LANES, LANES), LANES)


def chunk_of(tiles):
    return max(count for count in range(1, 12) if tiles % count == 0)


def load_kernel(width, probes_ref, observed_ref, coefficients_ref, *refs):
    theirs_ref, own_ref, seen_ref, window_ref, top_ref, bottom_ref, eight, rest, observed, sem = refs
    core = lax.axis_index("probe")
    move = probes_ref.shape[3] - width
    mine = pl.ds(pl.multiple_of(core * move, LANES), width)
    other = pl.ds(pl.multiple_of((1 - core) * move, LANES), width)
    copies = [
        pltpu.make_async_copy(coefficients_ref.at[:, :, mine], window_ref, sem.at[0]),
        pltpu.make_async_copy(observed_ref.at[:, :, mine], seen_ref, sem.at[1]),
        pltpu.make_async_copy(probes_ref.at[:, :, :, other], theirs_ref, sem.at[2]),
        pltpu.make_async_copy(probes_ref.at[:, :, :, mine], own_ref, sem.at[3]),
    ]
    for copy in copies:
        copy.start()
    rest[...] = jnp.zeros_like(rest)
    observed[...] = jnp.zeros_like(observed)
    copies[0].wait()
    copies[1].wait()
    tiles = width // LANES
    for tile in range(tiles):
        cols = pl.ds(tile * LANES, LANES)
        for channel in range(8):
            eight[tile, pl.ds(channel, SUBS, stride=SUBS), :] = window_ref[channel, :, cols]
        rest[tile // 8, pl.ds(tile % 8, SUBS, stride=SUBS), :] = window_ref[8, :, cols]
        for c in range(2):
            observed[tile // 4, pl.ds(2 * (tile % 4) + c, SUBS, stride=SUBS), :] = seen_ref[c, :, cols]
    flip = upside_down()
    first, last = placed(0, flip), placed(SUBS - 1, flip)
    base = 0
    for source in (eight, rest, observed):
        for index in range(source.shape[0]):
            top_ref[base + index] = source[index, first, :]
            bottom_ref[base + index] = source[index, last, :]
        base += source.shape[0]
    copies[2].wait()
    copies[3].wait()


def combine(kappa, across, along, skew, coupling, sign):
    scale = 4.0 / (upper_edge - lower_edge)
    shift = 2.0 * (upper_edge + lower_edge) / (upper_edge - lower_edge)
    return (
        scale * (kappa + 2.0 * (across + along)) - shift,
        -scale * across,
        -scale * along,
        (-0.5 * scale * sign) * skew,
        scale * coupling,
    )


def prep_kernel(window_ref, expanded_ref):
    tiles = expanded_ref.shape[1]
    chunk = chunk_of(tiles)
    sign = 1.0 - 2.0 * upside_down().astype(jnp.float32)

    def body(step, carry):
        for k in range(chunk):
            tile = step * chunk + k
            cols = tile_columns(tile)
            raw = [window_ref[channel, :, cols] for channel in range(9)]
            for c in range(2):
                values = combine(raw[c], raw[2 + c], raw[4 + c], raw[6 + c], raw[8], sign)
                for kind, value in enumerate(values):
                    for probe in range(4):
                        expanded_ref[kind, tile, pl.ds(4 * c + probe, SUBS, stride=SUBS), :] = value
        return carry

    lax.fori_loop(0, tiles // chunk, body, 0)


def layout_kernel(own_ref, other_ref, z_ref, top_ref, bottom_ref, natural):
    tiles = z_ref.shape[0]
    chunk = chunk_of(tiles)
    flip = upside_down()

    def body(step, carry):
        for k in range(chunk):
            tile = step * chunk + k
            cols = tile_columns(tile)
            for c in range(2):
                for probe in range(2):
                    natural[tile, pl.ds(4 * c + probe, SUBS, stride=SUBS), :] = own_ref[probe, c, :, cols]
                    natural[tile, pl.ds(4 * c + 2 + probe, SUBS, stride=SUBS), :] = other_ref[probe, c, :, cols]
        for k in range(chunk):
            tile = step * chunk + k
            for row in range(SUBS):
                value = natural[tile, placed(row, flip), :]
                z_ref[tile, sub(row), :] = value
                if row == 0:
                    top_ref[tile] = value
                if row == SUBS - 1:
                    bottom_ref[tile] = value
        return carry

    lax.fori_loop(0, tiles // chunk, body, 0)


def rim(edge_ref, rim_ref, tiles):
    chunk = chunk_of(tiles)

    sign = 1.0 - 2.0 * upside_down().astype(jnp.float32)

    def spread(index, row):
        return jnp.broadcast_to(edge_ref[index, pl.ds(row, 1), :], (SUBS, LANES))

    def body(step, carry):
        low = lax.broadcasted_iota(jnp.int32, (SUBS, LANES), 0) < 4
        for k in range(chunk):
            tile = step * chunk + k
            pairs = [jnp.where(low, spread(tile, 2 * kind), spread(tile, 2 * kind + 1)) for kind in range(4)]
            coupling = spread(tiles + tile // 8, tile % 8)
            for kind, value in enumerate(combine(*pairs, coupling, sign)):
                rim_ref[kind, tile] = value
        return carry

    lax.fori_loop(0, tiles // chunk, body, 0)


def sweep(tiles, low, count, load, factor, z_row, before, constants, store):
    weight, scale = constants
    chunk = tiles if count <= 2 else chunk_of(tiles)

    def body(step, carry):
        edges = masks()
        first = step * chunk
        for k in range(chunk):
            tile = first + k
            values, sums, slopes = [], [], []
            for row in range(low - 1, low + count + 1):
                here = load(row, tile)
                if k == 0 and chunk == tiles:
                    last = jnp.zeros_like(here)
                elif k == 0:
                    last = jnp.where(first > 0, load(row, jnp.maximum(first - 1, 0)), 0.0)
                else:
                    last = load(row, tile - 1)
                if k == chunk - 1 and chunk == tiles:
                    after = jnp.zeros_like(here)
                elif k == chunk - 1:
                    more = first + chunk < tiles
                    after = jnp.where(more, load(row, jnp.minimum(first + chunk, tiles - 1)), 0.0)
                else:
                    after = load(row, tile + 1)
                left, right = beside(last, here, after, edges)
                values.append(here)
                sums.append(left + right)
                slopes.append(right - left)
            for at in range(count):
                row = low + at
                total = (
                    factor(0, row, tile) * values[at + 1]
                    + factor(1, row, tile) * sums[at + 1]
                    + factor(2, row, tile) * (values[at] + values[at + 2])
                    + factor(3, row, tile) * (slopes[at + 2] - slopes[at])
                    + factor(4, row, tile) * pltpu.roll(values[at + 1], 4, 0)
                )
                if scale != 1.0:
                    total = scale * total
                total = total + weight * z_row(row, tile)
                if before is not None:
                    total = total - before(row, tile)
                store(row, tile, total)
        return carry

    if chunk == tiles:
        body(0, 0)
    else:
        lax.fori_loop(0, tiles // chunk, body, 0)


def first_kernel(part, constants, tiles, *refs):
    halo_ref = None
    if part != 1:
        halo_ref, refs = refs[0], refs[1:]
    z_ref, expanded_ref, out_ref = refs
    low, count = ((0, 2), (2, 4), (6, 2))[part]
    flip = upside_down()

    def now(row, tile):
        if row < 0 or row > 7:
            return halo_ref[tile]
        return z_ref[tile, sub(row), :]

    def store(row, tile, value):
        if part == 1:
            out_ref[tile, sub(row - low), :] = value
        else:
            out_ref[2 * tile + row - low] = value

    def factor(kind, row, tile):
        return expanded_ref[kind, tile, placed(row, flip), :]

    sweep(tiles, low, count, now, factor, lambda row, tile: z_ref[tile, sub(row), :], None, constants, store)


def inner_rows(top_ref, inner_ref, bottom_ref):
    def now(row, tile):
        if row < 2:
            return top_ref[2 * tile + row]
        if row < 6:
            return inner_ref[tile, sub(row - 2), :]
        return bottom_ref[2 * tile + row - 6]

    return now


def middle_kernel(steps, tiles, *refs):
    z_ref, expanded_ref, top_ref, inner_ref, bottom_ref = refs[:5]
    once_ref, twice_ref = refs[-2:]
    now = inner_rows(top_ref, inner_ref, bottom_ref)
    flip = upside_down()

    def factor(kind, row, tile):
        return expanded_ref[kind, tile, placed(row, flip), :]

    def z_row(row, tile):
        return z_ref[tile, sub(row), :]

    def once(row, tile):
        return once_ref[tile, sub(row - 1), :]

    def store_once(row, tile, value):
        once_ref[tile, sub(row - 1), :] = value

    def store_twice(row, tile, value):
        twice_ref[tile, sub(row - 2), :] = value

    older = None
    if len(refs) > 7:
        older = lambda row, tile: refs[5][tile, sub(row - 1), :]
    sweep(tiles, 1, 6, now, factor, z_row, older, steps[0], store_once)
    sweep(tiles, 2, 4, once, factor, z_row, now, steps[1], store_twice)


def edge_product(upper, constants, tiles, halo_ref, z_halo_ref, z_ref, expanded_ref, rim_ref, edge_ref, older_ref, once_ref):
    base = 0 if upper else 6
    flip = upside_down()
    low = -1 if upper else 7

    def now(row, tile):
        if row < 0 or row > 7:
            return halo_ref[2 * tile + (-1 - row if upper else 9 - row)]
        return edge_ref[2 * tile + row - base]

    def factor(kind, row, tile):
        if row < 0 or row > 7:
            return rim_ref[kind, tile]
        return expanded_ref[kind, tile, placed(row, flip), :]

    def z_row(row, tile):
        if row < 0 or row > 7:
            return z_halo_ref[tile]
        return z_ref[tile, sub(row), :]

    def store(row, tile, value):
        once_ref[tile, sub(row - low), :] = value

    older = None if older_ref is None else (lambda row, tile: older_ref[tile, sub(row - low), :])
    sweep(tiles, low, 2, now, factor, z_row, older, constants, store)
    return now, factor, z_row


def edge_kernel(upper, steps, tiles, *refs):
    halo_ref, z_halo_ref, z_ref, expanded_ref, rim_ref, edge_ref, inner_ref = refs[:7]
    once_ref, twice_ref = refs[-2:]
    older_ref = refs[7] if len(refs) > 9 else None
    now, factor, z_row = edge_product(
        upper, steps[0], tiles, halo_ref, z_halo_ref, z_ref, expanded_ref, rim_ref, edge_ref, older_ref, once_ref
    )
    base = 0 if upper else 6
    low = -1 if upper else 7

    def once(row, tile):
        if 1 <= row <= 6:
            return inner_ref[tile, sub(row - 1), :]
        return once_ref[tile, sub(row - low), :]

    def store_twice(row, tile, value):
        twice_ref[2 * tile + row - base] = value

    sweep(tiles, base, 2, once, factor, z_row, now, steps[1], store_twice)


def gradient_rows(low, count, tile, slot, load, z_ref, factor, tiles, products, flip):
    edges = masks()
    values, sums, slopes = [], [], []
    for row in range(low - 1, low + count + 1):
        before, here, after = window_tiles(lambda at: load(row, at), tile, 1, tiles)
        left, right = beside(before, here, after, edges)
        values.append(here)
        sums.append(left + right)
        slopes.append(right - left)
    for at in range(count):
        row = low + at
        left = factor * z_ref[tile, sub(row), :]
        value = values[at + 1]
        twice = 2.0 * value
        rows = placed(row, flip)
        products[slot, 0, rows, :] = left * value
        products[slot, 1, rows, :] = left * (twice - sums[at + 1])
        products[slot, 2, rows, :] = left * (twice - (values[at] + values[at + 2]))
        products[slot, 3, rows, :] = ((flip - 0.5) * left) * (slopes[at + 2] - slopes[at])
        products[slot, 4, rows, :] = left * pltpu.roll(value, 4, 0)


def gradient_sums(slot, products, start, store):
    for kind in range(5):
        parts = [products[slot, kind, pl.ds(s, SUBS, stride=SUBS), :] for s in range(SUBS)]
        sums = [(parts[4 * c] + parts[4 * c + 1]) + (parts[4 * c + 2] + parts[4 * c + 3]) for c in range(2)]
        if kind < 4:
            for c in range(2):
                store(2 * kind + c, sums[c] + start(2 * kind + c))
        else:
            store(8, (sums[0] + sums[1]) + start(8))


def gradient_kernel(constants, tiles, factor, *refs):
    z_ref, expanded_ref, top_ref, inner_ref, bottom_ref, older_ref, data_ref, series_ref, out_ref, products = refs
    now = inner_rows(top_ref, inner_ref, bottom_ref)
    flip = upside_down()

    def coefficient(kind, row, tile):
        return expanded_ref[kind, tile, placed(row, flip), :]

    def store(row, tile, value):
        series_ref[tile, sub(row - 1), :] = value

    def series(row, tile):
        return series_ref[tile, sub(row - 1), :]

    sweep(
        tiles,
        1,
        6,
        now,
        coefficient,
        lambda row, tile: z_ref[tile, sub(row), :],
        lambda row, tile: older_ref[tile, sub(row - 1), :],
        constants,
        store,
    )
    kept = out_ref.shape[2] // LANES
    offset = lax.axis_index("probe") * (tiles - kept)
    count = products.shape[0]
    products[...] = jnp.zeros_like(products)

    def body(turned, step, carry):
        for k in range(count):
            gradient_rows(2, 4, step * count + k + offset, k, series, z_ref, factor, tiles, products, turned)
        for k in range(count):
            index = step * count + k
            cols = tile_columns(index)

            def put(channel, value):
                out_ref[channel, :, cols] = value

            gradient_sums(k, products, lambda channel: data_ref[index + offset, channel], put)
        return carry

    for turned in range(2):

        @pl.when(flip == turned)
        def _():
            lax.fori_loop(0, kept // count, functools.partial(body, turned), 0)


def end_kernel(upper, constants, tiles, factor, *refs):
    halo_ref, z_halo_ref, z_ref, expanded_ref, rim_ref, edge_ref, older_ref, inner_ref, part_ref, out_ref, once_ref, products = refs[:12]
    target = refs[12] if upper else out_ref
    products[...] = jnp.zeros_like(products)
    edge_product(
        upper, constants, tiles, halo_ref, z_halo_ref, z_ref, expanded_ref, rim_ref, edge_ref, older_ref, once_ref
    )
    low = -1 if upper else 7

    def series(row, tile):
        if 1 <= row <= 6:
            return inner_ref[tile, sub(row - 1), :]
        return once_ref[tile, sub(row - low), :]

    kept = target.shape[2] // LANES
    offset = lax.axis_index("probe") * (tiles - kept)
    count = products.shape[0]
    steps = kept // count

    def body(turned, step, carry):
        for k in range(count):
            tile = step * count + k + offset
            gradient_rows(0 if upper else 6, 2, tile, k, series, z_ref, factor, tiles, products, turned)
        for k in range(count):
            cols = tile_columns(step * count + k)

            def put(channel, value):
                target[channel, :, cols] = value

            gradient_sums(k, products, lambda channel: part_ref[channel, :, cols], put)
        return carry

    def run(turned):
        if not upper:
            lax.fori_loop(0, steps, functools.partial(body, turned), 0)
            return
        sem = refs[13]
        groups = sem.shape[0]
        copies = []
        for group in range(groups):
            span = (group * steps // groups, (group + 1) * steps // groups)
            lax.fori_loop(*span, functools.partial(body, turned), 0)
            cols = pl.ds(group * kept // groups * LANES, kept // groups * LANES)
            copies.append(pltpu.make_async_copy(target.at[:, :, cols], out_ref.at[:, :, cols], sem.at[group]))
            copies[-1].start()
        for copy in copies:
            copy.wait()

    for turned in range(2):
        pl.when(upside_down() == turned)(functools.partial(run, turned))


def border_kernel(tiles, seen_ref, up_ref, down_ref, out_ref, rim_up_ref, rim_down_ref):
    rim(up_ref, rim_up_ref, tiles)
    rim(down_ref, rim_down_ref, tiles)
    chunk = chunk_of(tiles)

    base = tiles + -(-tiles // 8)
    flip = upside_down()

    def halo(near, far, c, tile):
        at = (base + tile // 4, pl.ds(2 * (tile % 4) + c, 1), slice(None))
        row = jnp.where(flip == 1, far[at], near[at])
        return jnp.broadcast_to(row, (SUBS, LANES))

    def body(step, carry):
        edges = masks()
        row = lax.broadcasted_iota(jnp.int32, (SUBS, LANES), 0)
        first = step * chunk
        kept = [[], []]
        for c in range(2):
            values = window_tiles(lambda tile: seen_ref[c, :, tile_columns(tile)], first, chunk, tiles)
            ups = window_tiles(lambda tile: halo(up_ref, down_ref, c, tile), first, chunk, tiles)
            downs = window_tiles(lambda tile: halo(down_ref, up_ref, c, tile), first, chunk, tiles)
            aboves = [jnp.where(row == 0, u, pltpu.roll(v, 1, 0)) for u, v in zip(ups, values)]
            belows = [jnp.where(row == SUBS - 1, d, pltpu.roll(v, SUBS - 1, 0)) for d, v in zip(downs, values)]
            tilts = [b - a for a, b in zip(aboves, belows)]
            for k in range(chunk):
                tile = first + k
                value = values[k + 1]
                left, right = beside(values[k], value, values[k + 2], edges)
                low, high = beside(tilts[k], tilts[k + 1], tilts[k + 2], edges)
                half = -0.5 * value
                out_ref[tile, c] = half * value
                out_ref[tile, 2 + c] = half * (2.0 * value - (left + right))
                out_ref[tile, 4 + c] = half * (2.0 * value - (aboves[k + 1] + belows[k + 1]))
                out_ref[tile, 6 + c] = (-0.5 * half) * (high - low)
                kept[c].append(value)
        for k in range(chunk):
            out_ref[first + k, 8] = -(kept[0][k] * kept[1][k])
        return carry

    lax.fori_loop(0, tiles // chunk, body, 0)


def per_device(observations, coefficients, probes):
    weights = cheb_weights(CHEB, lower_edge, upper_edge)
    f32 = jnp.float32
    columns = probes.shape[3]
    share = columns // lax.axis_size("probe")
    width = share + LANES
    tiles = width // LANES
    kept = share // LANES
    rows = lax.axis_size("row")
    near_pairs = [pair for i in range(0, rows - 1, 2) for pair in ((i, i + 1), (i + 1, i))]
    far_pairs = [pair for i in range(1, rows - 1, 2) for pair in ((i, i + 1), (i + 1, i))]

    def near(edge):
        return lax.ppermute(edge, "row", near_pairs)

    def far(edge):
        return lax.ppermute(edge, "row", far_pairs)

    def call(kernel, name, vregs, operands, outs, scratch=(), in_specs=None, out_specs=None):
        return pl.pallas_call(
            kernel,
            out_shape=outs,
            in_specs=in_specs or [vmem_spec()] * len(operands),
            out_specs=out_specs or jax.tree.map(lambda _: vmem_spec(), outs),
            scratch_shapes=scratch,
            compiler_params=params(),
            cost_estimate=cost(vregs),
            name=name,
        )(*operands)

    eights, fours = -(-tiles // 8), -(-tiles // 4)
    edge_shape = pltpu.VMEM((tiles + eights + fours, SUBS, LANES), f32)
    theirs, own, seen, window, edge_top, edge_bottom = call(
        functools.partial(load_kernel, width),
        "load",
        100,
        [
            pltpu.with_memory_space_constraint(array, pltpu.HBM)
            for array in (probes, observations, coefficients)
        ],
        [
            pltpu.VMEM((2, 2, SUBS, width), f32),
            pltpu.VMEM((2, 2, SUBS, width), f32),
            pltpu.VMEM((2, SUBS, width), f32),
            pltpu.VMEM((9, SUBS, width), f32),
            edge_shape,
            edge_shape,
        ],
        [pltpu.VMEM((count, SUBS * SUBS, LANES), f32) for count in (tiles, eights, fours)]
        + [pltpu.SemaphoreType.DMA((4,))],
        [pl.BlockSpec(memory_space=pltpu.HBM)] * 3,
    )
    other = lax.ppermute(theirs, "probe", [(0, 1), (1, 0)])
    edges_up, edges_down = near(edge_top), far(edge_bottom)
    expanded = call(
        prep_kernel, "prep", 5 * 8 * tiles, (window,), pltpu.VMEM((5, tiles, SUBS * SUBS, LANES), f32)
    )
    own, expanded = lax.optimization_barrier((own, expanded))
    def rows_of(count):
        return pltpu.VMEM((tiles, count * SUBS, LANES), f32)

    z, top, bottom = call(
        layout_kernel,
        "layout",
        8 * tiles,
        (own, other),
        [rows_of(SUBS), rows_of(1), rows_of(1)],
        [rows_of(SUBS)],
    )
    z_up, z_down = near(top), far(bottom)
    edge_rows = pltpu.VMEM((2 * tiles, SUBS, LANES), f32)
    constants = (weights[CHEB - 1], weights[CHEB])

    def first(part, halos, out):
        return call(
            functools.partial(first_kernel, part, constants, tiles),
            "first",
            (2 + part % 2 * 2) * tiles,
            [*halos, z, expanded],
            out,
        )

    rim_shape = pltpu.VMEM((5, tiles, SUBS, LANES), f32)
    data, rim_up, rim_down = call(
        functools.partial(border_kernel, tiles),
        "border",
        9 * tiles,
        (seen, edges_up, edges_down),
        [pltpu.VMEM((tiles, 9, SUBS, LANES), f32), rim_shape, rim_shape],
    )
    expanded, data = lax.optimization_barrier((expanded, data))
    inner = first(1, [], rows_of(4))
    bottom = first(2, [z_down], edge_rows)
    _, near_halo = lax.optimization_barrier((bottom, z_up))
    down = far(bottom)
    top = first(0, [near_halo], edge_rows)
    up = near(top)
    once = None
    for order in range(CHEB - 2, 0, -2):
        opening = weights[order] - (weights[CHEB] if order == CHEB - 2 else 0.0)
        steps = ((opening, 1.0), (weights[order - 1], 1.0))
        inner_once, inner_twice = call(
            functools.partial(middle_kernel, steps, tiles),
            "middle",
            10 * tiles,
            [z, expanded, top, inner, bottom] + ([once[1]] if once else []),
            [rows_of(6), rows_of(4)],
        )

        def edge(upper):
            operands = [up if upper else down, z_up if upper else z_down, z, expanded, rim_up if upper else rim_down]
            operands += [top if upper else bottom, inner_once]
            return call(
                functools.partial(edge_kernel, upper, steps, tiles),
                "upper" if upper else "lower",
                4 * tiles,
                operands + ([once[0 if upper else 2]] if once else []),
                [rows_of(2), edge_rows],
            )

        under = edge(False)
        _, up = lax.optimization_barrier((under[1], up))
        over = edge(True)
        once = (over[0], inner_once, under[0])
        top, inner, bottom = over[1], inner_twice, under[1]
        down, up = far(bottom), near(top)

    factor = 0.5 / (probes.shape[0] * lax.axis_size("probe"))
    count = max(n for n in range(1, 5) if kept % n == 0)
    constants = (weights[0], 0.5)
    products = pltpu.VMEM((count, 5, SUBS * SUBS, LANES), f32)
    whole = (9, SUBS, share)
    series, part = call(
        functools.partial(gradient_kernel, constants, tiles, factor),
        "gradient",
        24 * tiles,
        (z, expanded, top, inner, bottom, once[1], data),
        [rows_of(6), pltpu.VMEM(whole, f32)],
        [products],
    )
    part = call(
        functools.partial(end_kernel, False, constants, tiles, factor),
        "far_end",
        8 * tiles,
        (down, z_down, z, expanded, rim_down, bottom, once[2], series, part),
        pltpu.VMEM(whole, f32),
        [rows_of(2), products],
    )
    groups = max(n for n in range(1, 5) if kept // count % n == 0)
    return call(
        functools.partial(end_kernel, True, constants, tiles, factor),
        "finish",
        8 * tiles,
        (up, z_up, z, expanded, rim_up, top, once[0], series, part),
        jax.ShapeDtypeStruct(whole, f32),
        [rows_of(2), products, pltpu.VMEM(whole, f32), pltpu.SemaphoreType.DMA((groups,))],
        None,
        pl.BlockSpec(memory_space=pltpu.HBM),
    )


def solution(mesh):
    in_specs = (P("group", "row", None), P("group", "row", None), P("probe", "group", "row", None))
    out_specs = P("group", "row", "probe")
    return jax.shard_map(
        per_device, mesh=mesh, in_specs=in_specs, out_specs=out_specs, check_vma=False
    )
```
